32 devices in a mesh: ctx: 8 (over z, x), tp: 4 (over y, core).
Axes of the slice: x: 2, y: 2, z: 4, core: 2. Of those that a mesh axis runs over, the one named last changes fastest.
Arguments:
- queries: bfloat16 [256, 8192], P('ctx', 'tp'), may hold values from -15 to 15
- new_keys: bfloat16 [256, 1024], P('ctx', 'tp'), may hold values from -6 to 6
- new_values: bfloat16 [256, 1024], P('ctx', 'tp'), may hold values from -6 to 6
- cache_keys: bfloat16 [32768, 1024], P('ctx', 'tp'), may hold values from -6 to 6
- cache_values: bfloat16 [32768, 1024], P('ctx', 'tp'), may hold values from -6 to 6
- keep_tiles: int32 [8, 8, 24], P('ctx', 'tp'), may hold values from 0 to 31, as said below
- tile_count: int32 [8, 8], P('ctx', 'tp'), may hold values from 1 to 24
- owner_slot: int32 [8], replicated, may hold values from 0 to 7, each once
- out_weight: bfloat16 [8192, 8192], P('tp', 'ctx'), may hold values from -0.0625 to 0.0625
Outputs:
- projected_out: float32 [256, 8192], P('tp', 'ctx')
The draws below stay inside these ranges and needn't reach their ends.
Inputs may be any that keep to these rules, and one draw needn't show every extreme that they name: `keep_tiles`: the 24 entries of each keep list are distinct tile numbers; entries at or past tile_count are ignored.
All inputs are finite; a program needn't handle non-finite values.
Results may differ from the reference program's by a relative error of at most 0.0055.
Values may be sent and summed in bfloat16 or wider, within the bound.
No kernel may reach another device: no remote copies, remote signals or barrier semaphores. Data moves between devices by JAX's collectives and lax.ppermute only.
A program may use at most 128 MiB of HBM per device.

```python
import jax
import jax.numpy as jnp
from jax import lax

D = 8192
HQ = 64
KVH = 8
DH = 128
TILE = 128
TILES = 32
Q_DEV = 32
CAP = 24
Q_TOTAL = 256
N_CTX = 8


def pattern_signs(key):
    random_bits = jax.random.randint(jax.random.fold_in(key, 4242), (KVH, DH), 0, 2)
    return (2 * random_bits - 1).astype(jnp.float32)


def target_score(row_ids):
    return 120.0 + 90.0 * (row_ids // Q_DEV % 3).astype(jnp.float32)


def key_strength(row_ids):
    return jnp.sqrt(target_score(row_ids) / (2.5 * DH ** 0.5))


def draw_queries(key, part):
    inner_key = jax.random.fold_in(key, 11)
    values_out = jnp.clip(3.0 * jax.random.normal(inner_key, (Q_TOTAL, HQ * DH), jnp.float32), -15.0, 15.0)
    row_ids = jnp.arange(Q_TOTAL, dtype=jnp.int32)
    local_ids = row_ids % Q_DEV
    planted = (local_ids == 1) | (local_ids == Q_DEV - 1)
    signs_full = jnp.repeat(pattern_signs(key), HQ // KVH, axis=0).reshape(1, HQ * DH)
    strength = 2.5 * key_strength(row_ids)[:, None]
    values_out = jnp.where(planted[:, None], signs_full * strength, values_out)
    return values_out.astype(jnp.bfloat16)


def draw_new_keys(key, part):
    inner_key = jax.random.fold_in(key, 12)
    values_out = jnp.clip(jax.random.normal(inner_key, (Q_TOTAL, KVH * DH), jnp.float32), -6.0, 6.0)
    row_ids = jnp.arange(Q_TOTAL, dtype=jnp.int32)
    local_ids = row_ids % Q_DEV
    exact_rows = (local_ids == 1) | (local_ids == Q_DEV - 1)
    near_rows = (local_ids == 0) | (local_ids == Q_DEV - 2)
    signs_full = pattern_signs(key).reshape(1, KVH * DH)
    strength = key_strength(row_ids)[:, None]
    values_out = jnp.where(exact_rows[:, None], signs_full * strength, values_out)
    values_out = jnp.where(near_rows[:, None], signs_full * strength * 0.99, values_out)
    return values_out.astype(jnp.bfloat16)


def draw_keep_tiles(key, part):
    split_keys = jax.random.split(jax.random.fold_in(key, 21), N_CTX * KVH)
    orders = jax.vmap(lambda one_key: jax.random.permutation(one_key, TILES))(split_keys)
    return orders[:, :CAP].reshape(N_CTX, KVH, CAP).astype(jnp.int32)


def draw_tile_count(key, part):
    inner_key = jax.random.fold_in(key, 31)
    head_top = jax.random.randint(jax.random.fold_in(inner_key, 1), (1, KVH), CAP // 2, CAP + 1)
    lower = head_top // 2 + 1
    spread = head_top - head_top // 2
    raw_bits = jax.random.randint(jax.random.fold_in(inner_key, 2), (N_CTX, KVH), 0, 1048576)
    counts = lower + raw_bits % spread
    full_at = jax.random.randint(jax.random.fold_in(inner_key, 3), (), 0, N_CTX * KVH)
    flat_ids = jnp.arange(N_CTX * KVH, dtype=jnp.int32).reshape(N_CTX, KVH)
    counts = jnp.where(flat_ids == full_at, CAP, counts)
    return counts.astype(jnp.int32)


def levels(key, dims, pieces, low, largest):
    level = 1.0
    for axis_at, parts in pieces:
        heights = jax.random.uniform(jax.random.fold_in(jax.random.fold_in(key, 6), axis_at), (parts,), jnp.float32, low / len(pieces), largest / len(pieces))
        level = level * jnp.repeat(jnp.exp(heights), dims[axis_at] // parts).reshape((-1,) + (1,) * (len(dims) - 1 - axis_at))
    return level


def gaussian(stream_key, extent, scale, bound, pieces=(), kind=jnp.bfloat16):
    drawn = scale * jax.random.normal(stream_key, extent, jnp.float32)
    if pieces:
        drawn = drawn * levels(stream_key, extent, pieces, -0.22, 0.18)
    return jnp.clip(drawn, -bound, bound).astype(kind)


def setup_inputs(seed: int = 0) -> dict:
    arg_keys = jax.random.split(jax.random.key(seed), 10)
    queries = draw_queries(jax.random.fold_in(arg_keys[9], 71), 0)
    new_keys = draw_new_keys(jax.random.fold_in(arg_keys[9], 71), 0)
    new_values = gaussian(arg_keys[2], (Q_TOTAL, KVH * DH), 1.0, 6.0, ((0, 8), (1, 4)))
    cache_keys = gaussian(arg_keys[3], (N_CTX * TILES * TILE, KVH * DH), 1.0, 6.0, ((0, 8), (1, 4)))
    cache_values = gaussian(arg_keys[4], (N_CTX * TILES * TILE, KVH * DH), 1.0, 6.0, ((0, 8), (1, 4)))
    keep_tiles = draw_keep_tiles(jax.random.fold_in(arg_keys[9], 71), 0)
    tile_count = draw_tile_count(jax.random.fold_in(arg_keys[9], 71), 0)
    owner_slot = jax.random.permutation(arg_keys[7], N_CTX).astype(jnp.int32)
    out_weight = gaussian(arg_keys[8], (HQ * DH, D), (HQ * DH) ** -0.5, 0.0625, ((0, 4), (1, 8)))
    return dict(queries=queries, new_keys=new_keys, new_values=new_values, cache_keys=cache_keys, cache_values=cache_values, keep_tiles=keep_tiles, tile_count=tile_count, owner_slot=owner_slot, out_weight=out_weight)


def reference(queries, new_keys, new_values, cache_keys, cache_values, keep_tiles, tile_count, owner_slot, out_weight):
    group_size = HQ // KVH
    score_scale = DH ** -0.5
    row_ids = jnp.arange(Q_TOTAL, dtype=jnp.int32)
    place = owner_slot[row_ids // Q_DEV] * Q_DEV + row_ids % Q_DEV
    tiled_keys = cache_keys.reshape(N_CTX, TILES, TILE, KVH, DH)
    tiled_values = cache_values.reshape(N_CTX, TILES, TILE, KVH, DH)
    owner_ids = jnp.arange(N_CTX, dtype=jnp.int32)[:, None]
    live_slots = jnp.arange(CAP, dtype=jnp.int32)[None, None, :] < tile_count[:, :, None]
    head_outputs = []
    for kv_head in range(KVH):
        head_keys = tiled_keys[:, :, :, kv_head, :]
        head_values = tiled_values[:, :, :, kv_head, :]
        kept_keys = head_keys[owner_ids, keep_tiles[:, kv_head, :]].reshape(-1, DH)
        kept_values = head_values[owner_ids, keep_tiles[:, kv_head, :]].reshape(-1, DH)
        all_keys = jnp.concatenate([kept_keys, new_keys[:, kv_head * DH:(kv_head + 1) * DH]], 0).astype(jnp.float32)
        all_values = jnp.concatenate([kept_values, new_values[:, kv_head * DH:(kv_head + 1) * DH]], 0).astype(jnp.float32)
        key_live = jnp.repeat(live_slots[:, kv_head, :].reshape(-1), TILE)
        query_head = queries[:, kv_head * group_size * DH:(kv_head + 1) * group_size * DH]
        query_head = query_head.reshape(N_CTX, Q_DEV, group_size, DH)

        def one_block(inputs, all_keys=all_keys, all_values=all_values, key_live=key_live):
            query_block, place_block = inputs
            scores = jnp.einsum("rhd,kd->rhk", query_block.astype(jnp.float32), all_keys) * score_scale
            cached_ok = jnp.broadcast_to(key_live[None, :], (Q_DEV, key_live.shape[0]))
            fresh_ok = place_block[:, None] >= place[None, :]
            allowed = jnp.concatenate([cached_ok, fresh_ok], 1)
            scores = jnp.where(allowed[:, None, :], scores, -jnp.inf)
            top_score = jnp.max(scores, axis=-1, keepdims=True)
            weights = jnp.exp(scores - top_score)
            totals = jnp.sum(weights, axis=-1)
            rounded = lax.optimization_barrier(weights.astype(jnp.bfloat16)).astype(jnp.float32)
            numerator = jnp.einsum("rhk,kd->rhd", rounded, all_values)
            return (numerator / totals[..., None]).astype(jnp.bfloat16)

        attn_head = lax.map(one_block, (query_head, place.reshape(N_CTX, Q_DEV)))
        head_outputs.append(attn_head.reshape(Q_TOTAL, group_size * DH))
    attn = jnp.concatenate(head_outputs, 1)
    return jnp.dot(attn, out_weight, preferred_element_type=jnp.float32)
```

```python
import functools
import math

import jax
import jax.numpy as jnp
from jax import lax
from jax.experimental import pallas as pl
from jax.experimental.pallas import tpu as pltpu
from jax.sharding import PartitionSpec as P

DH = 128
TILE = 128
LANES = 128
CHUNK = 4
LOW = -1e30
VMEM_ATTN = 40 * 2**20
VMEM_PROJ = 32 * 2**20


def attention_kernel(
    blocks, group, shift_ref, keep_ref, count_ref, k_ref, v_ref, nk_ref, nv_ref, *rest
):
    q_refs, rest = rest[:blocks], rest[blocks:]
    out_refs, (acc_ref, max_ref) = rest[:blocks], rest[blocks:]
    q_dev = q_refs[0].shape[0]
    kv_local = nk_ref.shape[1] // DH
    heads = kv_local * group
    rows = q_dev * group
    slots = keep_ref.shape[1]
    scale = math.log2(math.e) / math.sqrt(DH)
    lane = lax.broadcasted_iota(jnp.int32, (q_dev, LANES), 1)
    stats = [jnp.zeros((q_dev, LANES), jnp.float32) for _ in range(blocks)]
    ones_new = jnp.ones((q_dev, LANES), jnp.bfloat16)
    place_row = lax.broadcasted_iota(jnp.int32, (rows, q_dev), 0) % q_dev
    place_key = lax.broadcasted_iota(jnp.int32, (rows, q_dev), 1)
    contract_last = (((1,), (1,)), ((), ()))

    for g in range(kv_local):
        cols = slice(g * DH, (g + 1) * DH)
        queries = [
            jnp.concatenate(
                [q[:, (g * group + h) * DH : (g * group + h + 1) * DH] for h in range(group)], 0
            )
            for q in q_refs
        ]
        fresh_values = jnp.concatenate([nv_ref[:, cols], ones_new], 1)
        for b in range(blocks):
            s = lax.dot_general(
                queries[b], nk_ref[:, cols], contract_last, preferred_element_type=jnp.float32
            )
            live = place_row - place_key + shift_ref[b] >= 0
            s = jnp.where(live, s * scale, LOW)
            top = jnp.broadcast_to(jnp.max(s, axis=1, keepdims=True), (rows, LANES))
            p = jnp.exp2(s - top[:, :q_dev]).astype(jnp.bfloat16)
            max_ref[b] = top
            acc_ref[b] = jnp.dot(p, fresh_values, preferred_element_type=jnp.float32)

        count = count_ref[g]

        def chunk_step(chunk, carry, g=g, cols=cols, queries=queries, count=count):
            key_parts, value_parts = [], []
            for i in range(CHUNK):
                slot = chunk * CHUNK + i
                live = slot < count
                tile = keep_ref[g, jnp.where(live, slot, 0)]
                at = pl.ds(pl.multiple_of(tile * TILE, TILE), TILE)
                key_parts.append(k_ref[at, cols])
                tail = jnp.concatenate(
                    [v_ref[at, cols], jnp.ones((TILE, LANES), jnp.bfloat16)], 1
                )
                value_parts.append(jnp.where(live, tail, jnp.zeros_like(tail)))
            keys = jnp.concatenate(key_parts, 0)
            values = jnp.concatenate(value_parts, 0)
            for b in range(blocks):
                s = lax.dot_general(
                    queries[b], keys, contract_last, preferred_element_type=jnp.float32
                )
                old = max_ref[b]
                top = jnp.maximum(old, jnp.max(s, axis=1, keepdims=True) * scale)
                p = jnp.concatenate(
                    [
                        jnp.exp2(s[:, j * LANES : (j + 1) * LANES] * scale - top)
                        for j in range(CHUNK * TILE // LANES)
                    ],
                    1,
                ).astype(jnp.bfloat16)
                shrink = jnp.exp2(old - top)
                max_ref[b] = top
                acc_ref[b] = acc_ref[b] * jnp.concatenate([shrink, shrink], 1) + jnp.dot(
                    p, values, preferred_element_type=jnp.float32
                )
            return carry

        lax.fori_loop(0, (count + CHUNK - 1) // CHUNK, chunk_step, 0)

        for b in range(blocks):
            total = acc_ref[b, :, DH:]
            mean = acc_ref[b, :, :DH] / total
            level = max_ref[b] + jnp.log2(total)
            for h in range(group):
                head = g * group + h
                part = slice(h * q_dev, (h + 1) * q_dev)
                out_refs[b][:, head * DH : (head + 1) * DH] = mean[part].astype(jnp.bfloat16)
                stats[b] = jnp.where(lane % heads == head, level[part], stats[b])

    for b in range(blocks):
        high = stats[b].astype(jnp.bfloat16).astype(jnp.float32)
        middle = (stats[b] - high).astype(jnp.bfloat16).astype(jnp.float32)
        low = stats[b] - high - middle
        packed = jnp.where(lane < heads, high, jnp.where(lane < 2 * heads, middle, low))
        out_refs[b][:, heads * DH :] = packed.astype(jnp.bfloat16)


def attention_call(blocks, shift, keep, count, keys, values, new_keys, new_values):
    n = len(blocks)
    q_dev, width = blocks[0].shape
    kv_local = new_keys.shape[1] // DH
    group = width // DH // kv_local
    rows = q_dev * group
    smem = pl.BlockSpec(memory_space=pltpu.SMEM)
    vmem = pl.BlockSpec(memory_space=pltpu.VMEM)
    work = n * rows * kv_local * keep.shape[1] * TILE
    return pl.pallas_call(
        functools.partial(attention_kernel, n, group),
        out_shape=[jax.ShapeDtypeStruct((q_dev, width + LANES), jnp.bfloat16)] * n,
        in_specs=[smem] * 3 + [vmem] * (4 + n),
        out_specs=[vmem] * n,
        scratch_shapes=[
            pltpu.VMEM((n, rows, DH + LANES), jnp.float32),
            pltpu.VMEM((n, rows, LANES), jnp.float32),
        ],
        compiler_params=pltpu.CompilerParams(vmem_limit_bytes=VMEM_ATTN),
        cost_estimate=pl.CostEstimate(
            flops=work * DH * 8, bytes_accessed=8 * 2**20, transcendentals=work
        ),
        name="attention",
    )(shift, keep, count, keys, values, new_keys, new_values, *blocks)


def merge_kernel(parts, *refs):
    in_refs, out_ref = refs[:parts], refs[parts]
    width = out_ref.shape[1]
    heads = width // DH
    levels = []
    for ref in in_refs:
        packed = ref[:, width:].astype(jnp.float32)
        levels.append(
            packed
            + pltpu.roll(packed, LANES - heads, 1)
            + pltpu.roll(packed, LANES - 2 * heads, 1)
        )
    top = functools.reduce(jnp.maximum, levels)
    shares = [jnp.exp2(level - top) for level in levels]
    total = functools.reduce(jnp.add, shares)
    shares = [share / total for share in shares]
    for h in range(heads):
        cols = slice(h * DH, (h + 1) * DH)
        mixed = functools.reduce(
            jnp.add,
            [share[:, h : h + 1] * ref[:, cols].astype(jnp.float32) for share, ref in zip(shares, in_refs)],
        )
        out_ref[:, cols] = mixed.astype(jnp.bfloat16)


def merge_call(parts):
    q_dev, wide = parts[0].shape
    vmem = pl.BlockSpec(memory_space=pltpu.VMEM)
    return pl.pallas_call(
        functools.partial(merge_kernel, len(parts)),
        out_shape=jax.ShapeDtypeStruct((q_dev, wide - LANES), jnp.bfloat16),
        in_specs=[vmem] * len(parts),
        out_specs=vmem,
        cost_estimate=pl.CostEstimate(
            flops=len(parts) * q_dev * wide * 2,
            bytes_accessed=len(parts) * q_dev * wide * 2,
            transcendentals=0,
        ),
        name="merge",
    )(*parts)


def projection_kernel(blocks, peers, place_ref, w_ref, *rest):
    in_refs, rest = rest[:blocks], rest[blocks:]
    own_ref, send_refs, (rows_ref, sum_ref) = rest[0], rest[1:peers], rest[peers:]
    q_dev = in_refs[0].shape[0]
    for b in range(blocks):
        at = pl.ds(pl.multiple_of(place_ref[b] * q_dev, q_dev), q_dev)
        rows_ref[at, :] = in_refs[b][...]
    sum_ref[...] = jnp.dot(rows_ref[...], w_ref[...], preferred_element_type=jnp.float32)
    part = own_ref.shape[0]
    me = place_ref[blocks]

    def piece(j):
        return sum_ref[pl.ds(pl.multiple_of((me ^ j) * part, part), part), :]

    own_ref[...] = piece(0)
    for j in range(1, peers):
        send_refs[j - 1][...] = piece(j).astype(jnp.bfloat16)


def projection_call(blocks, places, weight, peers):
    n = len(blocks)
    q_dev, width = blocks[0].shape
    columns = weight.shape[1]
    part = n * q_dev // peers
    vmem = pl.BlockSpec(memory_space=pltpu.VMEM)
    return pl.pallas_call(
        functools.partial(projection_kernel, n, peers),
        out_shape=[jax.ShapeDtypeStruct((part, columns), jnp.float32)]
        + [jax.ShapeDtypeStruct((part, columns), jnp.bfloat16)] * (peers - 1),
        in_specs=[pl.BlockSpec(memory_space=pltpu.SMEM)] + [vmem] * (1 + n),
        out_specs=[vmem] * peers,
        scratch_shapes=[
            pltpu.VMEM((n * q_dev, width), jnp.bfloat16),
            pltpu.VMEM((n * q_dev, columns), jnp.float32),
        ],
        compiler_params=pltpu.CompilerParams(vmem_limit_bytes=VMEM_PROJ),
        cost_estimate=pl.CostEstimate(
            flops=2 * n * q_dev * width * columns,
            bytes_accessed=2 * width * columns,
            transcendentals=0,
        ),
        name="projection",
    )(places, weight, *blocks)


def body(
    queries,
    new_keys,
    new_values,
    cache_keys,
    cache_values,
    keep_tiles,
    tile_count,
    owner_slot,
    out_weight,
):
    ctx_count = lax.axis_size("ctx")
    peers = lax.axis_size("tp")
    low = 2
    high = ctx_count // low
    q_dev = queries.shape[0]
    me = lax.axis_index("ctx")
    me_high, me_low = me // low, me % low

    def owner(step, flip):
        return (me_high + step) % high * low + (me_low + flip) % low

    def move(x, step, flip):
        pairs = [
            (i, (i // low + step) % high * low + (i % low + flip) % low) for i in range(ctx_count)
        ]
        return lax.ppermute(x, "ctx", pairs)

    steps = sorted(range(1, high), key=lambda k: (min(k, high - k), k))
    order = [(0, 0), (0, 1)] + [(k, 0) for k in steps] + [(k, 1) for k in steps]

    def gather(x):
        held = {(0, 0): x, (0, 1): move(x, 0, 1)}
        for k in steps:
            held[k, 0] = move(x, -k, 0)
        for k in steps:
            held[k, 1] = move(held[k, 0], 0, 1)
        return held

    held = gather(queries)
    groups = [order[:1]]
    rest = order[1:]
    while len(rest) > 3:
        groups.append(rest[:2])
        rest = rest[2:]
    groups.append(rest)

    my_slot = owner_slot[me]
    parts = []
    for members in groups:
        shift = jnp.stack([(owner_slot[owner(*m)] - my_slot) * q_dev for m in members])
        outs = attention_call(
            [held[m] for m in members],
            shift.astype(jnp.int32),
            keep_tiles[0],
            tile_count[0],
            cache_keys,
            cache_values,
            new_keys,
            new_values,
        )
        for m, out in zip(members, outs):
            parts.append(out if m == (0, 0) else move(out, *m))
    attn = merge_call(parts)

    held = gather(attn)
    my_tp = lax.axis_index("tp")
    places = jnp.stack([owner(*m) for m in order] + [my_tp]).astype(jnp.int32)
    own, *sends = projection_call([held[m] for m in order], places, out_weight, peers)
    for j, piece in enumerate(sends, 1):
        got = lax.ppermute(piece, "tp", [(i, i ^ j) for i in range(peers)])
        own = own + got.astype(jnp.float32)
    return own


def solution(mesh):
    return jax.shard_map(
        body,
        mesh=mesh,
        in_specs=(
            P("ctx", "tp"),
            P("ctx", "tp"),
            P("ctx", "tp"),
            P("ctx", "tp"),
            P("ctx", "tp"),
            P("ctx", "tp", None),
            P("ctx", "tp"),
            P(),
            P("tp", "ctx"),
        ),
        out_specs=P("tp", "ctx"),
        check_vma=False,
    )
```

```python
import functools
import math

import jax
import jax.numpy as jnp
from jax import lax
from jax.experimental import pallas as pl
from jax.experimental.pallas import tpu as pltpu
from jax.sharding import PartitionSpec as P

DH = 128
TILE = 128
LANES = 128
CHUNK = 4
W_COLUMNS = 256
LOW = -1e30
LOW_SIZE = 2
VMEM_ATTN = 32 * 2**20
VMEM_MERGE = 8 * 2**20
VMEM_PROJ = 16 * 2**20


def flipped(me, count, step, flip):
    high = count // LOW_SIZE
    return lax.rem(me // LOW_SIZE + step, high) * LOW_SIZE + lax.rem(me + flip, LOW_SIZE)


def attention_kernel(
    members, ctx_count, group, slot_ref, keep_ref, count_ref, nk_ref, nv_ref, k_hbm, v_hbm, *rest
):
    blocks = len(members)
    q_refs, rest = rest[:blocks], rest[blocks:]
    out_refs, rest = rest[:blocks], rest[blocks:]
    k_ref, v_ref, q_ref, acc_ref, max_ref, sems = rest
    q_dev = q_refs[0].shape[0]
    kv_local = nk_ref.shape[1] // DH
    heads = kv_local * group
    rows = q_dev * group
    slots = keep_ref.shape[1]
    scale = math.log2(math.e) / math.sqrt(DH)
    me = lax.axis_index("ctx")
    my_slot = slot_ref[me]

    def fetches(g, slot):
        tile = keep_ref[g, jnp.where(slot < count_ref[g], slot, 0)]
        source = pl.ds(pl.multiple_of(tile * TILE, TILE), TILE)
        target = pl.ds(pl.multiple_of(slot * TILE, TILE), TILE)
        cols = slice(g * DH, (g + 1) * DH)
        return [
            pltpu.make_async_copy(
                hbm.at[source, cols], vmem.at[g, target, :], sems.at[which, g, slot]
            )
            for which, (hbm, vmem) in enumerate(((k_hbm, k_ref), (v_hbm, v_ref)))
        ]

    def chunks_of(g):
        return (count_ref[g] + CHUNK - 1) // CHUNK

    for g in range(kv_local):

        def start(slot, carry, g=g):
            for copy in fetches(g, slot):
                copy.start()
            return carry

        lax.fori_loop(0, chunks_of(g) * CHUNK, start, 0)

    lane = lax.broadcasted_iota(jnp.int32, (q_dev, LANES), 1)
    stats = [jnp.zeros((q_dev, LANES), jnp.float32) for _ in range(blocks)]
    ones_new = jnp.ones((q_dev, LANES), jnp.bfloat16)
    ones_chunk = jnp.ones((TILE, LANES), jnp.bfloat16)
    place_row = lax.broadcasted_iota(jnp.int32, (rows, q_dev), 0) % q_dev
    place_key = lax.broadcasted_iota(jnp.int32, (rows, q_dev), 1)
    contract_last = (((1,), (1,)), ((), ()))

    for g in range(kv_local):
        cols = slice(g * DH, (g + 1) * DH)
        fresh_values = jnp.concatenate([nv_ref[:, cols], ones_new], 1)
        for b in range(blocks):
            for h in range(group):
                head = g * group + h
                q_ref[b, h * q_dev : (h + 1) * q_dev, :] = q_refs[b][
                    :, head * DH : (head + 1) * DH
                ]
            s = lax.dot_general(
                q_ref[b], nk_ref[:, cols], contract_last, preferred_element_type=jnp.float32
            )
            shift = (slot_ref[flipped(me, ctx_count, *members[b])] - my_slot) * q_dev
            s = jnp.where(place_row - place_key + shift >= 0, s * scale, LOW)
            top = jnp.broadcast_to(jnp.max(s, axis=1, keepdims=True), (rows, LANES))
            p = jnp.exp2(s - top[:, :q_dev]).astype(jnp.bfloat16)
            max_ref[b] = top
            acc_ref[b] = jnp.dot(p, fresh_values, preferred_element_type=jnp.float32)

        def chunk_step(chunk, carry, g=g):
            for i in range(CHUNK):
                for copy in fetches(g, chunk * CHUNK + i):
                    copy.wait()
            span = CHUNK * TILE
            at = pl.ds(pl.multiple_of(chunk * span, span), span)
            keys = k_ref[g, at, :]
            value_parts = []
            for i in range(CHUNK):
                slot = chunk * CHUNK + i
                tile = v_ref[g, pl.ds(pl.multiple_of(slot * TILE, TILE), TILE), :]
                tail = jnp.concatenate([tile, ones_chunk], 1)
                value_parts.append(jnp.where(slot < count_ref[g], tail, jnp.zeros_like(tail)))
            values = jnp.concatenate(value_parts, 0)
            for b in range(blocks):
                s = lax.dot_general(
                    q_ref[b], keys, contract_last, preferred_element_type=jnp.float32
                )
                old = max_ref[b]
                top = jnp.maximum(old, jnp.max(s, axis=1, keepdims=True) * scale)
                p = jnp.concatenate(
                    [
                        jnp.exp2(s[:, j * LANES : (j + 1) * LANES] * scale - top)
                        for j in range(span // LANES)
                    ],
                    1,
                ).astype(jnp.bfloat16)
                shrink = jnp.exp2(old - top)
                max_ref[b] = top
                acc_ref[b] = acc_ref[b] * jnp.concatenate([shrink, shrink], 1) + jnp.dot(
                    p, values, preferred_element_type=jnp.float32
                )
            return carry

        lax.fori_loop(0, chunks_of(g), chunk_step, 0)

        for b in range(blocks):
            total = acc_ref[b, :, DH:]
            mean = acc_ref[b, :, :DH] / total
            level = max_ref[b] + jnp.log2(total)
            for h in range(group):
                head = g * group + h
                part = slice(h * q_dev, (h + 1) * q_dev)
                out_refs[b][:, head * DH : (head + 1) * DH] = mean[part].astype(jnp.bfloat16)
                stats[b] = jnp.where(lane % heads == head, level[part], stats[b])

    for b in range(blocks):
        high = stats[b].astype(jnp.bfloat16).astype(jnp.float32)
        middle = (stats[b] - high).astype(jnp.bfloat16).astype(jnp.float32)
        low = stats[b] - high - middle
        packed = jnp.where(lane < heads, high, jnp.where(lane < 2 * heads, middle, low))
        out_refs[b][:, heads * DH :] = packed.astype(jnp.bfloat16)


def attention_call(members, ctx_count, blocks, slots, keep, count, new_keys, new_values, keys, values):
    n = len(blocks)
    q_dev, width = blocks[0].shape
    kv_local = new_keys.shape[1] // DH
    group = width // DH // kv_local
    rows = q_dev * group
    padded = -(-keep.shape[1] // CHUNK) * CHUNK
    smem = pl.BlockSpec(memory_space=pltpu.SMEM)
    vmem = pl.BlockSpec(memory_space=pltpu.VMEM)
    hbm = pl.BlockSpec(memory_space=pltpu.HBM)
    work = n * rows * kv_local * keep.shape[1] * TILE
    return pl.pallas_call(
        functools.partial(attention_kernel, members, ctx_count, group),
        out_shape=[jax.ShapeDtypeStruct((q_dev, width + LANES), jnp.bfloat16)] * n,
        in_specs=[smem] * 3 + [vmem] * 2 + [hbm] * 2 + [vmem] * n,
        out_specs=[vmem] * n,
        scratch_shapes=[
            pltpu.VMEM((kv_local, padded * TILE, DH), jnp.bfloat16),
            pltpu.VMEM((kv_local, padded * TILE, DH), jnp.bfloat16),
            pltpu.VMEM((n, rows, DH), jnp.bfloat16),
            pltpu.VMEM((n, rows, DH + LANES), jnp.float32),
            pltpu.VMEM((n, rows, LANES), jnp.float32),
            pltpu.SemaphoreType.DMA((2, kv_local, padded)),
        ],
        compiler_params=pltpu.CompilerParams(vmem_limit_bytes=VMEM_ATTN),
        cost_estimate=pl.CostEstimate(
            flops=work * DH * 8, bytes_accessed=8 * 2**20, transcendentals=work
        ),
        name="attention",
    )(slots, keep, count, new_keys, new_values, keys, values, *blocks)


def merge_kernel(parts, *refs):
    in_refs, out_ref = refs[:parts], refs[parts]
    width = out_ref.shape[1]
    heads = width // DH
    levels = []
    for ref in in_refs:
        packed = ref[:, width:].astype(jnp.float32)
        levels.append(
            packed
            + pltpu.roll(packed, LANES - heads, 1)
            + pltpu.roll(packed, LANES - 2 * heads, 1)
        )
    top = functools.reduce(jnp.maximum, levels)
    shares = [jnp.exp2(level - top) for level in levels]
    total = functools.reduce(jnp.add, shares)
    shares = [share / total for share in shares]
    for h in range(heads):
        cols = slice(h * DH, (h + 1) * DH)
        mixed = functools.reduce(
            jnp.add,
            [share[:, h : h + 1] * ref[:, cols].astype(jnp.float32) for share, ref in zip(shares, in_refs)],
        )
        out_ref[:, cols] = mixed.astype(jnp.bfloat16)


def merge_call(parts):
    q_dev, wide = parts[0].shape
    vmem = pl.BlockSpec(memory_space=pltpu.VMEM)
    return pl.pallas_call(
        functools.partial(merge_kernel, len(parts)),
        out_shape=jax.ShapeDtypeStruct((q_dev, wide - LANES), jnp.bfloat16),
        in_specs=[vmem] * len(parts),
        out_specs=vmem,
        compiler_params=pltpu.CompilerParams(vmem_limit_bytes=VMEM_MERGE),
        cost_estimate=pl.CostEstimate(
            flops=len(parts) * q_dev * wide * 2,
            bytes_accessed=len(parts) * q_dev * wide * 2,
            transcendentals=0,
        ),
        name="merge",
    )(*parts)


def projection_kernel(members, ctx_count, peers, w_hbm, *rest):
    blocks = len(members)
    in_refs, rest = rest[:blocks], rest[blocks:]
    own_ref, send_refs, (rows_ref, sum_ref, w_ref, sems) = rest[0], rest[1:peers], rest[peers:]
    q_dev = in_refs[0].shape[0]
    w_parts = w_ref.shape[1] // W_COLUMNS
    copies = []
    for i in range(w_parts):
        cols = slice(i * W_COLUMNS, (i + 1) * W_COLUMNS)
        copies.append(pltpu.make_async_copy(w_hbm.at[:, cols], w_ref.at[:, cols], sems.at[i]))
        copies[-1].start()
    me = lax.axis_index("ctx")
    for member, ref in zip(members, in_refs):
        at = flipped(me, ctx_count, *member) * q_dev
        rows_ref[pl.ds(pl.multiple_of(at, q_dev), q_dev), :] = ref[...]
    part = own_ref.shape[0]
    my_tp = lax.axis_index("tp")
    for i in range(w_parts):
        cols = slice(i * W_COLUMNS, (i + 1) * W_COLUMNS)
        copies[i].wait()
        sum_ref[:, cols] = jnp.dot(
            rows_ref[...], w_ref[:, cols], preferred_element_type=jnp.float32
        )
    own_ref[...] = sum_ref[pl.ds(pl.multiple_of(my_tp * part, part), part), :]
    for j in range(1, peers):
        at = pl.multiple_of((my_tp ^ j) * part, part)
        send_refs[j - 1][...] = sum_ref[pl.ds(at, part), :].astype(jnp.bfloat16)


def projection_call(members, ctx_count, blocks, weight, peers):
    n = len(blocks)
    q_dev, width = blocks[0].shape
    columns = weight.shape[1]
    part = n * q_dev // peers
    vmem = pl.BlockSpec(memory_space=pltpu.VMEM)
    return pl.pallas_call(
        functools.partial(projection_kernel, members, ctx_count, peers),
        out_shape=[jax.ShapeDtypeStruct((part, columns), jnp.float32)]
        + [jax.ShapeDtypeStruct((part, columns), jnp.bfloat16)] * (peers - 1),
        in_specs=[pl.BlockSpec(memory_space=pltpu.HBM)] + [vmem] * n,
        out_specs=[vmem] * peers,
        scratch_shapes=[
            pltpu.VMEM((n * q_dev, width), jnp.bfloat16),
            pltpu.VMEM((n * q_dev, columns), jnp.float32),
            pltpu.VMEM(weight.shape, weight.dtype),
            pltpu.SemaphoreType.DMA((columns // W_COLUMNS,)),
        ],
        compiler_params=pltpu.CompilerParams(vmem_limit_bytes=VMEM_PROJ),
        cost_estimate=pl.CostEstimate(
            flops=2 * n * q_dev * width * columns,
            bytes_accessed=2 * width * columns,
            transcendentals=0,
        ),
        name="projection",
    )(weight, *blocks)


def body(
    queries,
    new_keys,
    new_values,
    cache_keys,
    cache_values,
    keep_tiles,
    tile_count,
    owner_slot,
    out_weight,
):
    ctx_count = lax.axis_size("ctx")
    peers = lax.axis_size("tp")
    low = LOW_SIZE
    high = ctx_count // low

    def move(x, step, flip):
        pairs = [
            (i, (i // low + step) % high * low + (i % low + flip) % low) for i in range(ctx_count)
        ]
        return lax.ppermute(x, "ctx", pairs)

    steps = sorted(range(1, high), key=lambda k: (min(k, high - k), k))
    order = [(0, 0), (0, 1)] + [(k, 0) for k in steps] + [(k, 1) for k in steps]

    def gather(x):
        held = {(0, 0): x, (0, 1): move(x, 0, 1)}
        for k in steps:
            held[k, 0] = move(x, -k, 0)
        for k in steps:
            held[k, 1] = move(held[k, 0], 0, 1)
        return held

    held = gather(queries)
    groups = [order[:1], order[1:4]]
    for at in range(4, ctx_count, 4):
        groups.append(order[at : at + 4])

    def attend(members, blocks):
        return attention_call(
            members,
            ctx_count,
            blocks,
            owner_slot,
            keep_tiles[0],
            tile_count[0],
            new_keys,
            new_values,
            cache_keys,
            cache_values,
        )

    parts = []
    last = None
    for members in groups:
        blocks = [held[m] for m in members]
        if last is not None:
            blocks, last = lax.optimization_barrier((blocks, last))
            parts[-1] = last
        outs = attend(members, blocks)
        parts.extend(outs)
        last = outs[-1]
    parts = [out if m == (0, 0) else move(out, *m) for m, out in zip(order, parts)]
    attn = merge_call(parts)

    held = gather(attn)
    own, *sends = projection_call(order, ctx_count, [held[m] for m in order], out_weight, peers)
    for j, piece in enumerate(sends, 1):
        got = lax.ppermute(piece, "tp", [(i, i ^ j) for i in range(peers)])
        own = own + got.astype(jnp.float32)
    return own


def solution(mesh):
    return jax.shard_map(
        body,
        mesh=mesh,
        in_specs=(
            P("ctx", "tp"),
            P("ctx", "tp"),
            P("ctx", "tp"),
            P("ctx", "tp"),
            P("ctx", "tp"),
            P("ctx", "tp", None),
            P("ctx", "tp"),
            P(),
            P("tp", "ctx"),
        ),
        out_specs=P("tp", "ctx"),
        check_vma=False,
    )
```

```python
import functools
import math

import jax
import jax.numpy as jnp
from jax import lax
from jax.experimental import pallas as pl
from jax.experimental.pallas import tpu as pltpu
from jax.sharding import PartitionSpec as P

DH = 128
TILE = 128
LANES = 128
CHUNK = 4
LOW = -1e30
LOW_SIZE = 2
VMEM_ATTN = 60 * 2**20
VMEM_MERGE = 8 * 2**20
VMEM_PROJ = 16 * 2**20


def flipped(me, count, step, flip):
    high = count // LOW_SIZE
    return lax.rem(me // LOW_SIZE + step, high) * LOW_SIZE + lax.rem(me + flip, LOW_SIZE)


def attention_kernel(
    members, ctx_count, group, slot_ref, keep_ref, count_ref, nk_ref, nv_ref, k_hbm, v_hbm, *rest
):
    blocks = len(members)
    q_refs, rest = rest[:blocks], rest[blocks:]
    out_refs, rest = rest[:blocks], rest[blocks:]
    k_ref, v_ref, q_ref, acc_ref, max_ref, sems = rest
    copies = [
        pltpu.make_async_copy(k_hbm, k_ref, sems.at[0]),
        pltpu.make_async_copy(v_hbm, v_ref, sems.at[1]),
    ]
    for copy in copies:
        copy.start()
    q_dev = q_refs[0].shape[0]
    kv_local = nk_ref.shape[1] // DH
    heads = kv_local * group
    rows = q_dev * group
    span = CHUNK * TILE
    scale = math.log2(math.e) / math.sqrt(DH)
    me = lax.axis_index("ctx")
    my_slot = slot_ref[me]
    lane = lax.broadcasted_iota(jnp.int32, (q_dev, LANES), 1)
    ones_new = jnp.ones((q_dev, LANES), jnp.bfloat16)
    ones_tile = jnp.ones((TILE, LANES), jnp.bfloat16)
    place_row = lax.broadcasted_iota(jnp.int32, (rows, q_dev), 0) % q_dev
    place_key = lax.broadcasted_iota(jnp.int32, (rows, q_dev), 1)
    contract_last = (((1,), (1,)), ((), ()))

    for g in range(kv_local):
        cols = slice(g * DH, (g + 1) * DH)
        fresh_values = jnp.concatenate([nv_ref[:, cols], ones_new], 1)
        for b in range(blocks):
            for h in range(group):
                head = g * group + h
                q_ref[g, b, h * q_dev : (h + 1) * q_dev, :] = q_refs[b][
                    :, head * DH : (head + 1) * DH
                ]
            s = lax.dot_general(
                q_ref[g, b], nk_ref[:, cols], contract_last, preferred_element_type=jnp.float32
            )
            shift = (slot_ref[flipped(me, ctx_count, *members[b])] - my_slot) * q_dev
            s = jnp.where(place_row - place_key + shift >= 0, s * scale, LOW)
            top = jnp.broadcast_to(jnp.max(s, axis=1, keepdims=True), (rows, LANES))
            p = jnp.exp2(s - top[:, :q_dev]).astype(jnp.bfloat16)
            max_ref[g, b] = top
            acc_ref[g, b] = jnp.dot(p, fresh_values, preferred_element_type=jnp.float32)

    for copy in copies:
        copy.wait()

    def chunk_step(g, chunk):
        cols = slice(g * DH, (g + 1) * DH)
        count = count_ref[g]
        key_parts, value_parts = [], []
        for i in range(CHUNK):
            slot = chunk * CHUNK + i
            live = slot < count
            tile = keep_ref[g, jnp.where(live, slot, 0)]
            at = pl.ds(pl.multiple_of(tile * TILE, TILE), TILE)
            key_parts.append(k_ref[at, cols])
            tail = jnp.concatenate([v_ref[at, cols], ones_tile], 1)
            value_parts.append(jnp.where(live, tail, jnp.zeros_like(tail)))
        keys = jnp.concatenate(key_parts, 0)
        values = jnp.concatenate(value_parts, 0)
        for b in range(blocks):
            s = lax.dot_general(
                q_ref[g, b], keys, contract_last, preferred_element_type=jnp.float32
            )
            old = max_ref[g, b]
            top = jnp.maximum(old, jnp.max(s, axis=1, keepdims=True) * scale)
            p = jnp.concatenate(
                [
                    jnp.exp2(s[:, j * LANES : (j + 1) * LANES] * scale - top)
                    for j in range(span // LANES)
                ],
                1,
            ).astype(jnp.bfloat16)
            shrink = jnp.exp2(old - top)
            max_ref[g, b] = top
            acc_ref[g, b] = acc_ref[g, b] * jnp.concatenate([shrink, shrink], 1) + jnp.dot(
                p, values, preferred_element_type=jnp.float32
            )

    ends = [(count_ref[g] + CHUNK - 1) // CHUNK for g in range(kv_local)]
    shared = functools.reduce(jnp.minimum, ends)

    def step_all(chunk, carry):
        for g in range(kv_local):
            chunk_step(g, chunk)
        return carry

    lax.fori_loop(0, shared, step_all, 0)
    for g in range(kv_local):

        def step_one(chunk, carry, g=g):
            chunk_step(g, chunk)
            return carry

        lax.fori_loop(shared, ends[g], step_one, 0)

    stats = [jnp.zeros((q_dev, LANES), jnp.float32) for _ in range(blocks)]
    for b in range(blocks):
        for g in range(kv_local):
            total = acc_ref[g, b, :, DH:]
            mean = acc_ref[g, b, :, :DH] / total
            level = max_ref[g, b] + jnp.log2(total)
            for h in range(group):
                head = g * group + h
                part = slice(h * q_dev, (h + 1) * q_dev)
                out_refs[b][:, head * DH : (head + 1) * DH] = mean[part].astype(jnp.bfloat16)
                stats[b] = jnp.where(lane % heads == head, level[part], stats[b])

    for b in range(blocks):
        high = stats[b].astype(jnp.bfloat16).astype(jnp.float32)
        middle = (stats[b] - high).astype(jnp.bfloat16).astype(jnp.float32)
        low = stats[b] - high - middle
        packed = jnp.where(lane < heads, high, jnp.where(lane < 2 * heads, middle, low))
        out_refs[b][:, heads * DH :] = packed.astype(jnp.bfloat16)


def attention_call(members, ctx_count, blocks, slots, keep, count, new_keys, new_values, keys, values):
    n = len(blocks)
    q_dev, width = blocks[0].shape
    kv_local = new_keys.shape[1] // DH
    group = width // DH // kv_local
    rows = q_dev * group
    smem = pl.BlockSpec(memory_space=pltpu.SMEM)
    vmem = pl.BlockSpec(memory_space=pltpu.VMEM)
    hbm = pl.BlockSpec(memory_space=pltpu.HBM)
    work = n * rows * kv_local * keep.shape[1] * TILE
    return pl.pallas_call(
        functools.partial(attention_kernel, members, ctx_count, group),
        out_shape=[jax.ShapeDtypeStruct((q_dev, width + LANES), jnp.bfloat16)] * n,
        in_specs=[smem] * 3 + [vmem] * 2 + [hbm] * 2 + [vmem] * n,
        out_specs=[vmem] * n,
        scratch_shapes=[
            pltpu.VMEM(keys.shape, keys.dtype),
            pltpu.VMEM(values.shape, values.dtype),
            pltpu.VMEM((kv_local, n, rows, DH), jnp.bfloat16),
            pltpu.VMEM((kv_local, n, rows, DH + LANES), jnp.float32),
            pltpu.VMEM((kv_local, n, rows, LANES), jnp.float32),
            pltpu.SemaphoreType.DMA((2,)),
        ],
        compiler_params=pltpu.CompilerParams(vmem_limit_bytes=VMEM_ATTN),
        cost_estimate=pl.CostEstimate(
            flops=work * DH * 8, bytes_accessed=8 * 2**20, transcendentals=work
        ),
        name="attention",
    )(slots, keep, count, new_keys, new_values, keys, values, *blocks)


def merge_kernel(parts, *refs):
    in_refs, out_ref = refs[:parts], refs[parts]
    width = out_ref.shape[1]
    heads = width // DH
    levels = []
    for ref in in_refs:
        packed = ref[:, width:].astype(jnp.float32)
        levels.append(
            packed
            + pltpu.roll(packed, LANES - heads, 1)
            + pltpu.roll(packed, LANES - 2 * heads, 1)
        )
    top = functools.reduce(jnp.maximum, levels)
    shares = [jnp.exp2(level - top) for level in levels]
    total = functools.reduce(jnp.add, shares)
    shares = [share / total for share in shares]
    for h in range(heads):
        cols = slice(h * DH, (h + 1) * DH)
        mixed = functools.reduce(
            jnp.add,
            [share[:, h : h + 1] * ref[:, cols].astype(jnp.float32) for share, ref in zip(shares, in_refs)],
        )
        out_ref[:, cols] = mixed.astype(jnp.bfloat16)


def merge_call(parts):
    q_dev, wide = parts[0].shape
    vmem = pl.BlockSpec(memory_space=pltpu.VMEM)
    return pl.pallas_call(
        functools.partial(merge_kernel, len(parts)),
        out_shape=jax.ShapeDtypeStruct((q_dev, wide - LANES), jnp.bfloat16),
        in_specs=[vmem] * len(parts),
        out_specs=vmem,
        compiler_params=pltpu.CompilerParams(vmem_limit_bytes=VMEM_MERGE),
        cost_estimate=pl.CostEstimate(
            flops=len(parts) * q_dev * wide * 2,
            bytes_accessed=len(parts) * q_dev * wide * 2,
            transcendentals=0,
        ),
        name="merge",
    )(*parts)


def projection_kernel(members, ctx_count, peers, w_ref, *rest):
    blocks = len(members)
    in_refs, rest = rest[:blocks], rest[blocks:]
    own_ref, send_refs, (rows_ref, sum_ref) = rest[0], rest[1:peers], rest[peers:]
    q_dev = in_refs[0].shape[0]
    me = lax.axis_index("ctx")
    for member, ref in zip(members, in_refs):
        at = flipped(me, ctx_count, *member) * q_dev
        rows_ref[pl.ds(pl.multiple_of(at, q_dev), q_dev), :] = ref[...]
    part = own_ref.shape[0]
    my_tp = lax.axis_index("tp")
    sum_ref[...] = jnp.dot(rows_ref[...], w_ref[...], preferred_element_type=jnp.float32)
    own_ref[...] = sum_ref[pl.ds(pl.multiple_of(my_tp * part, part), part), :]
    for j in range(1, peers):
        at = pl.multiple_of((my_tp ^ j) * part, part)
        send_refs[j - 1][...] = sum_ref[pl.ds(at, part), :].astype(jnp.bfloat16)


def projection_call(members, ctx_count, blocks, weight, peers):
    n = len(blocks)
    q_dev, width = blocks[0].shape
    columns = weight.shape[1]
    part = n * q_dev // peers
    vmem = pl.BlockSpec(memory_space=pltpu.VMEM)
    return pl.pallas_call(
        functools.partial(projection_kernel, members, ctx_count, peers),
        out_shape=[jax.ShapeDtypeStruct((part, columns), jnp.float32)]
        + [jax.ShapeDtypeStruct((part, columns), jnp.bfloat16)] * (peers - 1),
        in_specs=[vmem] * (1 + n),
        out_specs=[vmem] * peers,
        scratch_shapes=[
            pltpu.VMEM((n * q_dev, width), jnp.bfloat16),
            pltpu.VMEM((n * q_dev, columns), jnp.float32),
        ],
        compiler_params=pltpu.CompilerParams(vmem_limit_bytes=VMEM_PROJ),
        cost_estimate=pl.CostEstimate(
            flops=2 * n * q_dev * width * columns,
            bytes_accessed=2 * width * columns,
            transcendentals=0,
        ),
        name="projection",
    )(weight, *blocks)


def body(
    queries,
    new_keys,
    new_values,
    cache_keys,
    cache_values,
    keep_tiles,
    tile_count,
    owner_slot,
    out_weight,
):
    ctx_count = lax.axis_size("ctx")
    peers = lax.axis_size("tp")
    low = LOW_SIZE
    high = ctx_count // low

    def move(x, step, flip):
        pairs = [
            (i, (i // low + step) % high * low + (i % low + flip) % low) for i in range(ctx_count)
        ]
        return lax.ppermute(x, "ctx", pairs)

    steps = sorted(range(1, high), key=lambda k: (min(k, high - k), k))
    order = [(k, 0) for k in (0, *steps)] + [(k, 1) for k in (0, *steps)]

    def gather(x):
        held = {(0, 0): x, (0, 1): move(x, 0, 1)}
        for k in steps:
            held[k, 0] = move(x, -k, 0)
        for k in steps:
            held[k, 1] = move(held[k, 0], 0, 1)
        return held

    held = gather(queries)
    groups = [order[:1], order[1:4]]
    for at in range(4, ctx_count, 4):
        groups.append(order[at : at + 4])

    def attend(members, blocks):
        return attention_call(
            members,
            ctx_count,
            blocks,
            owner_slot,
            keep_tiles[0],
            tile_count[0],
            new_keys,
            new_values,
            cache_keys,
            cache_values,
        )

    parts = []
    last = None
    for members in groups:
        blocks = [held[m] for m in members]
        if last is not None:
            blocks, last = lax.optimization_barrier((blocks, last))
            parts[-1] = last
        outs = attend(members, blocks)
        parts.extend(outs)
        last = outs[-1]
    parts = [out if m == (0, 0) else move(out, *m) for m, out in zip(order, parts)]
    attn = merge_call(parts)

    held = gather(attn)
    own, *sends = projection_call(order, ctx_count, [held[m] for m in order], out_weight, peers)
    for j, piece in enumerate(sends, 1):
        got = lax.ppermute(piece, "tp", [(i, i ^ j) for i in range(peers)])
        own = own + got.astype(jnp.float32)
    return own


def solution(mesh):
    return jax.shard_map(
        body,
        mesh=mesh,
        in_specs=(
            P("ctx", "tp"),
            P("ctx", "tp"),
            P("ctx", "tp"),
            P("ctx", "tp"),
            P("ctx", "tp"),
            P("ctx", "tp", None),
            P("ctx", "tp"),
            P(),
            P("tp", "ctx"),
        ),
        out_specs=P("tp", "ctx"),
        check_vma=False,
    )
```

```python
import functools
import math

import jax
import jax.numpy as jnp
from jax import lax
from jax.experimental import pallas as pl
from jax.experimental.pallas import tpu as pltpu
from jax.sharding import PartitionSpec as P

DH = 128
TILE = 128
LANES = 128
CHUNK = 4
LOW = -1e30
LOW_SIZE = 2
VMEM_ATTN = 24 * 2**20
VMEM_MERGE = 8 * 2**20
VMEM_PROJ = 16 * 2**20


def flipped(me, count, step, flip):
    high = count // LOW_SIZE
    return lax.rem(me // LOW_SIZE + step, high) * LOW_SIZE + lax.rem(me + flip, LOW_SIZE)


def attention_kernel(
    members, ctx_count, group, slot_ref, keep_ref, count_ref, nk_ref, nv_ref, k_ref, v_ref, *rest
):
    blocks = len(members)
    q_refs, rest = rest[:blocks], rest[blocks:]
    out_refs, rest = rest[:blocks], rest[blocks:]
    q_ref, acc_ref, max_ref = rest
    q_dev = q_refs[0].shape[0]
    kv_local = nk_ref.shape[1] // DH
    heads = kv_local * group
    rows = q_dev * group
    span = CHUNK * TILE
    scale = math.log2(math.e) / math.sqrt(DH)
    me = lax.axis_index("ctx")
    my_slot = slot_ref[me]
    lane = lax.broadcasted_iota(jnp.int32, (q_dev, LANES), 1)
    ones_new = jnp.ones((q_dev, LANES), jnp.bfloat16)
    ones_tile = jnp.ones((TILE, LANES), jnp.bfloat16)
    place_row = lax.broadcasted_iota(jnp.int32, (rows, q_dev), 0) % q_dev
    place_key = lax.broadcasted_iota(jnp.int32, (rows, q_dev), 1)
    contract_last = (((1,), (1,)), ((), ()))

    for g in range(kv_local):
        cols = slice(g * DH, (g + 1) * DH)
        fresh_values = jnp.concatenate([nv_ref[:, cols], ones_new], 1)
        for b in range(blocks):
            for h in range(group):
                head = g * group + h
                q_ref[g, b, h * q_dev : (h + 1) * q_dev, :] = q_refs[b][
                    :, head * DH : (head + 1) * DH
                ]
            s = lax.dot_general(
                q_ref[g, b], nk_ref[:, cols], contract_last, preferred_element_type=jnp.float32
            )
            shift = (slot_ref[flipped(me, ctx_count, *members[b])] - my_slot) * q_dev
            s = jnp.where(place_row - place_key + shift >= 0, s * scale, LOW)
            top = jnp.broadcast_to(jnp.max(s, axis=1, keepdims=True), (rows, LANES))
            p = jnp.exp2(s - top[:, :q_dev]).astype(jnp.bfloat16)
            max_ref[g, b] = top
            acc_ref[g, b] = jnp.dot(p, fresh_values, preferred_element_type=jnp.float32)

    def chunk_step(g, chunk):
        cols = slice(g * DH, (g + 1) * DH)
        count = count_ref[g]
        key_parts, value_parts = [], []
        for i in range(CHUNK):
            slot = chunk * CHUNK + i
            live = slot < count
            tile = keep_ref[g, jnp.where(live, slot, 0)]
            at = pl.ds(pl.multiple_of(tile * TILE, TILE), TILE)
            key_parts.append(k_ref[at, cols])
            tail = jnp.concatenate([v_ref[at, cols], ones_tile], 1)
            value_parts.append(jnp.where(live, tail, jnp.zeros_like(tail)))
        keys = jnp.concatenate(key_parts, 0)
        values = jnp.concatenate(value_parts, 0)
        for b in range(blocks):
            s = lax.dot_general(
                q_ref[g, b], keys, contract_last, preferred_element_type=jnp.float32
            )
            old = max_ref[g, b]
            top = jnp.maximum(old, jnp.max(s, axis=1, keepdims=True) * scale)
            p = jnp.concatenate(
                [
                    jnp.exp2(s[:, j * LANES : (j + 1) * LANES] * scale - top)
                    for j in range(span // LANES)
                ],
                1,
            ).astype(jnp.bfloat16)
            shrink = jnp.exp2(old - top)
            max_ref[g, b] = top
            acc_ref[g, b] = acc_ref[g, b] * jnp.concatenate([shrink, shrink], 1) + jnp.dot(
                p, values, preferred_element_type=jnp.float32
            )

    ends = [(count_ref[g] + CHUNK - 1) // CHUNK for g in range(kv_local)]
    shared = functools.reduce(jnp.minimum, ends)

    def step_all(chunk, carry):
        for g in range(kv_local):
            chunk_step(g, chunk)
        return carry

    lax.fori_loop(0, shared, step_all, 0)
    for g in range(kv_local):

        def step_one(chunk, carry, g=g):
            chunk_step(g, chunk)
            return carry

        lax.fori_loop(shared, ends[g], step_one, 0)

    stats = [jnp.zeros((q_dev, LANES), jnp.float32) for _ in range(blocks)]
    for b in range(blocks):
        for g in range(kv_local):
            total = acc_ref[g, b, :, DH:]
            mean = acc_ref[g, b, :, :DH] / total
            level = max_ref[g, b] + jnp.log2(total)
            for h in range(group):
                head = g * group + h
                part = slice(h * q_dev, (h + 1) * q_dev)
                out_refs[b][:, head * DH : (head + 1) * DH] = mean[part].astype(jnp.bfloat16)
                stats[b] = jnp.where(lane % heads == head, level[part], stats[b])

    for b in range(blocks):
        high = stats[b].astype(jnp.bfloat16).astype(jnp.float32)
        middle = (stats[b] - high).astype(jnp.bfloat16).astype(jnp.float32)
        low = stats[b] - high - middle
        packed = jnp.where(lane < heads, high, jnp.where(lane < 2 * heads, middle, low))
        out_refs[b][:, heads * DH :] = packed.astype(jnp.bfloat16)


def attention_call(members, ctx_count, blocks, slots, keep, count, new_keys, new_values, keys, values):
    n = len(blocks)
    q_dev, width = blocks[0].shape
    kv_local = new_keys.shape[1] // DH
    group = width // DH // kv_local
    rows = q_dev * group
    smem = pl.BlockSpec(memory_space=pltpu.SMEM)
    vmem = pl.BlockSpec(memory_space=pltpu.VMEM)
    work = n * rows * kv_local * keep.shape[1] * TILE
    return pl.pallas_call(
        functools.partial(attention_kernel, members, ctx_count, group),
        out_shape=[jax.ShapeDtypeStruct((q_dev, width + LANES), jnp.bfloat16)] * n,
        in_specs=[smem] * 3 + [vmem] * (4 + n),
        out_specs=[vmem] * n,
        scratch_shapes=[
            pltpu.VMEM((kv_local, n, rows, DH), jnp.bfloat16),
            pltpu.VMEM((kv_local, n, rows, DH + LANES), jnp.float32),
            pltpu.VMEM((kv_local, n, rows, LANES), jnp.float32),
        ],
        compiler_params=pltpu.CompilerParams(vmem_limit_bytes=VMEM_ATTN),
        cost_estimate=pl.CostEstimate(
            flops=work * DH * 8, bytes_accessed=8 * 2**20, transcendentals=work
        ),
        name="attention",
    )(slots, keep, count, new_keys, new_values, keys, values, *blocks)


def merge_kernel(parts, *refs):
    in_refs, out_ref = refs[:parts], refs[parts]
    width = out_ref.shape[1]
    heads = width // DH
    levels = []
    for ref in in_refs:
        packed = ref[:, width:].astype(jnp.float32)
        levels.append(
            packed
            + pltpu.roll(packed, LANES - heads, 1)
            + pltpu.roll(packed, LANES - 2 * heads, 1)
        )
    top = functools.reduce(jnp.maximum, levels)
    shares = [jnp.exp2(level - top) for level in levels]
    total = functools.reduce(jnp.add, shares)
    shares = [share / total for share in shares]
    for h in range(heads):
        cols = slice(h * DH, (h + 1) * DH)
        mixed = functools.reduce(
            jnp.add,
            [share[:, h : h + 1] * ref[:, cols].astype(jnp.float32) for share, ref in zip(shares, in_refs)],
        )
        out_ref[:, cols] = mixed.astype(jnp.bfloat16)


def merge_call(parts):
    q_dev, wide = parts[0].shape
    vmem = pl.BlockSpec(memory_space=pltpu.VMEM)
    return pl.pallas_call(
        functools.partial(merge_kernel, len(parts)),
        out_shape=jax.ShapeDtypeStruct((q_dev, wide - LANES), jnp.bfloat16),
        in_specs=[vmem] * len(parts),
        out_specs=vmem,
        compiler_params=pltpu.CompilerParams(vmem_limit_bytes=VMEM_MERGE),
        cost_estimate=pl.CostEstimate(
            flops=len(parts) * q_dev * wide * 2,
            bytes_accessed=len(parts) * q_dev * wide * 2,
            transcendentals=0,
        ),
        name="merge",
    )(*parts)


def projection_kernel(members, ctx_count, peers, w_ref, *rest):
    blocks = len(members)
    in_refs, rest = rest[:blocks], rest[blocks:]
    own_ref, send_refs, (rows_ref, sum_ref) = rest[0], rest[1:peers], rest[peers:]
    q_dev = in_refs[0].shape[0]
    me = lax.axis_index("ctx")
    for member, ref in zip(members, in_refs):
        at = flipped(me, ctx_count, *member) * q_dev
        rows_ref[pl.ds(pl.multiple_of(at, q_dev), q_dev), :] = ref[...]
    part = own_ref.shape[0]
    my_tp = lax.axis_index("tp")
    sum_ref[...] = jnp.dot(rows_ref[...], w_ref[...], preferred_element_type=jnp.float32)
    own_ref[...] = sum_ref[pl.ds(pl.multiple_of(my_tp * part, part), part), :]
    for j in range(1, peers):
        at = pl.multiple_of((my_tp ^ j) * part, part)
        send_refs[j - 1][...] = sum_ref[pl.ds(at, part), :].astype(jnp.bfloat16)


def projection_call(members, ctx_count, blocks, weight, peers):
    n = len(blocks)
    q_dev, width = blocks[0].shape
    columns = weight.shape[1]
    part = n * q_dev // peers
    vmem = pl.BlockSpec(memory_space=pltpu.VMEM)
    return pl.pallas_call(
        functools.partial(projection_kernel, members, ctx_count, peers),
        out_shape=[jax.ShapeDtypeStruct((part, columns), jnp.float32)]
        + [jax.ShapeDtypeStruct((part, columns), jnp.bfloat16)] * (peers - 1),
        in_specs=[vmem] * (1 + n),
        out_specs=[vmem] * peers,
        scratch_shapes=[
            pltpu.VMEM((n * q_dev, width), jnp.bfloat16),
            pltpu.VMEM((n * q_dev, columns), jnp.float32),
        ],
        compiler_params=pltpu.CompilerParams(vmem_limit_bytes=VMEM_PROJ),
        cost_estimate=pl.CostEstimate(
            flops=2 * n * q_dev * width * columns,
            bytes_accessed=2 * width * columns,
            transcendentals=0,
        ),
        name="projection",
    )(weight, *blocks)


def body(
    queries,
    new_keys,
    new_values,
    cache_keys,
    cache_values,
    keep_tiles,
    tile_count,
    owner_slot,
    out_weight,
):
    ctx_count = lax.axis_size("ctx")
    peers = lax.axis_size("tp")
    low = LOW_SIZE
    high = ctx_count // low

    def move(x, step, flip):
        pairs = [
            (i, (i // low + step) % high * low + (i % low + flip) % low) for i in range(ctx_count)
        ]
        return lax.ppermute(x, "ctx", pairs)

    steps = sorted(range(1, high), key=lambda k: (min(k, high - k), k))
    order = [(k, 0) for k in (0, *steps)] + [(k, 1) for k in (0, *steps)]

    def gather(x, chained):
        held = {(0, 0): x, (0, 1): move(x, 0, 1)}
        for k in steps:
            held[k, 0] = move(x, -k, 0)
        behind = None
        for k in steps:
            block = held[k, 0]
            if chained and 2 * k == high and behind is not None:
                block, held[behind] = lax.optimization_barrier((block, held[behind]))
            held[k, 1] = move(block, 0, 1)
            behind = (k, 1)
        return held

    held = gather(queries, False)
    groups = [order[:1], order[1:4]]
    for at in range(4, ctx_count, 4):
        groups.append(order[at : at + 4])

    def attend(members, blocks):
        return attention_call(
            members,
            ctx_count,
            blocks,
            owner_slot,
            keep_tiles[0],
            tile_count[0],
            new_keys,
            new_values,
            cache_keys,
            cache_values,
        )

    parts = []
    last = None
    for members in groups:
        blocks = [held[m] for m in members]
        if last is not None:
            blocks, last = lax.optimization_barrier((blocks, last))
            parts[-1] = last
        outs = attend(members, blocks)
        parts.extend(outs)
        last = outs[-1]
    parts = [out if m == (0, 0) else move(out, *m) for m, out in zip(order, parts)]
    attn = merge_call(parts)

    held = gather(attn, True)
    own, *sends = projection_call(order, ctx_count, [held[m] for m in order], out_weight, peers)
    for j, piece in enumerate(sends, 1):
        got = lax.ppermute(piece, "tp", [(i, i ^ j) for i in range(peers)])
        own = own + got.astype(jnp.float32)
    return own


def solution(mesh):
    return jax.shard_map(
        body,
        mesh=mesh,
        in_specs=(
            P("ctx", "tp"),
            P("ctx", "tp"),
            P("ctx", "tp"),
            P("ctx", "tp"),
            P("ctx", "tp"),
            P("ctx", "tp", None),
            P("ctx", "tp"),
            P(),
            P("tp", "ctx"),
        ),
        out_specs=P("tp", "ctx"),
        check_vma=False,
    )
```

```python
import functools
import math

import jax
import jax.numpy as jnp
from jax import lax
from jax.experimental import pallas as pl
from jax.experimental.pallas import tpu as pltpu
from jax.sharding import PartitionSpec as P

DH = 128
TILE = 128
LANES = 128
CHUNK = 4
LOW = -1e30
LOW_SIZE = 2
VMEM_ATTN = 24 * 2**20
VMEM_MERGE = 8 * 2**20
VMEM_PROJ = 16 * 2**20


def flipped(me, count, step, flip):
    high = count // LOW_SIZE
    return lax.rem(me // LOW_SIZE + step, high) * LOW_SIZE + lax.rem(me + flip, LOW_SIZE)


def attention_kernel(
    members, ctx_count, group, kv_heads, slot_ref, keep_ref, count_ref, nk_ref, nv_ref, k_ref, v_ref, *rest
):
    blocks = len(members)
    q_refs, rest = rest[:blocks], rest[blocks:]
    out_refs, rest = rest[: len(kv_heads)], rest[len(kv_heads) :]
    q_ref, acc_ref, max_ref = rest
    q_dev = q_refs[0].shape[0]
    rows = q_dev * group
    span = CHUNK * TILE
    scale = math.log2(math.e) / math.sqrt(DH)
    me = lax.axis_index("ctx")
    my_slot = slot_ref[me]
    lane = lax.broadcasted_iota(jnp.int32, (q_dev, LANES), 1)
    ones_new = jnp.ones((q_dev, LANES), jnp.bfloat16)
    ones_tile = jnp.ones((TILE, LANES), jnp.bfloat16)
    place_row = lax.broadcasted_iota(jnp.int32, (rows, q_dev), 0) % q_dev
    place_key = lax.broadcasted_iota(jnp.int32, (rows, q_dev), 1)
    contract_last = (((1,), (1,)), ((), ()))

    for at_g, g in enumerate(kv_heads):
        cols = slice(g * DH, (g + 1) * DH)
        fresh_values = jnp.concatenate([nv_ref[:, cols], ones_new], 1)
        for b in range(blocks):
            for h in range(group):
                head = g * group + h
                q_ref[at_g, b, h * q_dev : (h + 1) * q_dev, :] = q_refs[b][
                    :, head * DH : (head + 1) * DH
                ]
            s = lax.dot_general(
                q_ref[at_g, b], nk_ref[:, cols], contract_last, preferred_element_type=jnp.float32
            )
            shift = (slot_ref[flipped(me, ctx_count, *members[b])] - my_slot) * q_dev
            s = jnp.where(place_row - place_key + shift >= 0, s * scale, LOW)
            top = jnp.broadcast_to(jnp.max(s, axis=1, keepdims=True), (rows, LANES))
            p = jnp.exp2(s - top[:, :q_dev]).astype(jnp.bfloat16)
            max_ref[at_g, b] = top
            acc_ref[at_g, b] = jnp.dot(p, fresh_values, preferred_element_type=jnp.float32)

    def chunk_step(at_g, chunk):
        g = kv_heads[at_g]
        cols = slice(g * DH, (g + 1) * DH)
        count = count_ref[g]
        key_parts, value_parts = [], []
        for i in range(CHUNK):
            slot = chunk * CHUNK + i
            live = slot < count
            tile = keep_ref[g, jnp.where(live, slot, 0)]
            at = pl.ds(pl.multiple_of(tile * TILE, TILE), TILE)
            key_parts.append(k_ref[at, cols])
            tail = jnp.concatenate([v_ref[at, cols], ones_tile], 1)
            value_parts.append(jnp.where(live, tail, jnp.zeros_like(tail)))
        keys = jnp.concatenate(key_parts, 0)
        values = jnp.concatenate(value_parts, 0)
        for b in range(blocks):
            s = lax.dot_general(
                q_ref[at_g, b], keys, contract_last, preferred_element_type=jnp.float32
            )
            old = max_ref[at_g, b]
            top = jnp.maximum(old, jnp.max(s, axis=1, keepdims=True) * scale)
            p = jnp.concatenate(
                [
                    jnp.exp2(s[:, j * LANES : (j + 1) * LANES] * scale - top)
                    for j in range(span // LANES)
                ],
                1,
            ).astype(jnp.bfloat16)
            shrink = jnp.exp2(old - top)
            max_ref[at_g, b] = top
            acc_ref[at_g, b] = acc_ref[at_g, b] * jnp.concatenate([shrink, shrink], 1) + jnp.dot(
                p, values, preferred_element_type=jnp.float32
            )

    ends = [(count_ref[g] + CHUNK - 1) // CHUNK for g in kv_heads]
    shared = functools.reduce(jnp.minimum, ends)

    def step_all(chunk, carry):
        for at_g in range(len(kv_heads)):
            chunk_step(at_g, chunk)
        return carry

    lax.fori_loop(0, shared, step_all, 0)
    if len(kv_heads) > 1:
        for at_g in range(len(kv_heads)):

            def step_one(chunk, carry, at_g=at_g):
                chunk_step(at_g, chunk)
                return carry

            lax.fori_loop(shared, ends[at_g], step_one, 0)

    for at_g in range(len(kv_heads)):
        out_ref = out_refs[at_g]
        for b in range(blocks):
            to = 0 if blocks == 1 else flipped(me, ctx_count, *members[b])
            total = acc_ref[at_g, b, :, DH:]
            mean = acc_ref[at_g, b, :, :DH] / total
            level = max_ref[at_g, b] + jnp.log2(total)
            stats = jnp.zeros((q_dev, LANES), jnp.float32)
            for h in range(group):
                part = slice(h * q_dev, (h + 1) * q_dev)
                out_ref[to, :, h * DH : (h + 1) * DH] = mean[part].astype(jnp.bfloat16)
                stats = jnp.where(lane % group == h, level[part], stats)
            high = stats.astype(jnp.bfloat16).astype(jnp.float32)
            middle = (stats - high).astype(jnp.bfloat16).astype(jnp.float32)
            low = stats - high - middle
            packed = jnp.where(lane < group, high, jnp.where(lane < 2 * group, middle, low))
            out_ref[to, :, group * DH :] = packed.astype(jnp.bfloat16)
        if blocks > 1:
            out_ref[me] = jnp.zeros(out_ref.shape[1:], out_ref.dtype)


def attention_call(
    members, ctx_count, kv_heads, blocks, slots, keep, count, new_keys, new_values, keys, values
):
    n = len(blocks)
    q_dev, width = blocks[0].shape
    group = width // new_keys.shape[1]
    rows = q_dev * group
    smem = pl.BlockSpec(memory_space=pltpu.SMEM)
    vmem = pl.BlockSpec(memory_space=pltpu.VMEM)
    work = n * rows * len(kv_heads) * keep.shape[1] * TILE
    places = 1 if n == 1 else ctx_count
    return pl.pallas_call(
        functools.partial(attention_kernel, members, ctx_count, group, kv_heads),
        out_shape=[
            jax.ShapeDtypeStruct((places, q_dev, group * DH + LANES), jnp.bfloat16)
            for _ in kv_heads
        ],
        in_specs=[smem] * 3 + [vmem] * (4 + n),
        out_specs=[vmem] * len(kv_heads),
        scratch_shapes=[
            pltpu.VMEM((len(kv_heads), n, rows, DH), jnp.bfloat16),
            pltpu.VMEM((len(kv_heads), n, rows, DH + LANES), jnp.float32),
            pltpu.VMEM((len(kv_heads), n, rows, LANES), jnp.float32),
        ],
        compiler_params=pltpu.CompilerParams(vmem_limit_bytes=VMEM_ATTN),
        cost_estimate=pl.CostEstimate(
            flops=work * DH * 8, bytes_accessed=8 * 2**20, transcendentals=work
        ),
        name="attention",
    )(slots, keep, count, new_keys, new_values, keys, values, *blocks)


def merge_kernel(kv_local, *refs):
    got_refs, own_refs, out_ref = refs[:kv_local], refs[kv_local : 2 * kv_local], refs[-1]
    ctx_count = got_refs[0].shape[0]
    heads = out_ref.shape[1] // DH // kv_local
    me = lax.axis_index("ctx")
    for g in range(kv_local):
        parts = [own_refs[g][0]]
        for i in range(1, ctx_count):
            parts.append(got_refs[g][lax.rem(me + i, ctx_count)])
        levels = []
        for part in parts:
            packed = part[:, heads * DH :].astype(jnp.float32)
            levels.append(
                packed
                + pltpu.roll(packed, LANES - heads, 1)
                + pltpu.roll(packed, LANES - 2 * heads, 1)
            )
        top = functools.reduce(jnp.maximum, levels)
        shares = [jnp.exp2(level - top) for level in levels]
        total = functools.reduce(jnp.add, shares)
        shares = [share / total for share in shares]
        for h in range(heads):
            cols = slice(h * DH, (h + 1) * DH)
            mixed = functools.reduce(
                jnp.add,
                [
                    share[:, h : h + 1] * part[:, cols].astype(jnp.float32)
                    for share, part in zip(shares, parts)
                ],
            )
            to = (g * heads + h) * DH
            out_ref[:, to : to + DH] = mixed.astype(jnp.bfloat16)


def merge_call(got, own):
    kv_local = len(got)
    ctx_count, q_dev, wide = got[0].shape
    vmem = pl.BlockSpec(memory_space=pltpu.VMEM)
    return pl.pallas_call(
        functools.partial(merge_kernel, kv_local),
        out_shape=jax.ShapeDtypeStruct((q_dev, (wide - LANES) * kv_local), jnp.bfloat16),
        in_specs=[vmem] * (2 * kv_local),
        out_specs=vmem,
        compiler_params=pltpu.CompilerParams(vmem_limit_bytes=VMEM_MERGE),
        cost_estimate=pl.CostEstimate(
            flops=kv_local * ctx_count * q_dev * wide * 2,
            bytes_accessed=kv_local * ctx_count * q_dev * wide * 2,
            transcendentals=0,
        ),
        name="merge",
    )(*got, *own)


def projection_kernel(members, ctx_count, peers, w_ref, *rest):
    blocks = len(members)
    in_refs, rest = rest[:blocks], rest[blocks:]
    own_ref, send_refs, (rows_ref, sum_ref) = rest[0], rest[1:peers], rest[peers:]
    q_dev = in_refs[0].shape[0]
    me = lax.axis_index("ctx")
    for member, ref in zip(members, in_refs):
        at = flipped(me, ctx_count, *member) * q_dev
        rows_ref[pl.ds(pl.multiple_of(at, q_dev), q_dev), :] = ref[...]
    part = own_ref.shape[0]
    my_tp = lax.axis_index("tp")
    sum_ref[...] = jnp.dot(rows_ref[...], w_ref[...], preferred_element_type=jnp.float32)
    own_ref[...] = sum_ref[pl.ds(pl.multiple_of(my_tp * part, part), part), :]
    for j in range(1, peers):
        at = pl.multiple_of((my_tp ^ j) * part, part)
        send_refs[j - 1][...] = sum_ref[pl.ds(at, part), :].astype(jnp.bfloat16)


def projection_call(members, ctx_count, blocks, weight, peers):
    n = len(blocks)
    q_dev, width = blocks[0].shape
    columns = weight.shape[1]
    part = n * q_dev // peers
    vmem = pl.BlockSpec(memory_space=pltpu.VMEM)
    return pl.pallas_call(
        functools.partial(projection_kernel, members, ctx_count, peers),
        out_shape=[jax.ShapeDtypeStruct((part, columns), jnp.float32)]
        + [jax.ShapeDtypeStruct((part, columns), jnp.bfloat16)] * (peers - 1),
        in_specs=[vmem] * (1 + n),
        out_specs=[vmem] * peers,
        scratch_shapes=[
            pltpu.VMEM((n * q_dev, width), jnp.bfloat16),
            pltpu.VMEM((n * q_dev, columns), jnp.float32),
        ],
        compiler_params=pltpu.CompilerParams(vmem_limit_bytes=VMEM_PROJ),
        cost_estimate=pl.CostEstimate(
            flops=2 * n * q_dev * width * columns,
            bytes_accessed=2 * width * columns,
            transcendentals=0,
        ),
        name="projection",
    )(weight, *blocks)


def body(
    queries,
    new_keys,
    new_values,
    cache_keys,
    cache_values,
    keep_tiles,
    tile_count,
    owner_slot,
    out_weight,
):
    ctx_count = lax.axis_size("ctx")
    peers = lax.axis_size("tp")
    low = LOW_SIZE
    high = ctx_count // low

    def move(x, step, flip):
        pairs = [
            (i, (i // low + step) % high * low + (i % low + flip) % low) for i in range(ctx_count)
        ]
        return lax.ppermute(x, "ctx", pairs)

    steps = sorted(range(1, high), key=lambda k: (min(k, high - k), k))
    order = [(k, 0) for k in (0, *steps)] + [(k, 1) for k in (0, *steps)]

    def gather(x, chained):
        held = {(0, 0): x, (0, 1): move(x, 0, 1)}
        for k in steps:
            held[k, 0] = move(x, -k, 0)
        behind = None
        for k in steps:
            block = held[k, 0]
            if chained and 2 * k == high and behind is not None:
                block, held[behind] = lax.optimization_barrier((block, held[behind]))
            held[k, 1] = move(block, 0, 1)
            behind = (k, 1)
        return held

    held = gather(queries, False)
    kv_local = new_keys.shape[1] // DH

    def attend(members, kv_heads, blocks):
        return attention_call(
            members,
            ctx_count,
            kv_heads,
            blocks,
            owner_slot,
            keep_tiles[0],
            tile_count[0],
            new_keys,
            new_values,
            cache_keys,
            cache_values,
        )

    own_parts = attend(order[:1], list(range(kv_local)), [held[order[0]]])
    blocks = [held[m] for m in order[1:]]
    blocks, own_parts = lax.optimization_barrier((blocks, own_parts))
    got = []
    for g in range(kv_local):
        (part,) = attend(order[1:], [g], blocks)
        got.append(lax.all_to_all(part, "ctx", 0, 0, tiled=True))
        blocks, part = lax.optimization_barrier((blocks, part))
    attn = merge_call(got, own_parts)

    held = gather(attn, True)
    own, *sends = projection_call(order, ctx_count, [held[m] for m in order], out_weight, peers)
    for j, piece in enumerate(sends, 1):
        got = lax.ppermute(piece, "tp", [(i, i ^ j) for i in range(peers)])
        own = own + got.astype(jnp.float32)
    return own


def solution(mesh):
    return jax.shard_map(
        body,
        mesh=mesh,
        in_specs=(
            P("ctx", "tp"),
            P("ctx", "tp"),
            P("ctx", "tp"),
            P("ctx", "tp"),
            P("ctx", "tp"),
            P("ctx", "tp", None),
            P("ctx", "tp"),
            P(),
            P("tp", "ctx"),
        ),
        out_specs=P("tp", "ctx"),
        check_vma=False,
    )
```

```python
import functools
import math

import jax
import jax.numpy as jnp
from jax import lax
from jax.experimental import pallas as pl
from jax.experimental.pallas import tpu as pltpu
from jax.sharding import PartitionSpec as P

DH = 128
TILE = 128
LANES = 128
CHUNK = 4
LOW = -1e30
LOW_SIZE = 2
VMEM_ATTN = 24 * 2**20
VMEM_MERGE = 8 * 2**20
VMEM_PROJ = 16 * 2**20


def flipped(me, count, step, flip):
    high = count // LOW_SIZE
    return lax.rem(me // LOW_SIZE + step, high) * LOW_SIZE + lax.rem(me + flip, LOW_SIZE)


def attention_kernel(
    members, ctx_count, group, kv_local, slots, table_ref, new_ref, k_ref, v_ref, *rest
):
    blocks = len(members)
    q_refs, rest = rest[:blocks], rest[blocks:]
    out_refs, rest = rest[:blocks], rest[blocks:]
    q_ref, acc_ref, max_ref = rest
    q_dev = q_refs[0].shape[0]
    heads = kv_local * group
    rows = q_dev * group
    span = CHUNK * TILE
    scale = math.log2(math.e) / math.sqrt(DH)
    me = lax.axis_index("ctx")

    def count_of(g):
        return table_ref[kv_local * slots + g]

    def slot_of(ctx):
        return table_ref[kv_local * (slots + 1) + ctx]

    lane = lax.broadcasted_iota(jnp.int32, (q_dev, LANES), 1)
    ones_new = jnp.ones((q_dev, LANES), jnp.bfloat16)
    ones_tile = jnp.ones((TILE, LANES), jnp.bfloat16)
    place_row = lax.broadcasted_iota(jnp.int32, (rows, q_dev), 0) % q_dev
    place_key = lax.broadcasted_iota(jnp.int32, (rows, q_dev), 1)
    contract_last = (((1,), (1,)), ((), ()))

    for g in range(kv_local):
        cols = slice(g * DH, (g + 1) * DH)
        fresh_keys = new_ref[:, cols]
        fresh_values = jnp.concatenate(
            [new_ref[:, (kv_local + g) * DH : (kv_local + g + 1) * DH], ones_new], 1
        )
        for b in range(blocks):
            for h in range(group):
                head = g * group + h
                q_ref[g, b, h * q_dev : (h + 1) * q_dev, :] = q_refs[b][
                    :, head * DH : (head + 1) * DH
                ]
            s = lax.dot_general(
                q_ref[g, b], fresh_keys, contract_last, preferred_element_type=jnp.float32
            )
            shift = (slot_of(flipped(me, ctx_count, *members[b])) - slot_of(me)) * q_dev
            s = jnp.where(place_row - place_key + shift >= 0, s * scale, LOW)
            top = jnp.broadcast_to(jnp.max(s, axis=1, keepdims=True), (rows, LANES))
            p = jnp.exp2(s - top[:, :q_dev]).astype(jnp.bfloat16)
            max_ref[g, b] = top
            acc_ref[g, b] = jnp.dot(p, fresh_values, preferred_element_type=jnp.float32)

    def load_chunk(g, chunk):
        cols = slice(g * DH, (g + 1) * DH)
        key_parts, value_parts = [], []
        for i in range(CHUNK):
            slot = chunk * CHUNK + i
            live = slot < count_of(g)
            tile = table_ref[g * slots + jnp.where(live, slot, 0)]
            at = pl.ds(pl.multiple_of(tile * TILE, TILE), TILE)
            key_parts.append(k_ref[at, cols])
            tail = jnp.concatenate([v_ref[at, cols], ones_tile], 1)
            value_parts.append(jnp.where(live, tail, jnp.zeros_like(tail)))
        return jnp.concatenate(key_parts, 0), jnp.concatenate(value_parts, 0)

    def run(kv_heads, chunk):
        loaded = {g: load_chunk(g, chunk) for g in kv_heads}
        chains = [(g, b) for b in range(blocks) for g in kv_heads]

        def score(g, b):
            return lax.dot_general(
                q_ref[g, b], loaded[g][0], contract_last, preferred_element_type=jnp.float32
            )

        ahead = score(*chains[0])
        for at, (g, b) in enumerate(chains):
            s = ahead
            if at + 1 < len(chains):
                ahead = score(*chains[at + 1])
            old = max_ref[g, b]
            top = jnp.maximum(old, jnp.max(s, axis=1, keepdims=True) * scale)
            p = jnp.concatenate(
                [
                    jnp.exp2(s[:, j * LANES : (j + 1) * LANES] * scale - top)
                    for j in range(span // LANES)
                ],
                1,
            ).astype(jnp.bfloat16)
            shrink = jnp.exp2(old - top)
            max_ref[g, b] = top
            acc_ref[g, b] = acc_ref[g, b] * jnp.concatenate([shrink, shrink], 1) + jnp.dot(
                p, loaded[g][1], preferred_element_type=jnp.float32
            )

    ends = [(count_of(g) + CHUNK - 1) // CHUNK for g in range(kv_local)]
    shared = functools.reduce(jnp.minimum, ends)

    def step_all(chunk, carry):
        run(range(kv_local), chunk)
        return carry

    lax.fori_loop(0, shared, step_all, 0)
    for g in range(kv_local):

        def step_one(chunk, carry, g=g):
            run([g], chunk)
            return carry

        lax.fori_loop(shared, ends[g], step_one, 0)

    stats = [jnp.zeros((q_dev, LANES), jnp.float32) for _ in range(blocks)]
    for b in range(blocks):
        for g in range(kv_local):
            total = acc_ref[g, b, :, DH:]
            mean = acc_ref[g, b, :, :DH] / total
            level = max_ref[g, b] + jnp.log2(total)
            for h in range(group):
                head = g * group + h
                part = slice(h * q_dev, (h + 1) * q_dev)
                out_refs[b][:, head * DH : (head + 1) * DH] = mean[part].astype(jnp.bfloat16)
                stats[b] = jnp.where(lane % heads == head, level[part], stats[b])

    for b in range(blocks):
        high = stats[b].astype(jnp.bfloat16).astype(jnp.float32)
        middle = (stats[b] - high).astype(jnp.bfloat16).astype(jnp.float32)
        low = stats[b] - high - middle
        packed = jnp.where(lane < heads, high, jnp.where(lane < 2 * heads, middle, low))
        out_refs[b][:, heads * DH :] = packed.astype(jnp.bfloat16)


def attention_call(members, ctx_count, kv_local, slots, blocks, table, new_rows, keys, values):
    n = len(blocks)
    q_dev, width = blocks[0].shape
    group = width // DH // kv_local
    rows = q_dev * group
    smem = pl.BlockSpec(memory_space=pltpu.SMEM)
    vmem = pl.BlockSpec(memory_space=pltpu.VMEM)
    work = n * rows * kv_local * slots * TILE
    return pl.pallas_call(
        functools.partial(attention_kernel, members, ctx_count, group, kv_local, slots),
        out_shape=[jax.ShapeDtypeStruct((q_dev, width + LANES), jnp.bfloat16)] * n,
        in_specs=[smem] + [vmem] * (3 + n),
        out_specs=[vmem] * n,
        scratch_shapes=[
            pltpu.VMEM((kv_local, n, rows, DH), jnp.bfloat16),
            pltpu.VMEM((kv_local, n, rows, DH + LANES), jnp.float32),
            pltpu.VMEM((kv_local, n, rows, LANES), jnp.float32),
        ],
        compiler_params=pltpu.CompilerParams(vmem_limit_bytes=VMEM_ATTN),
        cost_estimate=pl.CostEstimate(
            flops=work * DH * 8, bytes_accessed=8 * 2**20, transcendentals=work
        ),
        name="attention",
    )(table, new_rows, keys, values, *blocks)


def merge_kernel(parts, *refs):
    in_refs, out_ref = refs[:parts], refs[parts]
    width = out_ref.shape[1]
    heads = width // DH
    levels = []
    for ref in in_refs:
        packed = ref[:, width:].astype(jnp.float32)
        levels.append(
            packed
            + pltpu.roll(packed, LANES - heads, 1)
            + pltpu.roll(packed, LANES - 2 * heads, 1)
        )
    top = functools.reduce(jnp.maximum, levels)
    shares = [jnp.exp2(level - top) for level in levels]
    total = functools.reduce(jnp.add, shares)
    shares = [share / total for share in shares]
    for h in range(heads):
        cols = slice(h * DH, (h + 1) * DH)
        mixed = functools.reduce(
            jnp.add,
            [share[:, h : h + 1] * ref[:, cols].astype(jnp.float32) for share, ref in zip(shares, in_refs)],
        )
        out_ref[:, cols] = mixed.astype(jnp.bfloat16)


def merge_call(parts):
    q_dev, wide = parts[0].shape
    vmem = pl.BlockSpec(memory_space=pltpu.VMEM)
    return pl.pallas_call(
        functools.partial(merge_kernel, len(parts)),
        out_shape=jax.ShapeDtypeStruct((q_dev, wide - LANES), jnp.bfloat16),
        in_specs=[vmem] * len(parts),
        out_specs=vmem,
        compiler_params=pltpu.CompilerParams(vmem_limit_bytes=VMEM_MERGE),
        cost_estimate=pl.CostEstimate(
            flops=len(parts) * q_dev * wide * 2,
            bytes_accessed=len(parts) * q_dev * wide * 2,
            transcendentals=0,
        ),
        name="merge",
    )(*parts)


def projection_kernel(members, ctx_count, peers, w_ref, *rest):
    blocks = len(members)
    in_refs, rest = rest[:blocks], rest[blocks:]
    own_ref, send_refs, (rows_ref, sum_ref) = rest[0], rest[1:peers], rest[peers:]
    q_dev = in_refs[0].shape[0]
    me = lax.axis_index("ctx")
    for member, ref in zip(members, in_refs):
        at = flipped(me, ctx_count, *member) * q_dev
        rows_ref[pl.ds(pl.multiple_of(at, q_dev), q_dev), :] = ref[...]
    part = own_ref.shape[0]
    my_tp = lax.axis_index("tp")
    sum_ref[...] = jnp.dot(rows_ref[...], w_ref[...], preferred_element_type=jnp.float32)
    own_ref[...] = sum_ref[pl.ds(pl.multiple_of(my_tp * part, part), part), :]
    for j in range(1, peers):
        at = pl.multiple_of((my_tp ^ j) * part, part)
        send_refs[j - 1][...] = sum_ref[pl.ds(at, part), :].astype(jnp.bfloat16)


def projection_call(members, ctx_count, blocks, weight, peers):
    n = len(blocks)
    q_dev, width = blocks[0].shape
    columns = weight.shape[1]
    part = n * q_dev // peers
    vmem = pl.BlockSpec(memory_space=pltpu.VMEM)
    return pl.pallas_call(
        functools.partial(projection_kernel, members, ctx_count, peers),
        out_shape=[jax.ShapeDtypeStruct((part, columns), jnp.float32)]
        + [jax.ShapeDtypeStruct((part, columns), jnp.bfloat16)] * (peers - 1),
        in_specs=[vmem] * (1 + n),
        out_specs=[vmem] * peers,
        scratch_shapes=[
            pltpu.VMEM((n * q_dev, width), jnp.bfloat16),
            pltpu.VMEM((n * q_dev, columns), jnp.float32),
        ],
        compiler_params=pltpu.CompilerParams(vmem_limit_bytes=VMEM_PROJ),
        cost_estimate=pl.CostEstimate(
            flops=2 * n * q_dev * width * columns,
            bytes_accessed=2 * width * columns,
            transcendentals=0,
        ),
        name="projection",
    )(weight, *blocks)


def body(
    queries,
    new_keys,
    new_values,
    cache_keys,
    cache_values,
    keep_tiles,
    tile_count,
    owner_slot,
    out_weight,
):
    ctx_count = lax.axis_size("ctx")
    peers = lax.axis_size("tp")
    low = LOW_SIZE
    high = ctx_count // low

    def move(x, step, flip):
        pairs = [
            (i, (i // low + step) % high * low + (i % low + flip) % low) for i in range(ctx_count)
        ]
        return lax.ppermute(x, "ctx", pairs)

    steps = sorted(range(1, high), key=lambda k: (min(k, high - k), k))
    order = [(k, 0) for k in (0, *steps)] + [(k, 1) for k in (0, *steps)]

    def gather(x, chained):
        held = {(0, 0): x, (0, 1): move(x, 0, 1)}
        for k in steps:
            held[k, 0] = move(x, -k, 0)
        behind = None
        for k in steps:
            block = held[k, 0]
            if chained and 2 * k == high and behind is not None:
                block, held[behind] = lax.optimization_barrier((block, held[behind]))
            held[k, 1] = move(block, 0, 1)
            behind = (k, 1)
        return held

    held = gather(queries, False)
    near = [m for m in order[1:] if not m[1]]
    far = sorted((m for m in order if m[1]), key=lambda m: -min(m[0], high - m[0]))
    groups = [order[:1]] + [near[i : i + 3] for i in range(0, len(near), 3)]
    groups += [far[i : i + 2] for i in range(0, len(far), 2)]
    kv_local = new_keys.shape[1] // DH
    table = jnp.concatenate([keep_tiles.reshape(-1), tile_count.reshape(-1), owner_slot])
    new_rows = jnp.concatenate([new_keys, new_values], 1)

    def attend(members, blocks):
        return attention_call(
            members,
            ctx_count,
            kv_local,
            keep_tiles.shape[2],
            blocks,
            table,
            new_rows,
            cache_keys,
            cache_values,
        )

    parts, back = {}, {}
    last = None
    for index, members in enumerate(groups):
        blocks = [held[m] for m in members]
        if last is not None:
            blocks, parts[last] = lax.optimization_barrier((blocks, parts[last]))
        if index >= 3:
            returned = {m: back[m] for m in groups[index - 2] if 2 * m[0] != high}
            blocks, returned = lax.optimization_barrier((blocks, returned))
            back.update(returned)
        parts.update(zip(members, attend(members, blocks)))
        last = members[-1]
        for m in members:
            back[m] = parts[m] if m == (0, 0) else move(parts[m], *m)
    attn = merge_call([back[m] for m in order])

    held = gather(attn, True)
    own, *sends = projection_call(order, ctx_count, [held[m] for m in order], out_weight, peers)
    for j, piece in enumerate(sends, 1):
        got = lax.ppermute(piece, "tp", [(i, i ^ j) for i in range(peers)])
        own = own + got.astype(jnp.float32)
    return own


def solution(mesh):
    return jax.shard_map(
        body,
        mesh=mesh,
        in_specs=(
            P("ctx", "tp"),
            P("ctx", "tp"),
            P("ctx", "tp"),
            P("ctx", "tp"),
            P("ctx", "tp"),
            P("ctx", "tp", None),
            P("ctx", "tp"),
            P(),
            P("tp", "ctx"),
        ),
        out_specs=P("tp", "ctx"),
        check_vma=False,
    )
```

```python
import functools
import math

import jax
import jax.numpy as jnp
from jax import lax
from jax.experimental import pallas as pl
from jax.experimental.pallas import tpu as pltpu
from jax.sharding import PartitionSpec as P

DH = 128
TILE = 128
LANES = 128
CHUNK = 4
LOW = -1e30
ONES = 16
LOW_SIZE = 2
VMEM_ATTN = 24 * 2**20
VMEM_MERGE = 8 * 2**20
VMEM_PROJ = 16 * 2**20


def flipped(me, count, step, flip):
    high = count // LOW_SIZE
    return lax.rem(me // LOW_SIZE + step, high) * LOW_SIZE + lax.rem(me + flip, LOW_SIZE)


def attention_kernel(
    members, ctx_count, group, kv_local, slots, table_ref, new_ref, k_ref, v_ref, *rest
):
    blocks = len(members)
    q_refs, rest = rest[:blocks], rest[blocks:]
    out_refs, rest = rest[:blocks], rest[blocks:]
    q_ref, turned_ref, acc_ref, max_ref = rest
    q_dev = q_refs[0].shape[0]
    heads = kv_local * group
    rows = q_dev * group
    span = CHUNK * TILE
    scale = math.log2(math.e) / math.sqrt(DH)
    me = lax.axis_index("ctx")

    def count_of(g):
        return table_ref[kv_local * slots + g]

    def slot_of(ctx):
        return table_ref[kv_local * (slots + 1) + ctx]

    def turned(x):
        return x.astype(jnp.float32).T.astype(jnp.bfloat16)

    def fold(g, b, s, values, first=False):
        peak = jnp.max(s, axis=0, keepdims=True) * scale
        top = peak if first else jnp.maximum(max_ref[g, b, :1], peak)
        p = jnp.exp2(s * scale - top).astype(jnp.bfloat16)
        mixed = jnp.dot(values, p, preferred_element_type=jnp.float32)
        if not first:
            mixed += acc_ref[g, b] * jnp.exp2(max_ref[g, b, :1] - top)
        max_ref[g, b] = jnp.broadcast_to(top, max_ref.shape[2:])
        acc_ref[g, b] = mixed

    ones_tile = jnp.ones((ONES, TILE), jnp.bfloat16)
    place_key = lax.broadcasted_iota(jnp.int32, (TILE, rows), 0)
    place_row = lax.broadcasted_iota(jnp.int32, (TILE, rows), 1) % q_dev
    padding = jnp.zeros((TILE - q_dev, DH), jnp.bfloat16)

    for g in range(kv_local):
        fresh_keys = jnp.concatenate([new_ref[:, g * DH : (g + 1) * DH], padding], 0)
        fresh_values = new_ref[:, (kv_local + g) * DH : (kv_local + g + 1) * DH]
        fresh_values = jnp.concatenate(
            [turned(jnp.concatenate([fresh_values, padding], 0)), ones_tile], 0
        )
        for b in range(blocks):
            for h in range(group):
                head = g * group + h
                q_ref[h * q_dev : (h + 1) * q_dev, :] = q_refs[b][
                    :, head * DH : (head + 1) * DH
                ].astype(jnp.float32)
            turned_ref[g, b] = q_ref[...].T.astype(jnp.bfloat16)
            s = jnp.dot(fresh_keys, turned_ref[g, b], preferred_element_type=jnp.float32)
            shift = (slot_of(flipped(me, ctx_count, *members[b])) - slot_of(me)) * q_dev
            live = (place_key < q_dev) & (place_row - place_key + shift >= 0)
            fold(g, b, jnp.where(live, s, LOW), fresh_values, first=True)

    def load_chunk(g, chunk):
        cols = slice(g * DH, (g + 1) * DH)
        key_parts, value_parts = [], []
        for i in range(CHUNK):
            slot = chunk * CHUNK + i
            live = slot < count_of(g)
            tile = table_ref[g * slots + jnp.where(live, slot, 0)]
            at = pl.ds(pl.multiple_of(tile * TILE, TILE), TILE)
            key_parts.append(k_ref[at, cols])
            tail = jnp.concatenate([turned(v_ref[at, cols]), ones_tile], 0)
            value_parts.append(jnp.where(live, tail, jnp.zeros_like(tail)))
        return jnp.concatenate(key_parts, 0), jnp.concatenate(value_parts, 1)

    def run(kv_heads, chunk):
        loaded = {g: load_chunk(g, chunk) for g in kv_heads}
        chains = [(g, b) for b in range(blocks) for g in kv_heads]

        def score(g, b):
            return jnp.dot(loaded[g][0], turned_ref[g, b], preferred_element_type=jnp.float32)

        ahead = score(*chains[0])
        for at, (g, b) in enumerate(chains):
            s = ahead
            if at + 1 < len(chains):
                ahead = score(*chains[at + 1])
            fold(g, b, s, loaded[g][1])

    ends = [(count_of(g) + CHUNK - 1) // CHUNK for g in range(kv_local)]
    shared = functools.reduce(jnp.minimum, ends)

    def step_all(chunk, carry):
        run(range(kv_local), chunk)
        return carry

    lax.fori_loop(0, shared, step_all, 0)
    for g in range(kv_local):

        def step_one(chunk, carry, g=g):
            run([g], chunk)
            return carry

        lax.fori_loop(shared, ends[g], step_one, 0)

    sublane = lax.broadcasted_iota(jnp.int32, (q_dev, LANES), 0)
    parts = rows // LANES
    for b in range(blocks):
        stats = jnp.zeros((q_dev, LANES), jnp.float32)
        for g in range(kv_local):
            total = acc_ref[g, b, DH : DH + 1, :]
            mean = (acc_ref[g, b, :DH, :] / total).T.astype(jnp.bfloat16)
            for h in range(group):
                head = g * group + h
                out_refs[b][:, head * DH : (head + 1) * DH] = mean[h * q_dev : (h + 1) * q_dev]
            level = max_ref[g, b, :1] + jnp.log2(total)
            high = level.astype(jnp.bfloat16).astype(jnp.float32)
            middle = (level - high).astype(jnp.bfloat16).astype(jnp.float32)
            for i, term in enumerate((high, middle, level - high - middle)):
                for j in range(parts):
                    at = (g * 3 + i) * parts + j
                    stats = jnp.where(sublane == at, term[:, j * LANES : (j + 1) * LANES], stats)
        out_refs[b][:, heads * DH :] = stats.astype(jnp.bfloat16)


def attention_call(members, ctx_count, kv_local, slots, blocks, table, new_rows, keys, values):
    n = len(blocks)
    q_dev, width = blocks[0].shape
    group = width // DH // kv_local
    rows = q_dev * group
    smem = pl.BlockSpec(memory_space=pltpu.SMEM)
    vmem = pl.BlockSpec(memory_space=pltpu.VMEM)
    work = n * rows * kv_local * slots * TILE
    return pl.pallas_call(
        functools.partial(attention_kernel, members, ctx_count, group, kv_local, slots),
        out_shape=[jax.ShapeDtypeStruct((q_dev, width + LANES), jnp.bfloat16)] * n,
        in_specs=[smem] + [vmem] * (3 + n),
        out_specs=[vmem] * n,
        scratch_shapes=[
            pltpu.VMEM((rows, DH), jnp.float32),
            pltpu.VMEM((kv_local, n, DH, rows), jnp.bfloat16),
            pltpu.VMEM((kv_local, n, DH + ONES, rows), jnp.float32),
            pltpu.VMEM((kv_local, n, 8, rows), jnp.float32),
        ],
        compiler_params=pltpu.CompilerParams(vmem_limit_bytes=VMEM_ATTN),
        cost_estimate=pl.CostEstimate(
            flops=work * DH * 8, bytes_accessed=8 * 2**20, transcendentals=work
        ),
        name="attention",
    )(table, new_rows, keys, values, *blocks)


def merge_kernel(parts, kv_local, *refs):
    in_refs, out_ref = refs[:parts], refs[parts]
    q_dev, width = out_ref.shape
    group = width // DH // kv_local
    lane_parts = q_dev * group // LANES
    per_part = LANES // q_dev
    stats = [ref[:, width:].astype(jnp.float32) for ref in in_refs]
    sublane = lax.broadcasted_iota(jnp.int32, (LANES, LANES), 0)
    for j in range(lane_parts):
        table = jnp.zeros((LANES, LANES), jnp.float32)
        for g in range(kv_local):
            at = [(g * 3 + i) * lane_parts + j for i in range(3)]
            levels = [stat[at[0]] + stat[at[1]] + stat[at[2]] for stat in stats]
            levels = [level.reshape(1, LANES) for level in levels]
            top = functools.reduce(jnp.maximum, levels)
            shares = [jnp.exp2(level - top) for level in levels]
            total = functools.reduce(jnp.add, shares)
            for c, share in enumerate(shares):
                table = jnp.where(sublane == g * parts + c, share / total, table)
        table = table.T
        for g in range(kv_local):
            for i in range(per_part):
                head = g * group + j * per_part + i
                cols = slice(head * DH, (head + 1) * DH)
                share = table[i * q_dev : (i + 1) * q_dev]
                mixed = functools.reduce(
                    jnp.add,
                    [
                        share[:, g * parts + c : g * parts + c + 1]
                        * in_refs[c][:, cols].astype(jnp.float32)
                        for c in range(parts)
                    ],
                )
                out_ref[:, cols] = mixed.astype(jnp.bfloat16)


def merge_call(parts, kv_local):
    q_dev, wide = parts[0].shape
    vmem = pl.BlockSpec(memory_space=pltpu.VMEM)
    return pl.pallas_call(
        functools.partial(merge_kernel, len(parts), kv_local),
        out_shape=jax.ShapeDtypeStruct((q_dev, wide - LANES), jnp.bfloat16),
        in_specs=[vmem] * len(parts),
        out_specs=vmem,
        compiler_params=pltpu.CompilerParams(vmem_limit_bytes=VMEM_MERGE),
        cost_estimate=pl.CostEstimate(
            flops=len(parts) * q_dev * wide * 2,
            bytes_accessed=len(parts) * q_dev * wide * 2,
            transcendentals=0,
        ),
        name="merge",
    )(*parts)


def projection_kernel(members, ctx_count, peers, w_ref, *rest):
    blocks = len(members)
    in_refs, rest = rest[:blocks], rest[blocks:]
    own_ref, send_refs, (rows_ref, sum_ref) = rest[0], rest[1:peers], rest[peers:]
    q_dev = in_refs[0].shape[0]
    me = lax.axis_index("ctx")
    for member, ref in zip(members, in_refs):
        at = flipped(me, ctx_count, *member) * q_dev
        rows_ref[pl.ds(pl.multiple_of(at, q_dev), q_dev), :] = ref[...]
    part = own_ref.shape[0]
    my_tp = lax.axis_index("tp")
    sum_ref[...] = jnp.dot(rows_ref[...], w_ref[...], preferred_element_type=jnp.float32)
    own_ref[...] = sum_ref[pl.ds(pl.multiple_of(my_tp * part, part), part), :]
    for j in range(1, peers):
        at = pl.multiple_of((my_tp ^ j) * part, part)
        send_refs[j - 1][...] = sum_ref[pl.ds(at, part), :].astype(jnp.bfloat16)


def projection_call(members, ctx_count, blocks, weight, peers):
    n = len(blocks)
    q_dev, width = blocks[0].shape
    columns = weight.shape[1]
    part = n * q_dev // peers
    vmem = pl.BlockSpec(memory_space=pltpu.VMEM)
    return pl.pallas_call(
        functools.partial(projection_kernel, members, ctx_count, peers),
        out_shape=[jax.ShapeDtypeStruct((part, columns), jnp.float32)]
        + [jax.ShapeDtypeStruct((part, columns), jnp.bfloat16)] * (peers - 1),
        in_specs=[vmem] * (1 + n),
        out_specs=[vmem] * peers,
        scratch_shapes=[
            pltpu.VMEM((n * q_dev, width), jnp.bfloat16),
            pltpu.VMEM((n * q_dev, columns), jnp.float32),
        ],
        compiler_params=pltpu.CompilerParams(vmem_limit_bytes=VMEM_PROJ),
        cost_estimate=pl.CostEstimate(
            flops=2 * n * q_dev * width * columns,
            bytes_accessed=2 * width * columns,
            transcendentals=0,
        ),
        name="projection",
    )(weight, *blocks)


def body(
    queries,
    new_keys,
    new_values,
    cache_keys,
    cache_values,
    keep_tiles,
    tile_count,
    owner_slot,
    out_weight,
):
    ctx_count = lax.axis_size("ctx")
    peers = lax.axis_size("tp")
    low = LOW_SIZE
    high = ctx_count // low

    def move(x, step, flip):
        pairs = [
            (i, (i // low + step) % high * low + (i % low + flip) % low) for i in range(ctx_count)
        ]
        return lax.ppermute(x, "ctx", pairs)

    steps = sorted(range(1, high), key=lambda k: (min(k, high - k), k))
    order = [(k, 0) for k in (0, *steps)] + [(k, 1) for k in (0, *steps)]

    def gather(x, chained):
        held = {(0, 0): x, (0, 1): move(x, 0, 1)}
        for k in steps:
            held[k, 0] = move(x, -k, 0)
        behind = None
        for k in steps:
            block = held[k, 0]
            if chained and 2 * k == high and behind is not None:
                block, held[behind] = lax.optimization_barrier((block, held[behind]))
            held[k, 1] = move(block, 0, 1)
            behind = (k, 1)
        return held

    held = gather(queries, False)
    near = [m for m in order[1:] if not m[1]]
    far = sorted((m for m in order if m[1]), key=lambda m: -min(m[0], high - m[0]))
    groups = [order[:1]] + [near[i : i + 3] for i in range(0, len(near), 3)]
    groups += [far[i : i + 2] for i in range(0, len(far), 2)]
    kv_local = new_keys.shape[1] // DH
    table = jnp.concatenate([keep_tiles.reshape(-1), tile_count.reshape(-1), owner_slot])
    new_rows = jnp.concatenate([new_keys, new_values], 1)

    def attend(members, blocks):
        return attention_call(
            members,
            ctx_count,
            kv_local,
            keep_tiles.shape[2],
            blocks,
            table,
            new_rows,
            cache_keys,
            cache_values,
        )

    parts, back = {}, {}
    last = None
    for index, members in enumerate(groups):
        blocks = [held[m] for m in members]
        if last is not None:
            blocks, parts[last] = lax.optimization_barrier((blocks, parts[last]))
        if index >= 3:
            returned = {m: back[m] for m in groups[index - 2] if 2 * m[0] != high}
            blocks, returned = lax.optimization_barrier((blocks, returned))
            back.update(returned)
        parts.update(zip(members, attend(members, blocks)))
        last = members[-1]
        for m in members:
            back[m] = parts[m] if m == (0, 0) else move(parts[m], *m)
    attn = merge_call([back[m] for m in order], kv_local)

    held = gather(attn, True)
    own, *sends = projection_call(order, ctx_count, [held[m] for m in order], out_weight, peers)
    for j, piece in enumerate(sends, 1):
        got = lax.ppermute(piece, "tp", [(i, i ^ j) for i in range(peers)])
        own = own + got.astype(jnp.float32)
    return own


def solution(mesh):
    return jax.shard_map(
        body,
        mesh=mesh,
        in_specs=(
            P("ctx", "tp"),
            P("ctx", "tp"),
            P("ctx", "tp"),
            P("ctx", "tp"),
            P("ctx", "tp"),
            P("ctx", "tp", None),
            P("ctx", "tp"),
            P(),
            P("tp", "ctx"),
        ),
        out_specs=P("tp", "ctx"),
        check_vma=False,
    )
```

```python
import functools
import math

import jax
import jax.numpy as jnp
from jax import lax
from jax.experimental import pallas as pl
from jax.experimental.pallas import tpu as pltpu
from jax.sharding import PartitionSpec as P

DH = 128
TILE = 128
LANES = 128
CHUNK = 6
LOW = -1e30
ONES = 16
LOW_SIZE = 2
VMEM_OWN = 59 * 2**20
VMEM_ATTN = 16 * 2**20
VMEM_MERGE = 8 * 2**20
VMEM_PROJ = 16 * 2**20


def flipped(me, count, step, flip):
    high = count // LOW_SIZE
    return lax.rem(me // LOW_SIZE + step, high) * LOW_SIZE + lax.rem(me + flip, LOW_SIZE)


def turned(x):
    return x.astype(jnp.float32).T.astype(jnp.bfloat16)


def fold(scores, values, acc_ref, max_ref, first=False):
    scale = math.log2(math.e) / math.sqrt(DH)
    peak = jnp.max(scores, axis=0, keepdims=True) * scale
    top = peak if first else jnp.maximum(max_ref[:1], peak)
    weights = jnp.exp2(scores * scale - top).astype(jnp.bfloat16)
    mixed = jnp.dot(values, weights, preferred_element_type=jnp.float32)
    if not first:
        mixed += acc_ref[...] * jnp.exp2(max_ref[:1] - top)
    max_ref[...] = jnp.broadcast_to(top, max_ref.shape)
    acc_ref[...] = mixed


def head_columns(g, h, group):
    return pl.ds(pl.multiple_of((g * group + h) * DH, DH), DH)


def begin(g, shifts, q_refs, keys, values, stage_ref, turned_ref, acc_ref, max_ref):
    q_dev = q_refs[0].shape[0]
    rows = stage_ref.shape[0]
    group = rows // q_dev
    place_key = lax.broadcasted_iota(jnp.int32, (TILE, rows), 0)
    place_row = lax.broadcasted_iota(jnp.int32, (TILE, rows), 1) % q_dev
    for b, q in enumerate(q_refs):
        for h in range(group):
            stage_ref[h * q_dev : (h + 1) * q_dev, :] = q[:, head_columns(g, h, group)].astype(
                jnp.float32
            )
        turned_ref[g, b] = stage_ref[...].T.astype(jnp.bfloat16)
        s = jnp.dot(keys, turned_ref[g, b], preferred_element_type=jnp.float32)
        live = (place_key < q_dev) & (place_row - place_key + shifts[b] >= 0)
        fold(jnp.where(live, s, LOW), values, acc_ref.at[g, b], max_ref.at[g, b], first=True)


def finish(g, out_refs, acc_ref, max_ref):
    q_dev = out_refs[0].shape[0]
    rows = acc_ref.shape[3]
    group = rows // q_dev
    heads = acc_ref.shape[0] * group
    parts = rows // LANES
    sublane = lax.broadcasted_iota(jnp.int32, (q_dev, LANES), 0)
    for b, out_ref in enumerate(out_refs):
        total = acc_ref[g, b, DH : DH + 1, :]
        mean = (acc_ref[g, b, :DH, :] / total).T.astype(jnp.bfloat16)
        for h in range(group):
            out_ref[:, head_columns(g, h, group)] = mean[h * q_dev : (h + 1) * q_dev]
        level = max_ref[g, b, :1] + jnp.log2(total)
        high = level.astype(jnp.bfloat16).astype(jnp.float32)
        middle = (level - high).astype(jnp.bfloat16).astype(jnp.float32)
        stats = out_ref[:, heads * DH :].astype(jnp.float32)
        for i, term in enumerate((high, middle, level - high - middle)):
            for j in range(parts):
                at = (g * 3 + i) * parts + j
                stats = jnp.where(sublane == at, term[:, j * LANES : (j + 1) * LANES], stats)
        out_ref[:, heads * DH :] = stats.astype(jnp.bfloat16)


def over_chunks(counts, step):
    ends = [(count + CHUNK - 1) // CHUNK for count in counts]

    def outer(i, carry):
        g, chunk = jnp.int32(0), i
        for end in ends[:-1]:
            past = chunk >= end
            g = jnp.where(past, g + 1, g)
            chunk = jnp.where(past, chunk - end, chunk)
        step(g, chunk)
        return carry

    lax.fori_loop(0, sum(ends), outer, 0)


def own_kernel(
    slot_ref, keep_ref, count_ref, nk_ref, nv_ref, k_hbm, v_hbm, q_ref, out_ref, kept_ref, values_ref,
    v_ref, stage_ref, turned_ref, acc_ref, max_ref, sems
):
    kv_local, slots = keep_ref.shape
    q_dev = q_ref.shape[0]
    counts = [count_ref[g] for g in range(kv_local)]
    ones_tile = jnp.ones((ONES, TILE), jnp.bfloat16)

    def tile_at(slot):
        return pl.ds(pl.multiple_of(slot * TILE, TILE), TILE)

    def copies(g, slot):
        tile = keep_ref[g, jnp.where(slot < count_ref[g], slot, 0)]
        cols = pl.ds(pl.multiple_of(g * DH, DH), DH)
        return [
            pltpu.make_async_copy(
                hbm.at[tile_at(tile), cols], vmem.at[g, tile_at(slot), :], sems.at[which, g, slot]
            )
            for which, (hbm, vmem) in enumerate(((k_hbm, kept_ref), (v_hbm, v_ref)))
        ]

    def start(g, chunk):
        def one(i, carry):
            for copy in copies(g, chunk * CHUNK + i):
                copy.start()
            return carry

        lax.fori_loop(0, CHUNK, one, 0)

    over_chunks(counts, start)

    out_ref[:, out_ref.shape[1] - LANES :] = jnp.zeros((q_dev, LANES), jnp.bfloat16)
    padding = jnp.zeros((TILE - q_dev, DH), jnp.bfloat16)
    last = kept_ref.shape[1] - TILE

    def first(g, carry):
        cols = pl.ds(pl.multiple_of(g * DH, DH), DH)
        keys = jnp.concatenate([nk_ref[:, cols], padding], 0)
        values = jnp.concatenate([nv_ref[:, cols], padding], 0)
        values = jnp.concatenate([turned(values), ones_tile], 0)
        kept_ref[g, last:, :] = keys
        values_ref[g, :, last:] = values
        begin(g, [0], [q_ref], keys, values, stage_ref, turned_ref, acc_ref, max_ref)
        return carry

    lax.fori_loop(0, kv_local, first, 0)

    def step(g, chunk):
        for i in range(CHUNK):
            for copy in copies(g, chunk * CHUNK + i):
                copy.wait()
        for i in range(CHUNK):
            slot = chunk * CHUNK + i
            tail = jnp.concatenate([turned(v_ref[g, tile_at(slot), :]), ones_tile], 0)
            values_ref[g, :, tile_at(slot)] = jnp.where(
                slot < count_ref[g], tail, jnp.zeros_like(tail)
            )
        span = CHUNK * TILE
        at = pl.ds(pl.multiple_of(chunk * span, span), span)
        s = jnp.dot(kept_ref[g, at, :], turned_ref[g, 0], preferred_element_type=jnp.float32)
        fold(s, values_ref[g, :, at], acc_ref.at[g, 0], max_ref.at[g, 0])

    over_chunks(counts, step)

    def end(g, carry):
        finish(g, [out_ref], acc_ref, max_ref)
        return carry

    lax.fori_loop(0, kv_local, end, 0)


def state_shapes(kv_local, n, rows):
    return [
        pltpu.VMEM((rows, DH), jnp.float32),
        pltpu.VMEM((kv_local, n, DH, rows), jnp.bfloat16),
        pltpu.VMEM((kv_local, n, DH + ONES, rows), jnp.float32),
        pltpu.VMEM((kv_local, n, 8, rows), jnp.float32),
    ]


def own_call(queries, slots, keep, count, new_keys, new_values, keys, values):
    q_dev, width = queries.shape
    kv_local = new_keys.shape[1] // DH
    rows = q_dev * (width // DH // kv_local)
    padded = -(-keep.shape[1] // CHUNK) * CHUNK
    smem = pl.BlockSpec(memory_space=pltpu.SMEM)
    vmem = pl.BlockSpec(memory_space=pltpu.VMEM)
    hbm = pl.BlockSpec(memory_space=pltpu.HBM)
    work = rows * kv_local * keep.shape[1] * TILE
    return pl.pallas_call(
        own_kernel,
        out_shape=[
            jax.ShapeDtypeStruct((q_dev, width + LANES), jnp.bfloat16),
            jax.ShapeDtypeStruct((kv_local, (padded + 1) * TILE, DH), jnp.bfloat16),
            jax.ShapeDtypeStruct((kv_local, DH + ONES, (padded + 1) * TILE), jnp.bfloat16),
        ],
        in_specs=[smem] * 3 + [vmem] * 2 + [hbm] * 2 + [vmem],
        out_specs=[vmem] * 3,
        scratch_shapes=[pltpu.VMEM((kv_local, padded * TILE, DH), jnp.bfloat16)]
        + state_shapes(kv_local, 1, rows)
        + [pltpu.SemaphoreType.DMA((2, kv_local, padded))],
        compiler_params=pltpu.CompilerParams(vmem_limit_bytes=VMEM_OWN),
        cost_estimate=pl.CostEstimate(
            flops=work * DH * 8, bytes_accessed=8 * 2**20, transcendentals=work
        ),
        name="own_attention",
    )(slots, keep, count, new_keys, new_values, keys, values, queries)


def attention_kernel(members, ctx_count, table_ref, kept_ref, values_ref, *rest):
    blocks = len(members)
    q_refs, rest = rest[:blocks], rest[blocks:]
    out_refs, rest = rest[:blocks], rest[blocks:]
    stage_ref, turned_ref, acc_ref, max_ref = rest
    kv_local = kept_ref.shape[0]
    q_dev = q_refs[0].shape[0]
    last = kept_ref.shape[1] - TILE
    me = lax.axis_index("ctx")

    def slot_of(ctx):
        return table_ref[kv_local + ctx]

    shifts = [(slot_of(flipped(me, ctx_count, *m)) - slot_of(me)) * q_dev for m in members]
    for out_ref in out_refs:
        out_ref[:, out_ref.shape[1] - LANES :] = jnp.zeros((q_dev, LANES), jnp.bfloat16)

    def first(g, carry):
        keys, values = kept_ref[g, last:, :], values_ref[g, :, last:]
        begin(g, shifts, q_refs, keys, values, stage_ref, turned_ref, acc_ref, max_ref)
        return carry

    lax.fori_loop(0, kv_local, first, 0)

    def step(g, chunk):
        span = CHUNK * TILE
        at = pl.ds(pl.multiple_of(chunk * span, span), span)
        keys, values = kept_ref[g, at, :], values_ref[g, :, at]

        def score(b):
            return jnp.dot(keys, turned_ref[g, b], preferred_element_type=jnp.float32)

        ahead = score(0)
        for b in range(blocks):
            s = ahead
            if b + 1 < blocks:
                ahead = score(b + 1)
            fold(s, values, acc_ref.at[g, b], max_ref.at[g, b])

    over_chunks([table_ref[g] for g in range(kv_local)], step)

    def end(g, carry):
        finish(g, out_refs, acc_ref, max_ref)
        return carry

    lax.fori_loop(0, kv_local, end, 0)


def attention_call(members, ctx_count, blocks, table, kept, values):
    n = len(blocks)
    q_dev, width = blocks[0].shape
    kv_local = kept.shape[0]
    rows = q_dev * (width // DH // kv_local)
    smem = pl.BlockSpec(memory_space=pltpu.SMEM)
    vmem = pl.BlockSpec(memory_space=pltpu.VMEM)
    work = n * rows * kv_local * kept.shape[1]
    return pl.pallas_call(
        functools.partial(attention_kernel, members, ctx_count),
        out_shape=[jax.ShapeDtypeStruct((q_dev, width + LANES), jnp.bfloat16)] * n,
        in_specs=[smem] + [vmem] * (2 + n),
        out_specs=[vmem] * n,
        scratch_shapes=state_shapes(kv_local, n, rows),
        compiler_params=pltpu.CompilerParams(vmem_limit_bytes=VMEM_ATTN),
        cost_estimate=pl.CostEstimate(
            flops=work * DH * 8, bytes_accessed=8 * 2**20, transcendentals=work
        ),
        name="attention",
    )(table, kept, values, *blocks)


def merge_kernel(parts, kv_local, *refs):
    in_refs, out_ref = refs[:parts], refs[parts]
    q_dev, width = out_ref.shape
    group = width // DH // kv_local
    lane_parts = q_dev * group // LANES
    per_part = LANES // q_dev
    stats = [ref[:, width:].astype(jnp.float32) for ref in in_refs]
    sublane = lax.broadcasted_iota(jnp.int32, (LANES, LANES), 0)
    for j in range(lane_parts):
        table = jnp.zeros((LANES, LANES), jnp.float32)
        for g in range(kv_local):
            at = [(g * 3 + i) * lane_parts + j for i in range(3)]
            levels = [stat[at[0]] + stat[at[1]] + stat[at[2]] for stat in stats]
            levels = [level.reshape(1, LANES) for level in levels]
            top = functools.reduce(jnp.maximum, levels)
            shares = [jnp.exp2(level - top) for level in levels]
            total = functools.reduce(jnp.add, shares)
            for c, share in enumerate(shares):
                table = jnp.where(sublane == g * parts + c, share / total, table)
        table = table.T
        for g in range(kv_local):
            for i in range(per_part):
                head = g * group + j * per_part + i
                cols = slice(head * DH, (head + 1) * DH)
                share = table[i * q_dev : (i + 1) * q_dev]
                mixed = functools.reduce(
                    jnp.add,
                    [
                        share[:, g * parts + c : g * parts + c + 1]
                        * in_refs[c][:, cols].astype(jnp.float32)
                        for c in range(parts)
                    ],
                )
                out_ref[:, cols] = mixed.astype(jnp.bfloat16)


def merge_call(parts, kv_local):
    q_dev, wide = parts[0].shape
    vmem = pl.BlockSpec(memory_space=pltpu.VMEM)
    return pl.pallas_call(
        functools.partial(merge_kernel, len(parts), kv_local),
        out_shape=jax.ShapeDtypeStruct((q_dev, wide - LANES), jnp.bfloat16),
        in_specs=[vmem] * len(parts),
        out_specs=vmem,
        compiler_params=pltpu.CompilerParams(vmem_limit_bytes=VMEM_MERGE),
        cost_estimate=pl.CostEstimate(
            flops=len(parts) * q_dev * wide * 2,
            bytes_accessed=len(parts) * q_dev * wide * 2,
            transcendentals=0,
        ),
        name="merge",
    )(*parts)


def projection_kernel(members, ctx_count, peers, w_ref, *rest):
    blocks = len(members)
    in_refs, rest = rest[:blocks], rest[blocks:]
    own_ref, send_refs, (rows_ref, sum_ref) = rest[0], rest[1:peers], rest[peers:]
    q_dev = in_refs[0].shape[0]
    me = lax.axis_index("ctx")
    for member, ref in zip(members, in_refs):
        at = flipped(me, ctx_count, *member) * q_dev
        rows_ref[pl.ds(pl.multiple_of(at, q_dev), q_dev), :] = ref[...]
    part = own_ref.shape[0]
    my_tp = lax.axis_index("tp")
    sum_ref[...] = jnp.dot(rows_ref[...], w_ref[...], preferred_element_type=jnp.float32)
    own_ref[...] = sum_ref[pl.ds(pl.multiple_of(my_tp * part, part), part), :]
    for j in range(1, peers):
        at = pl.multiple_of((my_tp ^ j) * part, part)
        send_refs[j - 1][...] = sum_ref[pl.ds(at, part), :].astype(jnp.bfloat16)


def projection_call(members, ctx_count, blocks, weight, peers):
    n = len(blocks)
    q_dev, width = blocks[0].shape
    columns = weight.shape[1]
    part = n * q_dev // peers
    vmem = pl.BlockSpec(memory_space=pltpu.VMEM)
    return pl.pallas_call(
        functools.partial(projection_kernel, members, ctx_count, peers),
        out_shape=[jax.ShapeDtypeStruct((part, columns), jnp.float32)]
        + [jax.ShapeDtypeStruct((part, columns), jnp.bfloat16)] * (peers - 1),
        in_specs=[vmem] * (1 + n),
        out_specs=[vmem] * peers,
        scratch_shapes=[
            pltpu.VMEM((n * q_dev, width), jnp.bfloat16),
            pltpu.VMEM((n * q_dev, columns), jnp.float32),
        ],
        compiler_params=pltpu.CompilerParams(vmem_limit_bytes=VMEM_PROJ),
        cost_estimate=pl.CostEstimate(
            flops=2 * n * q_dev * width * columns,
            bytes_accessed=2 * width * columns,
            transcendentals=0,
        ),
        name="projection",
    )(weight, *blocks)


def body(
    queries,
    new_keys,
    new_values,
    cache_keys,
    cache_values,
    keep_tiles,
    tile_count,
    owner_slot,
    out_weight,
):
    ctx_count = lax.axis_size("ctx")
    peers = lax.axis_size("tp")
    low = LOW_SIZE
    high = ctx_count // low

    def move(x, step, flip):
        pairs = [
            (i, (i // low + step) % high * low + (i % low + flip) % low) for i in range(ctx_count)
        ]
        return lax.ppermute(x, "ctx", pairs)

    steps = sorted(range(1, high), key=lambda k: (min(k, high - k), k))
    order = [(k, 0) for k in (0, *steps)] + [(k, 1) for k in (0, *steps)]

    def gather(x, chained):
        held = {(0, 0): x, (0, 1): move(x, 0, 1)}
        for k in steps:
            held[k, 0] = move(x, -k, 0)
        behind = None
        for k in steps:
            block = held[k, 0]
            if chained and 2 * k == high and behind is not None:
                block, held[behind] = lax.optimization_barrier((block, held[behind]))
            held[k, 1] = move(block, 0, 1)
            behind = (k, 1)
        return held

    held = gather(queries, False)
    kv_local = new_keys.shape[1] // DH
    near = [m for m in order[1:] if not m[1] and 2 * m[0] != high]
    middle = [m for m in order[1:] if not m[1] and 2 * m[0] == high]
    flip = [m for m in order if m[1] and m[0] and 2 * m[0] != high]
    late = [m for m in order if m[1] and 2 * m[0] == high] + [(0, 1)]
    groups = [near[i : i + 2] for i in range(0, len(near), 2)]
    groups += [middle + flip[:2]] + [flip[i : i + 2] for i in range(2, len(flip), 2)] + [late]

    table = jnp.concatenate([tile_count.reshape(-1), owner_slot])
    own, kept, values = own_call(
        queries,
        owner_slot,
        keep_tiles[0],
        tile_count[0],
        new_keys,
        new_values,
        cache_keys,
        cache_values,
    )
    parts, back = {}, {(0, 0): own}
    for index, members in enumerate(groups):
        blocks = [held[m] for m in members]
        if index:
            previous = groups[index - 1][-1]
            blocks, parts[previous] = lax.optimization_barrier((blocks, parts[previous]))
        if index >= 2:
            returned = {m: back[m] for m in groups[index - 2]}
            blocks, returned = lax.optimization_barrier((blocks, returned))
            back.update(returned)
        parts.update(
            zip(members, attention_call(members, ctx_count, blocks, table, kept, values))
        )
        for m in members:
            back[m] = move(parts[m], *m)
    attn = merge_call([back[m] for m in order], kv_local)

    held = gather(attn, True)
    own, *sends = projection_call(order, ctx_count, [held[m] for m in order], out_weight, peers)
    for j, piece in enumerate(sends, 1):
        got = lax.ppermute(piece, "tp", [(i, i ^ j) for i in range(peers)])
        own = own + got.astype(jnp.float32)
    return own


def solution(mesh):
    return jax.shard_map(
        body,
        mesh=mesh,
        in_specs=(
            P("ctx", "tp"),
            P("ctx", "tp"),
            P("ctx", "tp"),
            P("ctx", "tp"),
            P("ctx", "tp"),
            P("ctx", "tp", None),
            P("ctx", "tp"),
            P(),
            P("tp", "ctx"),
        ),
        out_specs=P("tp", "ctx"),
        check_vma=False,
    )
```

```python
import functools
import math

import jax
import jax.numpy as jnp
from jax import lax
from jax.experimental import pallas as pl
from jax.experimental.pallas import tpu as pltpu
from jax.sharding import PartitionSpec as P

DH = 128
TILE = 128
LANES = 128
CHUNK = 4
LOW = -1e30
ONES = 16
LOW_SIZE = 2
VMEM_ATTN = 24 * 2**20
VMEM_MERGE = 8 * 2**20
VMEM_PROJ = 16 * 2**20


def flipped(me, count, step, flip):
    high = count // LOW_SIZE
    return lax.rem(me // LOW_SIZE + step, high) * LOW_SIZE + lax.rem(me + flip, LOW_SIZE)


def attention_kernel(
    members, ctx_count, group, kv_local, slots, table_ref, new_ref, k_ref, v_ref, *rest
):
    blocks = len(members)
    q_refs, rest = rest[:blocks], rest[blocks:]
    out_refs, rest = rest[:blocks], rest[blocks:]
    q_ref, turned_ref, acc_ref, max_ref = rest
    q_dev = q_refs[0].shape[0]
    heads = kv_local * group
    rows = q_dev * group
    span = CHUNK * TILE
    scale = math.log2(math.e) / math.sqrt(DH)
    me = lax.axis_index("ctx")

    def count_of(g):
        return table_ref[kv_local * slots + g]

    def slot_of(ctx):
        return table_ref[kv_local * (slots + 1) + ctx]

    def turned(x):
        return x.astype(jnp.float32).T.astype(jnp.bfloat16)

    def fold(g, b, s, values, first=False):
        peak = jnp.max(s, axis=0, keepdims=True) * scale
        top = peak if first else jnp.maximum(max_ref[g, b, :1], peak)
        p = jnp.exp2(s * scale - top).astype(jnp.bfloat16)
        mixed = jnp.dot(values, p, preferred_element_type=jnp.float32)
        if not first:
            mixed += acc_ref[g, b] * jnp.exp2(max_ref[g, b, :1] - top)
        max_ref[g, b] = jnp.broadcast_to(top, max_ref.shape[2:])
        acc_ref[g, b] = mixed

    ones_tile = jnp.ones((ONES, TILE), jnp.bfloat16)
    place_key = lax.broadcasted_iota(jnp.int32, (TILE, rows), 0)
    place_row = lax.broadcasted_iota(jnp.int32, (TILE, rows), 1) % q_dev
    padding = jnp.zeros((TILE - q_dev, DH), jnp.bfloat16)

    for g in range(kv_local):
        fresh_keys = jnp.concatenate([new_ref[:, g * DH : (g + 1) * DH], padding], 0)
        fresh_values = new_ref[:, (kv_local + g) * DH : (kv_local + g + 1) * DH]
        fresh_values = jnp.concatenate(
            [turned(jnp.concatenate([fresh_values, padding], 0)), ones_tile], 0
        )
        for b in range(blocks):
            for h in range(group):
                head = g * group + h
                q_ref[h * q_dev : (h + 1) * q_dev, :] = q_refs[b][
                    :, head * DH : (head + 1) * DH
                ].astype(jnp.float32)
            turned_ref[g, b] = q_ref[...].T.astype(jnp.bfloat16)
            s = jnp.dot(fresh_keys, turned_ref[g, b], preferred_element_type=jnp.float32)
            shift = (slot_of(flipped(me, ctx_count, *members[b])) - slot_of(me)) * q_dev
            live = (place_key < q_dev) & (place_row - place_key + shift >= 0)
            fold(g, b, jnp.where(live, s, LOW), fresh_values, first=True)

    def load_chunk(g, chunk):
        cols = slice(g * DH, (g + 1) * DH)
        key_parts, value_parts = [], []
        for i in range(CHUNK):
            slot = chunk * CHUNK + i
            live = slot < count_of(g)
            tile = table_ref[g * slots + jnp.where(live, slot, 0)]
            at = pl.ds(pl.multiple_of(tile * TILE, TILE), TILE)
            key_parts.append(k_ref[at, cols])
            tail = jnp.concatenate([turned(v_ref[at, cols]), ones_tile], 0)
            value_parts.append(jnp.where(live, tail, jnp.zeros_like(tail)))
        return jnp.concatenate(key_parts, 0), jnp.concatenate(value_parts, 1)

    def run(kv_heads, chunk):
        loaded = {g: load_chunk(g, chunk) for g in kv_heads}
        chains = [(g, b) for b in range(blocks) for g in kv_heads]

        def score(g, b):
            return jnp.dot(loaded[g][0], turned_ref[g, b], preferred_element_type=jnp.float32)

        ahead = score(*chains[0])
        for at, (g, b) in enumerate(chains):
            s = ahead
            if at + 1 < len(chains):
                ahead = score(*chains[at + 1])
            fold(g, b, s, loaded[g][1])

    ends = [(count_of(g) + CHUNK - 1) // CHUNK for g in range(kv_local)]
    shared = functools.reduce(jnp.minimum, ends)

    def step_all(chunk, carry):
        run(range(kv_local), chunk)
        return carry

    lax.fori_loop(0, shared, step_all, 0)
    for g in range(kv_local):

        def step_one(chunk, carry, g=g):
            run([g], chunk)
            return carry

        lax.fori_loop(shared, ends[g], step_one, 0)

    sublane = lax.broadcasted_iota(jnp.int32, (q_dev, LANES), 0)
    parts = rows // LANES
    for b in range(blocks):
        stats = jnp.zeros((q_dev, LANES), jnp.float32)
        for g in range(kv_local):
            total = acc_ref[g, b, DH : DH + 1, :]
            mean = (acc_ref[g, b, :DH, :] / total).T.astype(jnp.bfloat16)
            for h in range(group):
                head = g * group + h
                out_refs[b][:, head * DH : (head + 1) * DH] = mean[h * q_dev : (h + 1) * q_dev]
            level = max_ref[g, b, :1] + jnp.log2(total)
            high = level.astype(jnp.bfloat16).astype(jnp.float32)
            middle = (level - high).astype(jnp.bfloat16).astype(jnp.float32)
            for i, term in enumerate((high, middle, level - high - middle)):
                for j in range(parts):
                    at = (g * 3 + i) * parts + j
                    stats = jnp.where(sublane == at, term[:, j * LANES : (j + 1) * LANES], stats)
        out_refs[b][:, heads * DH :] = stats.astype(jnp.bfloat16)


def attention_call(members, ctx_count, kv_local, slots, blocks, table, new_rows, keys, values):
    n = len(blocks)
    q_dev, width = blocks[0].shape
    group = width // DH // kv_local
    rows = q_dev * group
    smem = pl.BlockSpec(memory_space=pltpu.SMEM)
    vmem = pl.BlockSpec(memory_space=pltpu.VMEM)
    work = n * rows * kv_local * slots * TILE
    return pl.pallas_call(
        functools.partial(attention_kernel, members, ctx_count, group, kv_local, slots),
        out_shape=[jax.ShapeDtypeStruct((q_dev, width + LANES), jnp.bfloat16)] * n,
        in_specs=[smem] + [vmem] * (3 + n),
        out_specs=[vmem] * n,
        scratch_shapes=[
            pltpu.VMEM((rows, DH), jnp.float32),
            pltpu.VMEM((kv_local, n, DH, rows), jnp.bfloat16),
            pltpu.VMEM((kv_local, n, DH + ONES, rows), jnp.float32),
            pltpu.VMEM((kv_local, n, 8, rows), jnp.float32),
        ],
        compiler_params=pltpu.CompilerParams(vmem_limit_bytes=VMEM_ATTN),
        cost_estimate=pl.CostEstimate(
            flops=work * DH * 8, bytes_accessed=8 * 2**20, transcendentals=work
        ),
        name="attention",
    )(table, new_rows, keys, values, *blocks)


def merge_kernel(parts, kv_local, *refs):
    in_refs, out_ref = refs[:parts], refs[parts]
    q_dev, width = out_ref.shape
    group = width // DH // kv_local
    lane_parts = q_dev * group // LANES
    per_part = LANES // q_dev
    stats = [ref[:, width:].astype(jnp.float32) for ref in in_refs]
    sublane = lax.broadcasted_iota(jnp.int32, (LANES, LANES), 0)
    for j in range(lane_parts):
        table = jnp.zeros((LANES, LANES), jnp.float32)
        for g in range(kv_local):
            at = [(g * 3 + i) * lane_parts + j for i in range(3)]
            levels = [stat[at[0]] + stat[at[1]] + stat[at[2]] for stat in stats]
            levels = [level.reshape(1, LANES) for level in levels]
            top = functools.reduce(jnp.maximum, levels)
            shares = [jnp.exp2(level - top) for level in levels]
            total = functools.reduce(jnp.add, shares)
            for c, share in enumerate(shares):
                table = jnp.where(sublane == g * parts + c, share / total, table)
        table = table.T
        for g in range(kv_local):
            for i in range(per_part):
                head = g * group + j * per_part + i
                cols = slice(head * DH, (head + 1) * DH)
                share = table[i * q_dev : (i + 1) * q_dev]
                mixed = functools.reduce(
                    jnp.add,
                    [
                        share[:, g * parts + c : g * parts + c + 1]
                        * in_refs[c][:, cols].astype(jnp.float32)
                        for c in range(parts)
                    ],
                )
                out_ref[:, cols] = mixed.astype(jnp.bfloat16)


def merge_call(parts, kv_local):
    q_dev, wide = parts[0].shape
    vmem = pl.BlockSpec(memory_space=pltpu.VMEM)
    return pl.pallas_call(
        functools.partial(merge_kernel, len(parts), kv_local),
        out_shape=jax.ShapeDtypeStruct((q_dev, wide - LANES), jnp.bfloat16),
        in_specs=[vmem] * len(parts),
        out_specs=vmem,
        compiler_params=pltpu.CompilerParams(vmem_limit_bytes=VMEM_MERGE),
        cost_estimate=pl.CostEstimate(
            flops=len(parts) * q_dev * wide * 2,
            bytes_accessed=len(parts) * q_dev * wide * 2,
            transcendentals=0,
        ),
        name="merge",
    )(*parts)


def projection_kernel(members, ctx_count, peers, w_ref, *rest):
    blocks = len(members)
    in_refs, rest = rest[:blocks], rest[blocks:]
    own_ref, send_refs, (rows_ref, sum_ref) = rest[0], rest[1:peers], rest[peers:]
    q_dev = in_refs[0].shape[0]
    me = lax.axis_index("ctx")
    for member, ref in zip(members, in_refs):
        at = flipped(me, ctx_count, *member) * q_dev
        rows_ref[pl.ds(pl.multiple_of(at, q_dev), q_dev), :] = ref[...]
    part = own_ref.shape[0]
    my_tp = lax.axis_index("tp")
    sum_ref[...] = jnp.dot(rows_ref[...], w_ref[...], preferred_element_type=jnp.float32)
    own_ref[...] = sum_ref[pl.ds(pl.multiple_of(my_tp * part, part), part), :]
    for j in range(1, peers):
        at = pl.multiple_of((my_tp ^ j) * part, part)
        send_refs[j - 1][...] = sum_ref[pl.ds(at, part), :].astype(jnp.bfloat16)


def projection_call(members, ctx_count, blocks, weight, peers):
    n = len(blocks)
    q_dev, width = blocks[0].shape
    columns = weight.shape[1]
    part = n * q_dev // peers
    vmem = pl.BlockSpec(memory_space=pltpu.VMEM)
    return pl.pallas_call(
        functools.partial(projection_kernel, members, ctx_count, peers),
        out_shape=[jax.ShapeDtypeStruct((part, columns), jnp.float32)]
        + [jax.ShapeDtypeStruct((part, columns), jnp.bfloat16)] * (peers - 1),
        in_specs=[vmem] * (1 + n),
        out_specs=[vmem] * peers,
        scratch_shapes=[
            pltpu.VMEM((n * q_dev, width), jnp.bfloat16),
            pltpu.VMEM((n * q_dev, columns), jnp.float32),
        ],
        compiler_params=pltpu.CompilerParams(vmem_limit_bytes=VMEM_PROJ),
        cost_estimate=pl.CostEstimate(
            flops=2 * n * q_dev * width * columns,
            bytes_accessed=2 * width * columns,
            transcendentals=0,
        ),
        name="projection",
    )(weight, *blocks)


def body(
    queries,
    new_keys,
    new_values,
    cache_keys,
    cache_values,
    keep_tiles,
    tile_count,
    owner_slot,
    out_weight,
):
    ctx_count = lax.axis_size("ctx")
    peers = lax.axis_size("tp")
    low = LOW_SIZE
    high = ctx_count // low

    def move(x, step, flip):
        pairs = [
            (i, (i // low + step) % high * low + (i % low + flip) % low) for i in range(ctx_count)
        ]
        return lax.ppermute(x, "ctx", pairs)

    steps = sorted(range(1, high), key=lambda k: (min(k, high - k), k))
    order = [(k, 0) for k in (0, *steps)] + [(k, 1) for k in (0, *steps)]

    def gather(x, chained):
        held = {(0, 0): x, (0, 1): move(x, 0, 1)}
        for k in steps:
            held[k, 0] = move(x, -k, 0)
        behind = None
        for k in steps:
            block = held[k, 0]
            if chained and 2 * k == high and behind is not None:
                block, held[behind] = lax.optimization_barrier((block, held[behind]))
            held[k, 1] = move(block, 0, 1)
            behind = (k, 1)
        return held

    held = gather(queries, False)
    near = [m for m in order[1:] if not m[1] and 2 * m[0] != high]
    middle = [m for m in order[1:] if not m[1] and 2 * m[0] == high]
    flip = [m for m in order if m[1] and m[0] and 2 * m[0] != high]
    late = [m for m in order if m[1] and 2 * m[0] == high] + [(0, 1)]
    groups = [near[i : i + 2] for i in range(0, len(near), 2)]
    groups += [middle + flip[:2]] + [flip[i : i + 2] for i in range(2, len(flip), 2)]
    groups += [late, order[:1]]
    kv_local = new_keys.shape[1] // DH
    table = jnp.concatenate([keep_tiles.reshape(-1), tile_count.reshape(-1), owner_slot])
    new_rows = jnp.concatenate([new_keys, new_values], 1)

    def attend(members, blocks):
        return attention_call(
            members,
            ctx_count,
            kv_local,
            keep_tiles.shape[2],
            blocks,
            table,
            new_rows,
            cache_keys,
            cache_values,
        )

    parts, back = {}, {}
    last = None
    for index, members in enumerate(groups):
        blocks = [held[m] for m in members]
        if last is not None:
            blocks, parts[last] = lax.optimization_barrier((blocks, parts[last]))
        if 2 <= index < len(groups) - 1:
            returned = {m: back[m] for m in groups[index - 2] if 2 * m[0] != high}
            blocks, returned = lax.optimization_barrier((blocks, returned))
            back.update(returned)
        parts.update(zip(members, attend(members, blocks)))
        last = members[-1]
        for m in members:
            back[m] = parts[m] if m == (0, 0) else move(parts[m], *m)
    attn = merge_call([back[m] for m in order], kv_local)

    held = gather(attn, True)
    own, *sends = projection_call(order, ctx_count, [held[m] for m in order], out_weight, peers)
    for j, piece in enumerate(sends, 1):
        got = lax.ppermute(piece, "tp", [(i, i ^ j) for i in range(peers)])
        own = own + got.astype(jnp.float32)
    return own


def solution(mesh):
    return jax.shard_map(
        body,
        mesh=mesh,
        in_specs=(
            P("ctx", "tp"),
            P("ctx", "tp"),
            P("ctx", "tp"),
            P("ctx", "tp"),
            P("ctx", "tp"),
            P("ctx", "tp", None),
            P("ctx", "tp"),
            P(),
            P("tp", "ctx"),
        ),
        out_specs=P("tp", "ctx"),
        check_vma=False,
    )
```

```python
import functools
import math

import jax
import jax.numpy as jnp
from jax import lax
from jax.experimental import pallas as pl
from jax.experimental.pallas import tpu as pltpu
from jax.sharding import PartitionSpec as P

DH = 128
TILE = 128
LANES = 128
CHUNK = 4
LOW = -1e30
ONES = 16
LOW_SIZE = 2
VMEM_ATTN = 24 * 2**20
VMEM_MERGE = 8 * 2**20
VMEM_PROJ = 16 * 2**20


def flipped(me, count, step, flip):
    high = count // LOW_SIZE
    return lax.rem(me // LOW_SIZE + step, high) * LOW_SIZE + lax.rem(me + flip, LOW_SIZE)


def attention_kernel(
    members, ctx_count, group, kv_local, slots, table_ref, new_ref, k_ref, v_ref, *rest
):
    blocks = len(members)
    q_refs, rest = rest[:blocks], rest[blocks:]
    out_refs, rest = rest[:blocks], rest[blocks:]
    q_ref, turned_ref, acc_ref, max_ref = rest
    q_dev = q_refs[0].shape[0]
    heads = kv_local * group
    rows = q_dev * group
    span = CHUNK * TILE
    scale = math.log2(math.e) / math.sqrt(DH)
    me = lax.axis_index("ctx")

    def count_of(g):
        return table_ref[kv_local * slots + g]

    def slot_of(ctx):
        return table_ref[kv_local * (slots + 1) + ctx]

    def turned(x):
        return x.astype(jnp.float32).T.astype(jnp.bfloat16)

    def fold(g, b, s, values, first=False):
        peak = jnp.max(s, axis=0, keepdims=True) * scale
        top = peak if first else jnp.maximum(max_ref[g, b, :1], peak)
        p = jnp.exp2(s * scale - top).astype(jnp.bfloat16)
        mixed = jnp.dot(values, p, preferred_element_type=jnp.float32)
        if not first:
            mixed += acc_ref[g, b] * jnp.exp2(max_ref[g, b, :1] - top)
        max_ref[g, b] = jnp.broadcast_to(top, max_ref.shape[2:])
        acc_ref[g, b] = mixed

    ones_tile = jnp.ones((ONES, TILE), jnp.bfloat16)
    place_key = lax.broadcasted_iota(jnp.int32, (TILE, rows), 0)
    place_row = lax.broadcasted_iota(jnp.int32, (TILE, rows), 1) % q_dev
    padding = jnp.zeros((TILE - q_dev, DH), jnp.bfloat16)

    for g in range(kv_local):
        fresh_keys = jnp.concatenate([new_ref[:, g * DH : (g + 1) * DH], padding], 0)
        fresh_values = new_ref[:, (kv_local + g) * DH : (kv_local + g + 1) * DH]
        fresh_values = jnp.concatenate(
            [turned(jnp.concatenate([fresh_values, padding], 0)), ones_tile], 0
        )
        for b in range(blocks):
            for h in range(group):
                head = g * group + h
                q_ref[h * q_dev : (h + 1) * q_dev, :] = q_refs[b][
                    :, head * DH : (head + 1) * DH
                ].astype(jnp.float32)
            turned_ref[g, b] = q_ref[...].T.astype(jnp.bfloat16)
            s = jnp.dot(fresh_keys, turned_ref[g, b], preferred_element_type=jnp.float32)
            shift = (slot_of(flipped(me, ctx_count, *members[b])) - slot_of(me)) * q_dev
            live = (place_key < q_dev) & (place_row - place_key + shift >= 0)
            fold(g, b, jnp.where(live, s, LOW), fresh_values, first=True)

    def load_chunk(g, chunk):
        cols = slice(g * DH, (g + 1) * DH)
        key_parts, value_parts = [], []
        for i in range(CHUNK):
            slot = chunk * CHUNK + i
            live = slot < count_of(g)
            tile = table_ref[g * slots + jnp.where(live, slot, 0)]
            at = pl.ds(pl.multiple_of(tile * TILE, TILE), TILE)
            key_parts.append(k_ref[at, cols])
            tail = jnp.concatenate([turned(v_ref[at, cols]), ones_tile], 0)
            value_parts.append(jnp.where(live, tail, jnp.zeros_like(tail)))
        return jnp.concatenate(key_parts, 0), jnp.concatenate(value_parts, 1)

    def run(kv_heads, chunk):
        loaded = {g: load_chunk(g, chunk) for g in kv_heads}
        chains = [(g, b) for b in range(blocks) for g in kv_heads]

        def score(g, b):
            return jnp.dot(loaded[g][0], turned_ref[g, b], preferred_element_type=jnp.float32)

        ahead = score(*chains[0])
        for at, (g, b) in enumerate(chains):
            s = ahead
            if at + 1 < len(chains):
                ahead = score(*chains[at + 1])
            fold(g, b, s, loaded[g][1])

    ends = [(count_of(g) + CHUNK - 1) // CHUNK for g in range(kv_local)]
    shared = functools.reduce(jnp.minimum, ends)

    def step_all(chunk, carry):
        run(range(kv_local), chunk)
        return carry

    lax.fori_loop(0, shared, step_all, 0)
    for g in range(kv_local):

        def step_one(chunk, carry, g=g):
            run([g], chunk)
            return carry

        lax.fori_loop(shared, ends[g], step_one, 0)

    sublane = lax.broadcasted_iota(jnp.int32, (q_dev, LANES), 0)
    parts = rows // LANES
    for b in range(blocks):
        stats = jnp.zeros((q_dev, LANES), jnp.float32)
        for g in range(kv_local):
            total = acc_ref[g, b, DH : DH + 1, :]
            mean = (acc_ref[g, b, :DH, :] / total).T.astype(jnp.bfloat16)
            for h in range(group):
                head = g * group + h
                out_refs[b][:, head * DH : (head + 1) * DH] = mean[h * q_dev : (h + 1) * q_dev]
            level = max_ref[g, b, :1] + jnp.log2(total)
            high = level.astype(jnp.bfloat16).astype(jnp.float32)
            middle = (level - high).astype(jnp.bfloat16).astype(jnp.float32)
            for i, term in enumerate((high, middle, level - high - middle)):
                for j in range(parts):
                    at = (g * 3 + i) * parts + j
                    stats = jnp.where(sublane == at, term[:, j * LANES : (j + 1) * LANES], stats)
        out_refs[b][:, heads * DH :] = stats.astype(jnp.bfloat16)


def hand_on_kernel(in_ref, k_ref, v_ref, out_ref):
    out_ref[...] = in_ref[...]


def hand_on_call(new_rows, keys, values):
    vmem = pl.BlockSpec(memory_space=pltpu.VMEM)
    return pl.pallas_call(
        hand_on_kernel,
        out_shape=jax.ShapeDtypeStruct(new_rows.shape, new_rows.dtype),
        in_specs=[vmem] * 3,
        out_specs=vmem,
        compiler_params=pltpu.CompilerParams(vmem_limit_bytes=VMEM_ATTN),
        name="hand_on",
    )(new_rows, keys, values)


def attention_call(members, ctx_count, kv_local, slots, blocks, table, new_rows, keys, values):
    n = len(blocks)
    q_dev, width = blocks[0].shape
    group = width // DH // kv_local
    rows = q_dev * group
    smem = pl.BlockSpec(memory_space=pltpu.SMEM)
    vmem = pl.BlockSpec(memory_space=pltpu.VMEM)
    work = n * rows * kv_local * slots * TILE
    return pl.pallas_call(
        functools.partial(attention_kernel, members, ctx_count, group, kv_local, slots),
        out_shape=[jax.ShapeDtypeStruct((q_dev, width + LANES), jnp.bfloat16)] * n,
        in_specs=[smem] + [vmem] * (3 + n),
        out_specs=[vmem] * n,
        scratch_shapes=[
            pltpu.VMEM((rows, DH), jnp.float32),
            pltpu.VMEM((kv_local, n, DH, rows), jnp.bfloat16),
            pltpu.VMEM((kv_local, n, DH + ONES, rows), jnp.float32),
            pltpu.VMEM((kv_local, n, 8, rows), jnp.float32),
        ],
        compiler_params=pltpu.CompilerParams(vmem_limit_bytes=VMEM_ATTN),
        cost_estimate=pl.CostEstimate(
            flops=work * DH * 8, bytes_accessed=8 * 2**20, transcendentals=work
        ),
        name="attention",
    )(table, new_rows, keys, values, *blocks)


def merge_kernel(parts, kv_local, *refs):
    in_refs, out_ref = refs[:parts], refs[parts]
    q_dev, width = out_ref.shape
    group = width // DH // kv_local
    lane_parts = q_dev * group // LANES
    per_part = LANES // q_dev
    stats = [ref[:, width:].astype(jnp.float32) for ref in in_refs]
    sublane = lax.broadcasted_iota(jnp.int32, (LANES, LANES), 0)
    for j in range(lane_parts):
        table = jnp.zeros((LANES, LANES), jnp.float32)
        for g in range(kv_local):
            at = [(g * 3 + i) * lane_parts + j for i in range(3)]
            levels = [stat[at[0]] + stat[at[1]] + stat[at[2]] for stat in stats]
            levels = [level.reshape(1, LANES) for level in levels]
            top = functools.reduce(jnp.maximum, levels)
            shares = [jnp.exp2(level - top) for level in levels]
            total = functools.reduce(jnp.add, shares)
            for c, share in enumerate(shares):
                table = jnp.where(sublane == g * parts + c, share / total, table)
        table = table.T
        for g in range(kv_local):
            for i in range(per_part):
                head = g * group + j * per_part + i
                cols = slice(head * DH, (head + 1) * DH)
                share = table[i * q_dev : (i + 1) * q_dev]
                mixed = functools.reduce(
                    jnp.add,
                    [
                        share[:, g * parts + c : g * parts + c + 1]
                        * in_refs[c][:, cols].astype(jnp.float32)
                        for c in range(parts)
                    ],
                )
                out_ref[:, cols] = mixed.astype(jnp.bfloat16)


def merge_call(parts, kv_local):
    q_dev, wide = parts[0].shape
    vmem = pl.BlockSpec(memory_space=pltpu.VMEM)
    return pl.pallas_call(
        functools.partial(merge_kernel, len(parts), kv_local),
        out_shape=jax.ShapeDtypeStruct((q_dev, wide - LANES), jnp.bfloat16),
        in_specs=[vmem] * len(parts),
        out_specs=vmem,
        compiler_params=pltpu.CompilerParams(vmem_limit_bytes=VMEM_MERGE),
        cost_estimate=pl.CostEstimate(
            flops=len(parts) * q_dev * wide * 2,
            bytes_accessed=len(parts) * q_dev * wide * 2,
            transcendentals=0,
        ),
        name="merge",
    )(*parts)


def projection_kernel(members, ctx_count, peers, w_ref, *rest):
    blocks = len(members)
    in_refs, rest = rest[:blocks], rest[blocks:]
    own_ref, send_refs, (rows_ref, sum_ref) = rest[0], rest[1:peers], rest[peers:]
    q_dev = in_refs[0].shape[0]
    me = lax.axis_index("ctx")
    for member, ref in zip(members, in_refs):
        at = flipped(me, ctx_count, *member) * q_dev
        rows_ref[pl.ds(pl.multiple_of(at, q_dev), q_dev), :] = ref[...]
    part = own_ref.shape[0]
    my_tp = lax.axis_index("tp")
    sum_ref[...] = jnp.dot(rows_ref[...], w_ref[...], preferred_element_type=jnp.float32)
    own_ref[...] = sum_ref[pl.ds(pl.multiple_of(my_tp * part, part), part), :]
    for j in range(1, peers):
        at = pl.multiple_of((my_tp ^ j) * part, part)
        send_refs[j - 1][...] = sum_ref[pl.ds(at, part), :].astype(jnp.bfloat16)


def projection_call(members, ctx_count, blocks, weight, peers):
    n = len(blocks)
    q_dev, width = blocks[0].shape
    columns = weight.shape[1]
    part = n * q_dev // peers
    vmem = pl.BlockSpec(memory_space=pltpu.VMEM)
    return pl.pallas_call(
        functools.partial(projection_kernel, members, ctx_count, peers),
        out_shape=[jax.ShapeDtypeStruct((part, columns), jnp.float32)]
        + [jax.ShapeDtypeStruct((part, columns), jnp.bfloat16)] * (peers - 1),
        in_specs=[vmem] * (1 + n),
        out_specs=[vmem] * peers,
        scratch_shapes=[
            pltpu.VMEM((n * q_dev, width), jnp.bfloat16),
            pltpu.VMEM((n * q_dev, columns), jnp.float32),
        ],
        compiler_params=pltpu.CompilerParams(vmem_limit_bytes=VMEM_PROJ),
        cost_estimate=pl.CostEstimate(
            flops=2 * n * q_dev * width * columns,
            bytes_accessed=2 * width * columns,
            transcendentals=0,
        ),
        name="projection",
    )(weight, *blocks)


def body(
    queries,
    new_keys,
    new_values,
    cache_keys,
    cache_values,
    keep_tiles,
    tile_count,
    owner_slot,
    out_weight,
):
    ctx_count = lax.axis_size("ctx")
    peers = lax.axis_size("tp")
    low = LOW_SIZE
    high = ctx_count // low

    def move(x, step, flip):
        pairs = [
            (i, (i // low + step) % high * low + (i % low + flip) % low) for i in range(ctx_count)
        ]
        return lax.ppermute(x, "ctx", pairs)

    steps = sorted(range(1, high), key=lambda k: (min(k, high - k), k))
    order = [(k, 0) for k in (0, *steps)] + [(k, 1) for k in (0, *steps)]

    def gather(x, chained):
        held = {(0, 0): x, (0, 1): move(x, 0, 1)}
        for k in steps:
            block = x
            if not chained and 2 * k == high:
                ready = {m: held[m] for m in held if m[0]}
                block, ready = lax.optimization_barrier((block, ready))
                held.update(ready)
            held[k, 0] = move(block, -k, 0)
        behind = None
        for k in steps:
            block = held[k, 0]
            if chained and 2 * k == high and behind is not None:
                block, held[behind] = lax.optimization_barrier((block, held[behind]))
            held[k, 1] = move(block, 0, 1)
            behind = (k, 1)
        return held

    held = gather(queries, False)
    near = [m for m in order[1:] if not m[1] and 2 * m[0] != high]
    middle = [m for m in order[1:] if not m[1] and 2 * m[0] == high]
    flip = [m for m in order if m[1] and m[0] and 2 * m[0] != high]
    late = [m for m in order if m[1] and 2 * m[0] == high] + [(0, 1)]
    groups = [near[i : i + 2] for i in range(0, len(near), 2)]
    groups += [middle + flip[:2]] + [flip[i : i + 2] for i in range(2, len(flip), 2)]
    groups += [late, order[:1]]
    kv_local = new_keys.shape[1] // DH
    table = jnp.concatenate([keep_tiles.reshape(-1), tile_count.reshape(-1), owner_slot])
    new_rows = jnp.concatenate([new_keys, new_values], 1)
    new_rows = hand_on_call(new_rows, cache_keys, cache_values)

    def attend(members, blocks):
        return attention_call(
            members,
            ctx_count,
            kv_local,
            keep_tiles.shape[2],
            blocks,
            table,
            new_rows,
            cache_keys,
            cache_values,
        )

    parts, back = {}, {}
    last = None
    for index, members in enumerate(groups):
        blocks = [held[m] for m in members]
        if last is not None:
            blocks, parts[last] = lax.optimization_barrier((blocks, parts[last]))
        if 2 <= index < len(groups) - 1:
            returned = {m: back[m] for m in groups[index - 2] if 2 * m[0] != high}
            blocks, returned = lax.optimization_barrier((blocks, returned))
            back.update(returned)
        parts.update(zip(members, attend(members, blocks)))
        last = members[-1]
        for m in members:
            back[m] = parts[m] if m == (0, 0) else move(parts[m], *m)
    attn = merge_call([back[m] for m in order], kv_local)

    held = gather(attn, True)
    own, *sends = projection_call(order, ctx_count, [held[m] for m in order], out_weight, peers)
    for j, piece in enumerate(sends, 1):
        got = lax.ppermute(piece, "tp", [(i, i ^ j) for i in range(peers)])
        own = own + got.astype(jnp.float32)
    return own


def solution(mesh):
    return jax.shard_map(
        body,
        mesh=mesh,
        in_specs=(
            P("ctx", "tp"),
            P("ctx", "tp"),
            P("ctx", "tp"),
            P("ctx", "tp"),
            P("ctx", "tp"),
            P("ctx", "tp", None),
            P("ctx", "tp"),
            P(),
            P("tp", "ctx"),
        ),
        out_specs=P("tp", "ctx"),
        check_vma=False,
    )
```

```python
import functools
import math

import jax
import jax.numpy as jnp
from jax import lax
from jax.experimental import pallas as pl
from jax.experimental.pallas import tpu as pltpu
from jax.sharding import PartitionSpec as P

DH = 128
TILE = 128
LANES = 128
CHUNK = 4
LOW = -1e30
ONES = 16
LOW_SIZE = 2
VMEM_PACK = 58 * 2**20
VMEM_ATTN = 24 * 2**20
VMEM_MERGE = 8 * 2**20
VMEM_PROJ = 16 * 2**20


def flipped(me, count, step, flip):
    high = count // LOW_SIZE
    return lax.rem(me // LOW_SIZE + step, high) * LOW_SIZE + lax.rem(me + flip, LOW_SIZE)


def attention_kernel(
    members, ctx_count, group, kv_local, slots, table_ref, new_ref, k_ref, v_ref, *rest
):
    blocks = len(members)
    q_refs, rest = rest[:blocks], rest[blocks:]
    out_refs, rest = rest[:blocks], rest[blocks:]
    q_ref, turned_ref, acc_ref, max_ref = rest
    q_dev = q_refs[0].shape[0]
    heads = kv_local * group
    rows = q_dev * group
    span = CHUNK * TILE
    scale = math.log2(math.e) / math.sqrt(DH)
    me = lax.axis_index("ctx")

    def count_of(g):
        return table_ref[kv_local * slots + g]

    def slot_of(ctx):
        return table_ref[kv_local * (slots + 1) + ctx]

    def turned(x):
        return x.astype(jnp.float32).T.astype(jnp.bfloat16)

    def fold(g, b, s, values, first=False):
        peak = jnp.max(s, axis=0, keepdims=True) * scale
        top = peak if first else jnp.maximum(max_ref[g, b, :1], peak)
        p = jnp.exp2(s * scale - top).astype(jnp.bfloat16)
        mixed = jnp.dot(values, p, preferred_element_type=jnp.float32)
        if not first:
            mixed += acc_ref[g, b] * jnp.exp2(max_ref[g, b, :1] - top)
        max_ref[g, b] = jnp.broadcast_to(top, max_ref.shape[2:])
        acc_ref[g, b] = mixed

    ones_tile = jnp.ones((ONES, TILE), jnp.bfloat16)
    place_key = lax.broadcasted_iota(jnp.int32, (TILE, rows), 0)
    place_row = lax.broadcasted_iota(jnp.int32, (TILE, rows), 1) % q_dev
    padding = jnp.zeros((TILE - q_dev, DH), jnp.bfloat16)

    for g in range(kv_local):
        fresh_keys = jnp.concatenate([new_ref[:, g * DH : (g + 1) * DH], padding], 0)
        fresh_values = new_ref[:, (kv_local + g) * DH : (kv_local + g + 1) * DH]
        fresh_values = jnp.concatenate(
            [turned(jnp.concatenate([fresh_values, padding], 0)), ones_tile], 0
        )
        for b in range(blocks):
            for h in range(group):
                head = g * group + h
                q_ref[h * q_dev : (h + 1) * q_dev, :] = q_refs[b][
                    :, head * DH : (head + 1) * DH
                ].astype(jnp.float32)
            turned_ref[g, b] = q_ref[...].T.astype(jnp.bfloat16)
            s = jnp.dot(fresh_keys, turned_ref[g, b], preferred_element_type=jnp.float32)
            shift = (slot_of(flipped(me, ctx_count, *members[b])) - slot_of(me)) * q_dev
            live = (place_key < q_dev) & (place_row - place_key + shift >= 0)
            fold(g, b, jnp.where(live, s, LOW), fresh_values, first=True)

    def load_chunk(g, chunk):
        cols = slice(g * DH, (g + 1) * DH)
        key_parts, value_parts = [], []
        for i in range(CHUNK):
            slot = chunk * CHUNK + i
            live = slot < count_of(g)
            tile = table_ref[g * slots + jnp.where(live, slot, 0)]
            at = pl.ds(pl.multiple_of(tile * TILE, TILE), TILE)
            key_parts.append(k_ref[at, cols])
            tail = jnp.concatenate([turned(v_ref[at, cols]), ones_tile], 0)
            value_parts.append(jnp.where(live, tail, jnp.zeros_like(tail)))
        return jnp.concatenate(key_parts, 0), jnp.concatenate(value_parts, 1)

    def run(kv_heads, chunk):
        loaded = {g: load_chunk(g, chunk) for g in kv_heads}
        chains = [(g, b) for b in range(blocks) for g in kv_heads]

        def score(g, b):
            return jnp.dot(loaded[g][0], turned_ref[g, b], preferred_element_type=jnp.float32)

        ahead = score(*chains[0])
        for at, (g, b) in enumerate(chains):
            s = ahead
            if at + 1 < len(chains):
                ahead = score(*chains[at + 1])
            fold(g, b, s, loaded[g][1])

    ends = [(count_of(g) + CHUNK - 1) // CHUNK for g in range(kv_local)]
    shared = functools.reduce(jnp.minimum, ends)

    def step_all(chunk, carry):
        run(range(kv_local), chunk)
        return carry

    lax.fori_loop(0, shared, step_all, 0)
    for g in range(kv_local):

        def step_one(chunk, carry, g=g):
            run([g], chunk)
            return carry

        lax.fori_loop(shared, ends[g], step_one, 0)

    sublane = lax.broadcasted_iota(jnp.int32, (q_dev, LANES), 0)
    parts = rows // LANES
    for b in range(blocks):
        stats = jnp.zeros((q_dev, LANES), jnp.float32)
        for g in range(kv_local):
            total = acc_ref[g, b, DH : DH + 1, :]
            mean = (acc_ref[g, b, :DH, :] / total).T.astype(jnp.bfloat16)
            for h in range(group):
                head = g * group + h
                out_refs[b][:, head * DH : (head + 1) * DH] = mean[h * q_dev : (h + 1) * q_dev]
            level = max_ref[g, b, :1] + jnp.log2(total)
            high = level.astype(jnp.bfloat16).astype(jnp.float32)
            middle = (level - high).astype(jnp.bfloat16).astype(jnp.float32)
            for i, term in enumerate((high, middle, level - high - middle)):
                for j in range(parts):
                    at = (g * 3 + i) * parts + j
                    stats = jnp.where(sublane == at, term[:, j * LANES : (j + 1) * LANES], stats)
        out_refs[b][:, heads * DH :] = stats.astype(jnp.bfloat16)


def pack_kernel(slot_ref, keep_ref, count_ref, nk_ref, nv_ref, k_hbm, v_hbm, table_ref, rows_ref):
    kv_local, slots = keep_ref.shape
    for g in range(kv_local):
        for t in range(slots):
            table_ref[g * slots + t] = keep_ref[g, t]
        table_ref[kv_local * slots + g] = count_ref[g]
    for c in range(slot_ref.shape[0]):
        table_ref[kv_local * (slots + 1) + c] = slot_ref[c]
    width = nk_ref.shape[1]
    rows_ref[:, :width] = nk_ref[...]
    rows_ref[:, width:] = nv_ref[...]


def pack_call(slot, keep, count, new_keys, new_values, keys, values):
    smem = pl.BlockSpec(memory_space=pltpu.SMEM)
    vmem = pl.BlockSpec(memory_space=pltpu.VMEM)
    hbm = pl.BlockSpec(memory_space=pltpu.HBM)
    q_dev, width = new_keys.shape
    entries = keep.size + count.size + slot.size
    return pl.pallas_call(
        pack_kernel,
        out_shape=[
            jax.ShapeDtypeStruct((entries,), jnp.int32),
            jax.ShapeDtypeStruct((q_dev, 2 * width), new_keys.dtype),
        ],
        in_specs=[smem] * 3 + [vmem] * 2 + [hbm] * 2,
        out_specs=[smem, vmem],
        compiler_params=pltpu.CompilerParams(vmem_limit_bytes=VMEM_PACK),
        name="pack",
    )(slot, keep, count, new_keys, new_values, keys, values)


def attention_call(members, ctx_count, kv_local, slots, blocks, table, new_rows, keys, values):
    n = len(blocks)
    q_dev, width = blocks[0].shape
    group = width // DH // kv_local
    rows = q_dev * group
    smem = pl.BlockSpec(memory_space=pltpu.SMEM)
    vmem = pl.BlockSpec(memory_space=pltpu.VMEM)
    work = n * rows * kv_local * slots * TILE
    return pl.pallas_call(
        functools.partial(attention_kernel, members, ctx_count, group, kv_local, slots),
        out_shape=[jax.ShapeDtypeStruct((q_dev, width + LANES), jnp.bfloat16)] * n,
        in_specs=[smem] + [vmem] * (3 + n),
        out_specs=[vmem] * n,
        scratch_shapes=[
            pltpu.VMEM((rows, DH), jnp.float32),
            pltpu.VMEM((kv_local, n, DH, rows), jnp.bfloat16),
            pltpu.VMEM((kv_local, n, DH + ONES, rows), jnp.float32),
            pltpu.VMEM((kv_local, n, 8, rows), jnp.float32),
        ],
        compiler_params=pltpu.CompilerParams(vmem_limit_bytes=VMEM_ATTN),
        cost_estimate=pl.CostEstimate(
            flops=work * DH * 8, bytes_accessed=8 * 2**20, transcendentals=work
        ),
        name="attention",
    )(table, new_rows, keys, values, *blocks)


def merge_kernel(parts, kv_local, *refs):
    in_refs, out_ref = refs[:parts], refs[parts]
    q_dev, width = out_ref.shape
    group = width // DH // kv_local
    lane_parts = q_dev * group // LANES
    per_part = LANES // q_dev
    stats = [ref[:, width:].astype(jnp.float32) for ref in in_refs]
    sublane = lax.broadcasted_iota(jnp.int32, (LANES, LANES), 0)
    for j in range(lane_parts):
        table = jnp.zeros((LANES, LANES), jnp.float32)
        for g in range(kv_local):
            at = [(g * 3 + i) * lane_parts + j for i in range(3)]
            levels = [stat[at[0]] + stat[at[1]] + stat[at[2]] for stat in stats]
            levels = [level.reshape(1, LANES) for level in levels]
            top = functools.reduce(jnp.maximum, levels)
            shares = [jnp.exp2(level - top) for level in levels]
            total = functools.reduce(jnp.add, shares)
            for c, share in enumerate(shares):
                table = jnp.where(sublane == g * parts + c, share / total, table)
        table = table.T
        for g in range(kv_local):
            for i in range(per_part):
                head = g * group + j * per_part + i
                cols = slice(head * DH, (head + 1) * DH)
                share = table[i * q_dev : (i + 1) * q_dev]
                mixed = functools.reduce(
                    jnp.add,
                    [
                        share[:, g * parts + c : g * parts + c + 1]
                        * in_refs[c][:, cols].astype(jnp.float32)
                        for c in range(parts)
                    ],
                )
                out_ref[:, cols] = mixed.astype(jnp.bfloat16)


def merge_call(parts, kv_local):
    q_dev, wide = parts[0].shape
    vmem = pl.BlockSpec(memory_space=pltpu.VMEM)
    return pl.pallas_call(
        functools.partial(merge_kernel, len(parts), kv_local),
        out_shape=jax.ShapeDtypeStruct((q_dev, wide - LANES), jnp.bfloat16),
        in_specs=[vmem] * len(parts),
        out_specs=vmem,
        compiler_params=pltpu.CompilerParams(vmem_limit_bytes=VMEM_MERGE),
        cost_estimate=pl.CostEstimate(
            flops=len(parts) * q_dev * wide * 2,
            bytes_accessed=len(parts) * q_dev * wide * 2,
            transcendentals=0,
        ),
        name="merge",
    )(*parts)


def projection_kernel(members, ctx_count, peers, w_ref, *rest):
    blocks = len(members)
    in_refs, rest = rest[:blocks], rest[blocks:]
    own_ref, send_ref, rows_ref, sum_ref = rest
    q_dev = in_refs[0].shape[0]
    me = lax.axis_index("ctx")
    for member, ref in zip(members, in_refs):
        at = flipped(me, ctx_count, *member) * q_dev
        rows_ref[pl.ds(pl.multiple_of(at, q_dev), q_dev), :] = ref[...]
    steps, part = own_ref.shape[:2]
    my_tp = lax.axis_index("tp")
    sum_ref[...] = jnp.dot(rows_ref[...], w_ref[...], preferred_element_type=jnp.float32)

    def piece(peer):
        return sum_ref[pl.ds(pl.multiple_of(peer * part, part), part), :]

    for j in range(steps):
        own_ref[j] = piece(my_tp ^ (2 * j))
        send_ref[j] = piece(my_tp ^ (2 * j + 1)).astype(jnp.bfloat16)


def projection_call(members, ctx_count, blocks, weight, peers):
    n = len(blocks)
    q_dev, width = blocks[0].shape
    columns = weight.shape[1]
    part = n * q_dev // peers
    vmem = pl.BlockSpec(memory_space=pltpu.VMEM)
    return pl.pallas_call(
        functools.partial(projection_kernel, members, ctx_count, peers),
        out_shape=[
            jax.ShapeDtypeStruct((peers // 2, part, columns), jnp.float32),
            jax.ShapeDtypeStruct((peers // 2, part, columns), jnp.bfloat16),
        ],
        in_specs=[vmem] * (1 + n),
        out_specs=[vmem] * 2,
        scratch_shapes=[
            pltpu.VMEM((n * q_dev, width), jnp.bfloat16),
            pltpu.VMEM((n * q_dev, columns), jnp.float32),
        ],
        compiler_params=pltpu.CompilerParams(vmem_limit_bytes=VMEM_PROJ),
        cost_estimate=pl.CostEstimate(
            flops=2 * n * q_dev * width * columns,
            bytes_accessed=2 * width * columns,
            transcendentals=0,
        ),
        name="projection",
    )(weight, *blocks)


def body(
    queries,
    new_keys,
    new_values,
    cache_keys,
    cache_values,
    keep_tiles,
    tile_count,
    owner_slot,
    out_weight,
):
    ctx_count = lax.axis_size("ctx")
    peers = lax.axis_size("tp")
    low = LOW_SIZE
    high = ctx_count // low

    def move(x, step, flip):
        pairs = [
            (i, (i // low + step) % high * low + (i % low + flip) % low) for i in range(ctx_count)
        ]
        return lax.ppermute(x, "ctx", pairs)

    steps = sorted(range(1, high), key=lambda k: (min(k, high - k), k))
    order = [(k, 0) for k in (0, *steps)] + [(k, 1) for k in (0, *steps)]

    def gather(x, chained):
        held = {(0, 0): x, (0, 1): move(x, 0, 1)}
        for k in steps:
            block = x
            if not chained and 2 * k == high:
                ready = {m: held[m] for m in held if m[0]}
                block, ready = lax.optimization_barrier((block, ready))
                held.update(ready)
            held[k, 0] = move(block, -k, 0)
        behind = None
        for k in steps:
            block = held[k, 0]
            if chained and 2 * k == high and behind is not None:
                block, held[behind] = lax.optimization_barrier((block, held[behind]))
            held[k, 1] = move(block, 0, 1)
            behind = (k, 1)
        return held

    held = gather(queries, False)
    near = [m for m in order[1:] if not m[1] and 2 * m[0] != high]
    middle = [m for m in order[1:] if not m[1] and 2 * m[0] == high]
    flip = [m for m in order if m[1] and m[0] and 2 * m[0] != high]
    late = [m for m in order if m[1] and 2 * m[0] == high] + [(0, 1)]
    groups = [near[i : i + 2] for i in range(0, len(near), 2)]
    groups += [middle + flip[:2]] + [flip[i : i + 2] for i in range(2, len(flip), 2)]
    groups += [late, order[:1]]
    kv_local = new_keys.shape[1] // DH
    table, new_rows = pack_call(
        owner_slot,
        keep_tiles[0],
        tile_count[0],
        new_keys,
        new_values,
        cache_keys,
        cache_values,
    )

    def attend(members, blocks):
        return attention_call(
            members,
            ctx_count,
            kv_local,
            keep_tiles.shape[2],
            blocks,
            table,
            new_rows,
            cache_keys,
            cache_values,
        )

    parts, back = {}, {}
    last = None
    for index, members in enumerate(groups):
        blocks = [held[m] for m in members]
        if last is not None:
            blocks, parts[last] = lax.optimization_barrier((blocks, parts[last]))
        if 2 <= index < len(groups) - 1:
            returned = {m: back[m] for m in groups[index - 2] if 2 * m[0] != high}
            blocks, returned = lax.optimization_barrier((blocks, returned))
            back.update(returned)
        parts.update(zip(members, attend(members, blocks)))
        last = members[-1]
        for m in members:
            back[m] = parts[m] if m == (0, 0) else move(parts[m], *m)
    attn = merge_call([back[m] for m in order], kv_local)

    held = gather(attn, True)
    own, send = projection_call(order, ctx_count, [held[m] for m in order], out_weight, peers)
    got = lax.ppermute(send, "tp", [(i, i ^ 1) for i in range(peers)])
    total = own[0] + got[0].astype(jnp.float32)
    for j in range(1, peers // 2):
        piece = (own[j] + got[j].astype(jnp.float32)).astype(jnp.bfloat16)
        piece = lax.ppermute(piece, "tp", [(i, i ^ (2 * j)) for i in range(peers)])
        total = total + piece.astype(jnp.float32)
    return total


def solution(mesh):
    return jax.shard_map(
        body,
        mesh=mesh,
        in_specs=(
            P("ctx", "tp"),
            P("ctx", "tp"),
            P("ctx", "tp"),
            P("ctx", "tp"),
            P("ctx", "tp"),
            P("ctx", "tp", None),
            P("ctx", "tp"),
            P(),
            P("tp", "ctx"),
        ),
        out_specs=P("tp", "ctx"),
        check_vma=False,
    )
```

```python
import functools
import math

import jax
import jax.numpy as jnp
from jax import lax
from jax.experimental import pallas as pl
from jax.experimental.pallas import tpu as pltpu
from jax.sharding import PartitionSpec as P

DH = 128
TILE = 128
LANES = 128
CHUNK = 4
LOW = -1e30
ONES = 16
LOW_SIZE = 2
VMEM_PACK = 58 * 2**20
VMEM_ATTN = 24 * 2**20
VMEM_MERGE = 8 * 2**20
VMEM_PROJ = 16 * 2**20


def flipped(me, count, step, flip):
    high = count // LOW_SIZE
    return lax.rem(me // LOW_SIZE + step, high) * LOW_SIZE + lax.rem(me + flip, LOW_SIZE)


def attention_kernel(
    members, ctx_count, group, kv_local, slots, turn, table_ref, new_ref, k_ref, v_ref, *rest
):
    blocks = len(members)
    q_refs, rest = rest[:blocks], rest[blocks:]
    out_refs, rest = rest[:blocks], rest[blocks:]
    turned_ref, acc_ref, max_ref = rest[-3:]
    kept_ref = rest[0] if turn else v_ref
    last = kept_ref.shape[2] - TILE
    q_dev = q_refs[0].shape[0]
    heads = kv_local * group
    rows = q_dev * group
    span = CHUNK * TILE
    scale = math.log2(math.e) / math.sqrt(DH)
    me = lax.axis_index("ctx")

    def count_of(g):
        return table_ref[kv_local * slots + g]

    def slot_of(ctx):
        return table_ref[kv_local * (slots + 1) + ctx]

    def turned(x):
        return x.T

    def fold(g, b, s, values, first=False):
        peak = jnp.max(s, axis=0, keepdims=True) * scale
        top = peak if first else jnp.maximum(max_ref[g, b, :1], peak)
        p = jnp.exp2(s * scale - top).astype(jnp.bfloat16)
        mixed = jnp.dot(values, p, preferred_element_type=jnp.float32)
        if not first:
            mixed += acc_ref[g, b] * jnp.exp2(max_ref[g, b, :1] - top)
        max_ref[g, b] = jnp.broadcast_to(top, max_ref.shape[2:])
        acc_ref[g, b] = mixed

    ones_tile = jnp.ones((ONES, TILE), jnp.bfloat16)
    place_key = lax.broadcasted_iota(jnp.int32, (TILE, rows), 0)
    place_row = lax.broadcasted_iota(jnp.int32, (TILE, rows), 1) % q_dev
    padding = jnp.zeros((TILE - q_dev, DH), jnp.bfloat16)

    for g in range(kv_local):
        fresh_keys = jnp.concatenate([new_ref[:, g * DH : (g + 1) * DH], padding], 0)
        if turn:
            fresh_values = new_ref[:, (kv_local + g) * DH : (kv_local + g + 1) * DH]
            fresh_values = jnp.concatenate(
                [turned(jnp.concatenate([fresh_values, padding], 0)), ones_tile], 0
            )
            kept_ref[g, :, last:] = fresh_values
        else:
            fresh_values = kept_ref[g, :, last:]
        for b in range(blocks):
            columns = [
                q_refs[b][:, (g * group + h) * DH : (g * group + h + 1) * DH]
                for h in range(group)
            ]
            turned_ref[g, b] = turned(jnp.concatenate(columns, 0))
            s = jnp.dot(fresh_keys, turned_ref[g, b], preferred_element_type=jnp.float32)
            shift = (slot_of(flipped(me, ctx_count, *members[b])) - slot_of(me)) * q_dev
            live = (place_key < q_dev) & (place_row - place_key + shift >= 0)
            fold(g, b, jnp.where(live, s, LOW), fresh_values, first=True)

    def load_chunk(g, chunk):
        cols = slice(g * DH, (g + 1) * DH)
        whole = pl.ds(pl.multiple_of(chunk * span, span), span)
        key_parts, value_parts = [], []
        for i in range(CHUNK):
            slot = chunk * CHUNK + i
            live = slot < count_of(g)
            tile = table_ref[g * slots + jnp.where(live, slot, 0)]
            at = pl.ds(pl.multiple_of(tile * TILE, TILE), TILE)
            key_parts.append(k_ref[at, cols])
            if turn:
                tail = jnp.concatenate([turned(v_ref[at, cols]), ones_tile], 0)
                value_parts.append(jnp.where(live, tail, jnp.zeros_like(tail)))
        keys = jnp.concatenate(key_parts, 0)
        if not turn:
            return keys, kept_ref[g, :, whole]
        values = jnp.concatenate(value_parts, 1)
        kept_ref[g, :, whole] = values
        return keys, values

    def run(kv_heads, chunk):
        loaded = {g: load_chunk(g, chunk) for g in kv_heads}
        chains = [(g, b) for b in range(blocks) for g in kv_heads]

        def score(g, b):
            return jnp.dot(loaded[g][0], turned_ref[g, b], preferred_element_type=jnp.float32)

        ahead = score(*chains[0])
        for at, (g, b) in enumerate(chains):
            s = ahead
            if at + 1 < len(chains):
                ahead = score(*chains[at + 1])
            fold(g, b, s, loaded[g][1])

    ends = [(count_of(g) + CHUNK - 1) // CHUNK for g in range(kv_local)]
    shared = functools.reduce(jnp.minimum, ends)

    def step_all(chunk, carry):
        run(range(kv_local), chunk)
        return carry

    lax.fori_loop(0, shared, step_all, 0)
    for g in range(kv_local):

        def step_one(chunk, carry, g=g):
            run([g], chunk)
            return carry

        lax.fori_loop(shared, ends[g], step_one, 0)

    sublane = lax.broadcasted_iota(jnp.int32, (q_dev, LANES), 0)
    parts = rows // LANES
    for b in range(blocks):
        stats = jnp.zeros((q_dev, LANES), jnp.float32)
        for g in range(kv_local):
            total = acc_ref[g, b, DH : DH + 1, :]
            mean = (acc_ref[g, b, :DH, :] / total).T.astype(jnp.bfloat16)
            for h in range(group):
                head = g * group + h
                out_refs[b][:, head * DH : (head + 1) * DH] = mean[h * q_dev : (h + 1) * q_dev]
            level = max_ref[g, b, :1] + jnp.log2(total)
            high = level.astype(jnp.bfloat16).astype(jnp.float32)
            middle = (level - high).astype(jnp.bfloat16).astype(jnp.float32)
            for i, term in enumerate((high, middle, level - high - middle)):
                for j in range(parts):
                    at = (g * 3 + i) * parts + j
                    stats = jnp.where(sublane == at, term[:, j * LANES : (j + 1) * LANES], stats)
        out_refs[b][:, heads * DH :] = stats.astype(jnp.bfloat16)


def pack_kernel(slot_ref, keep_ref, count_ref, nk_ref, nv_ref, k_hbm, v_hbm, table_ref, rows_ref):
    kv_local, slots = keep_ref.shape
    for g in range(kv_local):
        for t in range(slots):
            table_ref[g * slots + t] = keep_ref[g, t]
        table_ref[kv_local * slots + g] = count_ref[g]
    for c in range(slot_ref.shape[0]):
        table_ref[kv_local * (slots + 1) + c] = slot_ref[c]
    width = nk_ref.shape[1]
    rows_ref[:, :width] = nk_ref[...]
    rows_ref[:, width:] = nv_ref[...]


def pack_call(slot, keep, count, new_keys, new_values, keys, values):
    smem = pl.BlockSpec(memory_space=pltpu.SMEM)
    vmem = pl.BlockSpec(memory_space=pltpu.VMEM)
    hbm = pl.BlockSpec(memory_space=pltpu.HBM)
    q_dev, width = new_keys.shape
    entries = keep.size + count.size + slot.size
    return pl.pallas_call(
        pack_kernel,
        out_shape=[
            jax.ShapeDtypeStruct((entries,), jnp.int32),
            jax.ShapeDtypeStruct((q_dev, 2 * width), new_keys.dtype),
        ],
        in_specs=[smem] * 3 + [vmem] * 2 + [hbm] * 2,
        out_specs=[smem, vmem],
        compiler_params=pltpu.CompilerParams(vmem_limit_bytes=VMEM_PACK),
        name="pack",
    )(slot, keep, count, new_keys, new_values, keys, values)


def attention_call(
    members, ctx_count, kv_local, slots, turn, blocks, table, new_rows, keys, values
):
    n = len(blocks)
    q_dev, width = blocks[0].shape
    group = width // DH // kv_local
    rows = q_dev * group
    smem = pl.BlockSpec(memory_space=pltpu.SMEM)
    vmem = pl.BlockSpec(memory_space=pltpu.VMEM)
    work = n * rows * kv_local * slots * TILE
    kept = -(-slots // CHUNK) * CHUNK + 1
    return pl.pallas_call(
        functools.partial(
            attention_kernel, members, ctx_count, group, kv_local, slots, turn
        ),
        out_shape=[jax.ShapeDtypeStruct((q_dev, width + LANES), jnp.bfloat16)] * n
        + [jax.ShapeDtypeStruct((kv_local, DH + ONES, kept * TILE), jnp.bfloat16)] * turn,
        in_specs=[smem] + [vmem] * (3 + n),
        out_specs=[vmem] * (n + turn),
        scratch_shapes=[
            pltpu.VMEM((kv_local, n, DH, rows), jnp.bfloat16),
            pltpu.VMEM((kv_local, n, DH + ONES, rows), jnp.float32),
            pltpu.VMEM((kv_local, n, 8, rows), jnp.float32),
        ],
        compiler_params=pltpu.CompilerParams(vmem_limit_bytes=VMEM_ATTN),
        cost_estimate=pl.CostEstimate(
            flops=work * DH * 8, bytes_accessed=8 * 2**20, transcendentals=work
        ),
        name="attention",
    )(table, new_rows, keys, values, *blocks)


def merge_kernel(parts, kv_local, *refs):
    in_refs, out_ref = refs[:parts], refs[parts]
    q_dev, width = out_ref.shape
    group = width // DH // kv_local
    lane_parts = q_dev * group // LANES
    per_part = LANES // q_dev
    stats = [ref[:, width:].astype(jnp.float32) for ref in in_refs]
    sublane = lax.broadcasted_iota(jnp.int32, (LANES, LANES), 0)
    for j in range(lane_parts):
        table = jnp.zeros((LANES, LANES), jnp.float32)
        for g in range(kv_local):
            at = [(g * 3 + i) * lane_parts + j for i in range(3)]
            levels = [stat[at[0]] + stat[at[1]] + stat[at[2]] for stat in stats]
            levels = [level.reshape(1, LANES) for level in levels]
            top = functools.reduce(jnp.maximum, levels)
            shares = [jnp.exp2(level - top) for level in levels]
            total = functools.reduce(jnp.add, shares)
            for c, share in enumerate(shares):
                table = jnp.where(sublane == g * parts + c, share / total, table)
        table = table.T
        for g in range(kv_local):
            for i in range(per_part):
                head = g * group + j * per_part + i
                cols = slice(head * DH, (head + 1) * DH)
                share = table[i * q_dev : (i + 1) * q_dev]
                mixed = functools.reduce(
                    jnp.add,
                    [
                        share[:, g * parts + c : g * parts + c + 1]
                        * in_refs[c][:, cols].astype(jnp.float32)
                        for c in range(parts)
                    ],
                )
                out_ref[:, cols] = mixed.astype(jnp.bfloat16)


def merge_call(parts, kv_local):
    q_dev, wide = parts[0].shape
    vmem = pl.BlockSpec(memory_space=pltpu.VMEM)
    return pl.pallas_call(
        functools.partial(merge_kernel, len(parts), kv_local),
        out_shape=jax.ShapeDtypeStruct((q_dev, wide - LANES), jnp.bfloat16),
        in_specs=[vmem] * len(parts),
        out_specs=vmem,
        compiler_params=pltpu.CompilerParams(vmem_limit_bytes=VMEM_MERGE),
        cost_estimate=pl.CostEstimate(
            flops=len(parts) * q_dev * wide * 2,
            bytes_accessed=len(parts) * q_dev * wide * 2,
            transcendentals=0,
        ),
        name="merge",
    )(*parts)


def projection_kernel(members, ctx_count, peers, w_ref, *rest):
    blocks = len(members)
    in_refs, rest = rest[:blocks], rest[blocks:]
    own_ref, send_ref, rows_ref, sum_ref = rest
    q_dev = in_refs[0].shape[0]
    me = lax.axis_index("ctx")
    for member, ref in zip(members, in_refs):
        at = flipped(me, ctx_count, *member) * q_dev
        rows_ref[pl.ds(pl.multiple_of(at, q_dev), q_dev), :] = ref[...]
    steps, part = own_ref.shape[:2]
    my_tp = lax.axis_index("tp")
    sum_ref[...] = jnp.dot(rows_ref[...], w_ref[...], preferred_element_type=jnp.float32)

    def piece(peer):
        return sum_ref[pl.ds(pl.multiple_of(peer * part, part), part), :]

    for j in range(steps):
        own_ref[j] = piece(my_tp ^ (2 * j))
        send_ref[j] = piece(my_tp ^ (2 * j + 1)).astype(jnp.bfloat16)


def projection_call(members, ctx_count, blocks, weight, peers):
    n = len(blocks)
    q_dev, width = blocks[0].shape
    columns = weight.shape[1]
    part = n * q_dev // peers
    vmem = pl.BlockSpec(memory_space=pltpu.VMEM)
    return pl.pallas_call(
        functools.partial(projection_kernel, members, ctx_count, peers),
        out_shape=[
            jax.ShapeDtypeStruct((peers // 2, part, columns), jnp.float32),
            jax.ShapeDtypeStruct((peers // 2, part, columns), jnp.bfloat16),
        ],
        in_specs=[vmem] * (1 + n),
        out_specs=[vmem] * 2,
        scratch_shapes=[
            pltpu.VMEM((n * q_dev, width), jnp.bfloat16),
            pltpu.VMEM((n * q_dev, columns), jnp.float32),
        ],
        compiler_params=pltpu.CompilerParams(vmem_limit_bytes=VMEM_PROJ),
        cost_estimate=pl.CostEstimate(
            flops=2 * n * q_dev * width * columns,
            bytes_accessed=2 * width * columns,
            transcendentals=0,
        ),
        name="projection",
    )(weight, *blocks)


def body(
    queries,
    new_keys,
    new_values,
    cache_keys,
    cache_values,
    keep_tiles,
    tile_count,
    owner_slot,
    out_weight,
):
    ctx_count = lax.axis_size("ctx")
    peers = lax.axis_size("tp")
    low = LOW_SIZE
    high = ctx_count // low

    def move(x, step, flip):
        pairs = [
            (i, (i // low + step) % high * low + (i % low + flip) % low) for i in range(ctx_count)
        ]
        return lax.ppermute(x, "ctx", pairs)

    steps = sorted(range(1, high), key=lambda k: (min(k, high - k), k))
    order = [(k, 0) for k in (0, *steps)] + [(k, 1) for k in (0, *steps)]

    def gather(x, chained):
        held = {(0, 0): x, (0, 1): move(x, 0, 1)}
        for k in steps:
            block = x
            if not chained and 2 * k == high:
                ready = {m: held[m] for m in held if m[0]}
                block, ready = lax.optimization_barrier((block, ready))
                held.update(ready)
            held[k, 0] = move(block, -k, 0)
        behind = None
        for k in steps:
            block = held[k, 0]
            if chained and 2 * k == high and behind is not None:
                block, held[behind] = lax.optimization_barrier((block, held[behind]))
            held[k, 1] = move(block, 0, 1)
            behind = (k, 1)
        return held

    held = gather(queries, False)
    near = [m for m in order[1:] if not m[1] and 2 * m[0] != high]
    middle = [m for m in order[1:] if not m[1] and 2 * m[0] == high]
    flip = [m for m in order if m[1] and m[0] and 2 * m[0] != high]
    late = [m for m in order if m[1] and 2 * m[0] == high] + [(0, 1)]
    groups = [near[i : i + 2] for i in range(0, len(near), 2)]
    groups += [middle + flip[:2]] + [flip[i : i + 2] for i in range(2, len(flip), 2)]
    groups += [late, order[:1]]
    kv_local = new_keys.shape[1] // DH
    table, new_rows = pack_call(
        owner_slot,
        keep_tiles[0],
        tile_count[0],
        new_keys,
        new_values,
        cache_keys,
        cache_values,
    )

    def attend(members, blocks, turn, values):
        return attention_call(
            members,
            ctx_count,
            kv_local,
            keep_tiles.shape[2],
            turn,
            blocks,
            table,
            new_rows,
            cache_keys,
            values,
        )

    values = cache_values
    parts, back = {}, {}
    last = None
    for index, members in enumerate(groups):
        blocks = [held[m] for m in members]
        if last is not None:
            blocks, parts[last] = lax.optimization_barrier((blocks, parts[last]))
        if 2 <= index < len(groups) - 1:
            returned = {m: back[m] for m in groups[index - 2] if 2 * m[0] != high}
            blocks, returned = lax.optimization_barrier((blocks, returned))
            back.update(returned)
        outs = attend(members, blocks, index == 0, values)
        parts.update(zip(members, outs))
        if index == 0:
            values = outs[-1]
        last = members[-1]
        for m in members:
            back[m] = parts[m] if m == (0, 0) else move(parts[m], *m)
    attn = merge_call([back[m] for m in order], kv_local)

    held = gather(attn, True)
    own, send = projection_call(order, ctx_count, [held[m] for m in order], out_weight, peers)
    got = lax.ppermute(send, "tp", [(i, i ^ 1) for i in range(peers)])
    total = own[0] + got[0].astype(jnp.float32)
    for j in range(1, peers // 2):
        piece = (own[j] + got[j].astype(jnp.float32)).astype(jnp.bfloat16)
        piece = lax.ppermute(piece, "tp", [(i, i ^ (2 * j)) for i in range(peers)])
        total = total + piece.astype(jnp.float32)
    return total


def solution(mesh):
    return jax.shard_map(
        body,
        mesh=mesh,
        in_specs=(
            P("ctx", "tp"),
            P("ctx", "tp"),
            P("ctx", "tp"),
            P("ctx", "tp"),
            P("ctx", "tp"),
            P("ctx", "tp", None),
            P("ctx", "tp"),
            P(),
            P("tp", "ctx"),
        ),
        out_specs=P("tp", "ctx"),
        check_vma=False,
    )
```

```python
import functools
import math

import jax
import jax.numpy as jnp
from jax import lax
from jax.experimental import pallas as pl
from jax.experimental.pallas import tpu as pltpu
from jax.sharding import PartitionSpec as P

DH = 128
TILE = 128
LANES = 128
CHUNK = 4
LOW = -1e30
LIMIT = 2.0**100
ONES = 16
LOW_SIZE = 2
VMEM_PACK = 58 * 2**20
VMEM_ATTN = 24 * 2**20
VMEM_MERGE = 8 * 2**20
VMEM_PROJ = 16 * 2**20


def flipped(me, count, step, flip):
    high = count // LOW_SIZE
    return lax.rem(me // LOW_SIZE + step, high) * LOW_SIZE + lax.rem(me + flip, LOW_SIZE)


def attention_kernel(
    members, ctx_count, group, kv_local, slots, turn, table_ref, new_ref, k_ref, v_ref, *rest
):
    blocks = len(members)
    q_refs, rest = rest[:blocks], rest[blocks:]
    out_refs, rest = rest[:blocks], rest[blocks:]
    turned_ref, acc_ref, max_ref = rest[-3:]
    kept_ref = rest[0] if turn else v_ref
    last = kept_ref.shape[2] - TILE
    q_dev = q_refs[0].shape[0]
    heads = kv_local * group
    rows = q_dev * group
    span = CHUNK * TILE
    scale = math.log2(math.e) / math.sqrt(DH)
    me = lax.axis_index("ctx")

    def count_of(g):
        return table_ref[kv_local * slots + g]

    def slot_of(ctx):
        return table_ref[kv_local * (slots + 1) + ctx]

    ones_tile = jnp.ones((ONES, TILE), jnp.bfloat16)
    place_key = lax.broadcasted_iota(jnp.int32, (TILE, rows), 0)
    place_row = lax.broadcasted_iota(jnp.int32, (TILE, rows), 1) % q_dev
    padding = jnp.zeros((TILE - q_dev, DH), jnp.bfloat16)

    def keys_of(g, chunk):
        cols = slice(g * DH, (g + 1) * DH)
        parts = []
        for i in range(CHUNK):
            slot = chunk * CHUNK + i
            tile = table_ref[g * slots + jnp.where(slot < count_of(g), slot, 0)]
            parts.append(k_ref[pl.ds(pl.multiple_of(tile * TILE, TILE), TILE), cols])
        return jnp.concatenate(parts, 0)

    def values_of(g, chunk):
        whole = pl.ds(pl.multiple_of(chunk * span, span), span)
        if not turn:
            return kept_ref[g, :, whole]
        cols = slice(g * DH, (g + 1) * DH)
        parts = []
        for i in range(CHUNK):
            slot = chunk * CHUNK + i
            live = slot < count_of(g)
            tile = table_ref[g * slots + jnp.where(live, slot, 0)]
            at = pl.ds(pl.multiple_of(tile * TILE, TILE), TILE)
            tail = jnp.concatenate([v_ref[at, cols].T, ones_tile], 0)
            parts.append(jnp.where(live, tail, jnp.zeros_like(tail)))
        values = jnp.concatenate(parts, 1)
        kept_ref[g, :, whole] = values
        return values

    def open_state(g, b, keys, values):
        s = jnp.dot(keys, turned_ref[g, b], preferred_element_type=jnp.float32)
        shift = (slot_of(flipped(me, ctx_count, *members[b])) - slot_of(me)) * q_dev
        live = (place_key < q_dev) & (place_row - place_key + shift >= 0)
        s = jnp.concatenate([s[:span], jnp.where(live, s[span:], LOW)], 0)
        top = jnp.max(s, axis=0, keepdims=True) * scale
        p = jnp.exp2(s * scale - top).astype(jnp.bfloat16)
        max_ref[g, b] = jnp.broadcast_to(top, max_ref.shape[2:])
        acc_ref[g, b] = jnp.dot(values, p, preferred_element_type=jnp.float32)

    def open_head(g, first_values):
        fresh = jnp.concatenate([new_ref[:, g * DH : (g + 1) * DH], padding], 0)
        keys = jnp.concatenate([keys_of(g, 0), fresh], 0)
        values = jnp.concatenate([first_values, kept_ref[g, :, last:]], 1)
        for b in range(blocks):
            open_state(g, b, keys, values)

    for g in range(kv_local):
        if turn:
            fresh_values = new_ref[:, (kv_local + g) * DH : (kv_local + g + 1) * DH]
            fresh_values = jnp.concatenate([fresh_values, padding], 0).T
            kept_ref[g, :, last:] = jnp.concatenate([fresh_values, ones_tile], 0)
        for b in range(blocks):
            columns = [
                q_refs[b][:, (g * group + h) * DH : (g * group + h + 1) * DH]
                for h in range(group)
            ]
            turned_ref[g, b] = jnp.concatenate(columns, 0).T
        open_head(g, values_of(g, 0))

    def run(kv_heads, chunk):
        loaded = {g: (keys_of(g, chunk), values_of(g, chunk)) for g in kv_heads}
        for b in range(blocks):
            for g in kv_heads:
                keys, values = loaded[g]
                s = jnp.dot(keys, turned_ref[g, b], preferred_element_type=jnp.float32)
                p = jnp.exp2(s * scale - max_ref[g, b, :1]).astype(jnp.bfloat16)
                acc_ref[g, b] += jnp.dot(values, p, preferred_element_type=jnp.float32)

    ends = [(count_of(g) + CHUNK - 1) // CHUNK for g in range(kv_local)]
    shared = functools.reduce(jnp.minimum, ends)

    def step_all(chunk, carry):
        run(range(kv_local), chunk)
        return carry

    lax.fori_loop(1, shared, step_all, 0)
    for g in range(kv_local):

        def step_one(chunk, carry, g=g):
            run([g], chunk)
            return carry

        lax.fori_loop(shared, ends[g], step_one, 0)

    large = jnp.zeros((1, rows), jnp.float32)
    for g in range(kv_local):
        for b in range(blocks):
            fits = acc_ref[g, b, DH : DH + 1, :] < LIMIT
            large = jnp.maximum(large, jnp.where(fits, 0.0, 1.0))

    @pl.when(jnp.max(large) > 0.0)
    def again():
        for g in range(kv_local):
            open_head(g, kept_ref[g, :, :span])

            def step_exact(chunk, carry, g=g):
                keys = keys_of(g, chunk)
                values = kept_ref[g, :, pl.ds(pl.multiple_of(chunk * span, span), span)]
                for b in range(blocks):
                    s = jnp.dot(keys, turned_ref[g, b], preferred_element_type=jnp.float32)
                    old = max_ref[g, b, :1]
                    top = jnp.maximum(old, jnp.max(s, axis=0, keepdims=True) * scale)
                    p = jnp.exp2(s * scale - top).astype(jnp.bfloat16)
                    max_ref[g, b] = jnp.broadcast_to(top, max_ref.shape[2:])
                    acc_ref[g, b] = acc_ref[g, b] * jnp.exp2(old - top) + jnp.dot(
                        values, p, preferred_element_type=jnp.float32
                    )
                return carry

            lax.fori_loop(1, ends[g], step_exact, 0)

    sublane = lax.broadcasted_iota(jnp.int32, (q_dev, LANES), 0)
    parts = rows // LANES
    for b in range(blocks):
        stats = jnp.zeros((q_dev, LANES), jnp.float32)
        for g in range(kv_local):
            total = acc_ref[g, b, DH : DH + 1, :]
            mean = (acc_ref[g, b, :DH, :] / total).T.astype(jnp.bfloat16)
            for h in range(group):
                head = g * group + h
                out_refs[b][:, head * DH : (head + 1) * DH] = mean[h * q_dev : (h + 1) * q_dev]
            level = max_ref[g, b, :1] + jnp.log2(total)
            high = level.astype(jnp.bfloat16).astype(jnp.float32)
            middle = (level - high).astype(jnp.bfloat16).astype(jnp.float32)
            for i, term in enumerate((high, middle, level - high - middle)):
                for j in range(parts):
                    at = (g * 3 + i) * parts + j
                    stats = jnp.where(sublane == at, term[:, j * LANES : (j + 1) * LANES], stats)
        out_refs[b][:, heads * DH :] = stats.astype(jnp.bfloat16)


def pack_kernel(slot_ref, keep_ref, count_ref, nk_ref, nv_ref, k_hbm, v_hbm, table_ref, rows_ref):
    kv_local, slots = keep_ref.shape
    for g in range(kv_local):
        for t in range(slots):
            table_ref[g * slots + t] = keep_ref[g, t]
        table_ref[kv_local * slots + g] = count_ref[g]
    for c in range(slot_ref.shape[0]):
        table_ref[kv_local * (slots + 1) + c] = slot_ref[c]
    width = nk_ref.shape[1]
    rows_ref[:, :width] = nk_ref[...]
    rows_ref[:, width:] = nv_ref[...]


def pack_call(slot, keep, count, new_keys, new_values, keys, values):
    smem = pl.BlockSpec(memory_space=pltpu.SMEM)
    vmem = pl.BlockSpec(memory_space=pltpu.VMEM)
    hbm = pl.BlockSpec(memory_space=pltpu.HBM)
    q_dev, width = new_keys.shape
    entries = keep.size + count.size + slot.size
    return pl.pallas_call(
        pack_kernel,
        out_shape=[
            jax.ShapeDtypeStruct((entries,), jnp.int32),
            jax.ShapeDtypeStruct((q_dev, 2 * width), new_keys.dtype),
        ],
        in_specs=[smem] * 3 + [vmem] * 2 + [hbm] * 2,
        out_specs=[smem, vmem],
        compiler_params=pltpu.CompilerParams(vmem_limit_bytes=VMEM_PACK),
        name="pack",
    )(slot, keep, count, new_keys, new_values, keys, values)


def attention_call(
    members, ctx_count, kv_local, slots, turn, blocks, table, new_rows, keys, values
):
    n = len(blocks)
    q_dev, width = blocks[0].shape
    group = width // DH // kv_local
    rows = q_dev * group
    smem = pl.BlockSpec(memory_space=pltpu.SMEM)
    vmem = pl.BlockSpec(memory_space=pltpu.VMEM)
    work = n * rows * kv_local * slots * TILE
    kept = -(-slots // CHUNK) * CHUNK + 1
    return pl.pallas_call(
        functools.partial(
            attention_kernel, members, ctx_count, group, kv_local, slots, turn
        ),
        out_shape=[jax.ShapeDtypeStruct((q_dev, width + LANES), jnp.bfloat16)] * n
        + [jax.ShapeDtypeStruct((kv_local, DH + ONES, kept * TILE), jnp.bfloat16)] * turn,
        in_specs=[smem] + [vmem] * (3 + n),
        out_specs=[vmem] * (n + turn),
        scratch_shapes=[
            pltpu.VMEM((kv_local, n, DH, rows), jnp.bfloat16),
            pltpu.VMEM((kv_local, n, DH + ONES, rows), jnp.float32),
            pltpu.VMEM((kv_local, n, 8, rows), jnp.float32),
        ],
        compiler_params=pltpu.CompilerParams(vmem_limit_bytes=VMEM_ATTN),
        cost_estimate=pl.CostEstimate(
            flops=work * DH * 8, bytes_accessed=8 * 2**20, transcendentals=work
        ),
        name="attention",
    )(table, new_rows, keys, values, *blocks)


def merge_kernel(parts, kv_local, *refs):
    in_refs, out_ref = refs[:parts], refs[parts]
    q_dev, width = out_ref.shape
    group = width // DH // kv_local
    lane_parts = q_dev * group // LANES
    per_part = LANES // q_dev
    stats = [ref[:, width:].astype(jnp.float32) for ref in in_refs]
    sublane = lax.broadcasted_iota(jnp.int32, (LANES, LANES), 0)
    for j in range(lane_parts):
        table = jnp.zeros((LANES, LANES), jnp.float32)
        for g in range(kv_local):
            at = [(g * 3 + i) * lane_parts + j for i in range(3)]
            levels = [stat[at[0]] + stat[at[1]] + stat[at[2]] for stat in stats]
            levels = [level.reshape(1, LANES) for level in levels]
            top = functools.reduce(jnp.maximum, levels)
            shares = [jnp.exp2(level - top) for level in levels]
            total = functools.reduce(jnp.add, shares)
            for c, share in enumerate(shares):
                table = jnp.where(sublane == g * parts + c, share / total, table)
        table = table.T
        for g in range(kv_local):
            for i in range(per_part):
                head = g * group + j * per_part + i
                cols = slice(head * DH, (head + 1) * DH)
                share = table[i * q_dev : (i + 1) * q_dev]
                mixed = functools.reduce(
                    jnp.add,
                    [
                        share[:, g * parts + c : g * parts + c + 1]
                        * in_refs[c][:, cols].astype(jnp.float32)
                        for c in range(parts)
                    ],
                )
                out_ref[:, cols] = mixed.astype(jnp.bfloat16)


def merge_call(parts, kv_local):
    q_dev, wide = parts[0].shape
    vmem = pl.BlockSpec(memory_space=pltpu.VMEM)
    return pl.pallas_call(
        functools.partial(merge_kernel, len(parts), kv_local),
        out_shape=jax.ShapeDtypeStruct((q_dev, wide - LANES), jnp.bfloat16),
        in_specs=[vmem] * len(parts),
        out_specs=vmem,
        compiler_params=pltpu.CompilerParams(vmem_limit_bytes=VMEM_MERGE),
        cost_estimate=pl.CostEstimate(
            flops=len(parts) * q_dev * wide * 2,
            bytes_accessed=len(parts) * q_dev * wide * 2,
            transcendentals=0,
        ),
        name="merge",
    )(*parts)


def projection_kernel(members, ctx_count, peers, w_ref, *rest):
    blocks = len(members)
    in_refs, rest = rest[:blocks], rest[blocks:]
    own_ref, send_ref, rows_ref, sum_ref = rest
    q_dev = in_refs[0].shape[0]
    me = lax.axis_index("ctx")
    for member, ref in zip(members, in_refs):
        at = flipped(me, ctx_count, *member) * q_dev
        rows_ref[pl.ds(pl.multiple_of(at, q_dev), q_dev), :] = ref[...]
    steps, part = own_ref.shape[:2]
    my_tp = lax.axis_index("tp")
    sum_ref[...] = jnp.dot(rows_ref[...], w_ref[...], preferred_element_type=jnp.float32)

    def piece(peer):
        return sum_ref[pl.ds(pl.multiple_of(peer * part, part), part), :]

    for j in range(steps):
        own_ref[j] = piece(my_tp ^ (2 * j))
        send_ref[j] = piece(my_tp ^ (2 * j + 1)).astype(jnp.bfloat16)


def projection_call(members, ctx_count, blocks, weight, peers):
    n = len(blocks)
    q_dev, width = blocks[0].shape
    columns = weight.shape[1]
    part = n * q_dev // peers
    vmem = pl.BlockSpec(memory_space=pltpu.VMEM)
    return pl.pallas_call(
        functools.partial(projection_kernel, members, ctx_count, peers),
        out_shape=[
            jax.ShapeDtypeStruct((peers // 2, part, columns), jnp.float32),
            jax.ShapeDtypeStruct((peers // 2, part, columns), jnp.bfloat16),
        ],
        in_specs=[vmem] * (1 + n),
        out_specs=[vmem] * 2,
        scratch_shapes=[
            pltpu.VMEM((n * q_dev, width), jnp.bfloat16),
            pltpu.VMEM((n * q_dev, columns), jnp.float32),
        ],
        compiler_params=pltpu.CompilerParams(vmem_limit_bytes=VMEM_PROJ),
        cost_estimate=pl.CostEstimate(
            flops=2 * n * q_dev * width * columns,
            bytes_accessed=2 * width * columns,
            transcendentals=0,
        ),
        name="projection",
    )(weight, *blocks)


def body(
    queries,
    new_keys,
    new_values,
    cache_keys,
    cache_values,
    keep_tiles,
    tile_count,
    owner_slot,
    out_weight,
):
    ctx_count = lax.axis_size("ctx")
    peers = lax.axis_size("tp")
    low = LOW_SIZE
    high = ctx_count // low

    def move(x, step, flip):
        pairs = [
            (i, (i // low + step) % high * low + (i % low + flip) % low) for i in range(ctx_count)
        ]
        return lax.ppermute(x, "ctx", pairs)

    steps = sorted(range(1, high), key=lambda k: (min(k, high - k), k))
    order = [(k, 0) for k in (0, *steps)] + [(k, 1) for k in (0, *steps)]

    def gather(x, chained):
        held = {(0, 0): x, (0, 1): move(x, 0, 1)}
        for k in steps:
            block = x
            if not chained and 2 * k == high:
                ready = {m: held[m] for m in held if m[0]}
                block, ready = lax.optimization_barrier((block, ready))
                held.update(ready)
            held[k, 0] = move(block, -k, 0)
        behind = None
        for k in steps:
            block = held[k, 0]
            if chained and 2 * k == high and behind is not None:
                block, held[behind] = lax.optimization_barrier((block, held[behind]))
            held[k, 1] = move(block, 0, 1)
            behind = (k, 1)
        return held

    held = gather(queries, False)
    near = [m for m in order[1:] if not m[1] and 2 * m[0] != high]
    middle = [m for m in order[1:] if not m[1] and 2 * m[0] == high]
    flip = [m for m in order if m[1] and m[0] and 2 * m[0] != high]
    late = [m for m in order if m[1] and 2 * m[0] == high] + [(0, 1)]
    groups = [near[i : i + 2] for i in range(0, len(near), 2)]
    groups += [middle + flip[:2]] + [flip[i : i + 2] for i in range(2, len(flip), 2)]
    groups += [late, order[:1]]
    kv_local = new_keys.shape[1] // DH
    table, new_rows = pack_call(
        owner_slot,
        keep_tiles[0],
        tile_count[0],
        new_keys,
        new_values,
        cache_keys,
        cache_values,
    )

    def attend(members, blocks, turn, values):
        return attention_call(
            members,
            ctx_count,
            kv_local,
            keep_tiles.shape[2],
            turn,
            blocks,
            table,
            new_rows,
            cache_keys,
            values,
        )

    values = cache_values
    parts, back = {}, {}
    last = None
    for index, members in enumerate(groups):
        blocks = [held[m] for m in members]
        if last is not None:
            blocks, parts[last] = lax.optimization_barrier((blocks, parts[last]))
        if 2 <= index < len(groups) - 1:
            returned = {m: back[m] for m in groups[index - 2] if 2 * m[0] != high}
            blocks, returned = lax.optimization_barrier((blocks, returned))
            back.update(returned)
        outs = attend(members, blocks, index == 0, values)
        parts.update(zip(members, outs))
        if index == 0:
            values = outs[-1]
        last = members[-1]
        for m in members:
            back[m] = parts[m] if m == (0, 0) else move(parts[m], *m)
    attn = merge_call([back[m] for m in order], kv_local)

    held = gather(attn, True)
    own, send = projection_call(order, ctx_count, [held[m] for m in order], out_weight, peers)
    got = lax.ppermute(send, "tp", [(i, i ^ 1) for i in range(peers)])
    total = own[0] + got[0].astype(jnp.float32)
    for j in range(1, peers // 2):
        piece = (own[j] + got[j].astype(jnp.float32)).astype(jnp.bfloat16)
        piece = lax.ppermute(piece, "tp", [(i, i ^ (2 * j)) for i in range(peers)])
        total = total + piece.astype(jnp.float32)
    return total


def solution(mesh):
    return jax.shard_map(
        body,
        mesh=mesh,
        in_specs=(
            P("ctx", "tp"),
            P("ctx", "tp"),
            P("ctx", "tp"),
            P("ctx", "tp"),
            P("ctx", "tp"),
            P("ctx", "tp", None),
            P("ctx", "tp"),
            P(),
            P("tp", "ctx"),
        ),
        out_specs=P("tp", "ctx"),
        check_vma=False,
    )
```

```python
import functools
import math

import jax
import jax.numpy as jnp
from jax import lax
from jax.experimental import pallas as pl
from jax.experimental.pallas import tpu as pltpu
from jax.sharding import PartitionSpec as P

DH = 128
TILE = 128
LANES = 128
CHUNK = 4
LOW = -1e30
LIMIT = 2.0**100
ONES = 16
LOW_SIZE = 2
VMEM_PACK = 58 * 2**20
VMEM_ATTN = 24 * 2**20
VMEM_MERGE = 8 * 2**20
VMEM_PROJ = 16 * 2**20


def flipped(me, count, step, flip):
    high = count // LOW_SIZE
    return lax.rem(me // LOW_SIZE + step, high) * LOW_SIZE + lax.rem(me + flip, LOW_SIZE)


def attention_kernel(
    members, ctx_count, group, kv_local, slots, turn, extra, slot_ref, keep_ref, count_ref, nk_ref, nv_ref, k_ref, v_ref, *rest
):
    blocks = len(members)
    q_refs, rest = rest[:blocks], rest[blocks + extra :]
    out_refs, rest = rest[:blocks], rest[blocks:]
    turned_ref, acc_ref, max_ref = rest[-3:]
    kept_ref = rest[0] if turn else v_ref
    last = kept_ref.shape[2] - TILE
    q_dev = q_refs[0].shape[0]
    heads = kv_local * group
    rows = q_dev * group
    span = CHUNK * TILE
    scale = math.log2(math.e) / math.sqrt(DH)
    me = lax.axis_index("ctx")

    def count_of(g):
        return count_ref[g]

    def slot_of(ctx):
        return slot_ref[ctx]

    ones_tile = jnp.ones((ONES, TILE), jnp.bfloat16)
    place_key = lax.broadcasted_iota(jnp.int32, (TILE, rows), 0)
    place_row = lax.broadcasted_iota(jnp.int32, (TILE, rows), 1) % q_dev
    padding = jnp.zeros((TILE - q_dev, DH), jnp.bfloat16)

    def keys_of(g, chunk):
        cols = slice(g * DH, (g + 1) * DH)
        parts = []
        for i in range(CHUNK):
            slot = chunk * CHUNK + i
            tile = keep_ref[g, jnp.where(slot < count_of(g), slot, 0)]
            parts.append(k_ref[pl.ds(pl.multiple_of(tile * TILE, TILE), TILE), cols])
        return jnp.concatenate(parts, 0)

    def values_of(g, chunk):
        whole = pl.ds(pl.multiple_of(chunk * span, span), span)
        if not turn:
            return kept_ref[g, :, whole]
        cols = slice(g * DH, (g + 1) * DH)
        parts = []
        for i in range(CHUNK):
            slot = chunk * CHUNK + i
            live = slot < count_of(g)
            tile = keep_ref[g, jnp.where(live, slot, 0)]
            at = pl.ds(pl.multiple_of(tile * TILE, TILE), TILE)
            tail = jnp.concatenate([v_ref[at, cols].T, ones_tile], 0)
            parts.append(jnp.where(live, tail, jnp.zeros_like(tail)))
        values = jnp.concatenate(parts, 1)
        kept_ref[g, :, whole] = values
        return values

    def open_head(g):
        cols = slice(g * DH, (g + 1) * DH)
        first = pl.ds(pl.multiple_of(keep_ref[g, 0] * TILE, TILE), TILE)
        keys = jnp.concatenate([nk_ref[:, cols], padding, k_ref[first, cols]], 0)
        for b in range(blocks):
            s = jnp.dot(keys, turned_ref[g, b], preferred_element_type=jnp.float32)
            shift = (slot_of(flipped(me, ctx_count, *members[b])) - slot_of(me)) * q_dev
            live = (place_key < q_dev) & (place_row - place_key + shift >= 0)
            fresh = jnp.where(live, s[:TILE], LOW)
            top = jnp.max(jnp.maximum(fresh, s[TILE:]), axis=0, keepdims=True) * scale
            p = jnp.exp2(fresh * scale - top).astype(jnp.bfloat16)
            max_ref[g, b] = jnp.broadcast_to(top, max_ref.shape[2:])
            acc_ref[g, b] = jnp.dot(
                kept_ref[g, :, last:], p, preferred_element_type=jnp.float32
            )

    for g in range(kv_local):
        if turn:
            fresh_values = nv_ref[:, g * DH : (g + 1) * DH]
            fresh_values = jnp.concatenate([fresh_values, padding], 0).T
            kept_ref[g, :, last:] = jnp.concatenate([fresh_values, ones_tile], 0)
        for b in range(blocks):
            columns = [
                q_refs[b][:, (g * group + h) * DH : (g * group + h + 1) * DH]
                for h in range(group)
            ]
            turned_ref[g, b] = jnp.concatenate(columns, 0).T
        open_head(g)

    def run(kv_heads, chunk):
        loaded = {g: (keys_of(g, chunk), values_of(g, chunk)) for g in kv_heads}
        chains = [(g, b) for b in range(blocks) for g in kv_heads]

        def score(g, b):
            return jnp.dot(loaded[g][0], turned_ref[g, b], preferred_element_type=jnp.float32)

        ahead = score(*chains[0])
        for at, (g, b) in enumerate(chains):
            s = ahead
            if at + 1 < len(chains):
                ahead = score(*chains[at + 1])
            p = jnp.exp2(s * scale - max_ref[g, b, :1]).astype(jnp.bfloat16)
            acc_ref[g, b] += jnp.dot(loaded[g][1], p, preferred_element_type=jnp.float32)

    ends = [(count_of(g) + CHUNK - 1) // CHUNK for g in range(kv_local)]
    shared = functools.reduce(jnp.minimum, ends)

    def step_all(chunk, carry):
        run(range(kv_local), chunk)
        return carry

    lax.fori_loop(0, shared, step_all, 0)
    for g in range(kv_local):

        def step_one(chunk, carry, g=g):
            run([g], chunk)
            return carry

        lax.fori_loop(shared, ends[g], step_one, 0)

    large = jnp.zeros((1, rows), jnp.float32)
    for g in range(kv_local):
        for b in range(blocks):
            fits = acc_ref[g, b, DH : DH + 1, :] < LIMIT
            large = jnp.maximum(large, jnp.where(fits, 0.0, 1.0))

    @pl.when(jnp.max(large) > 0.0)
    def again():
        for g in range(kv_local):
            open_head(g)

            def step_exact(chunk, carry, g=g):
                keys = keys_of(g, chunk)
                values = kept_ref[g, :, pl.ds(pl.multiple_of(chunk * span, span), span)]
                for b in range(blocks):
                    s = jnp.dot(keys, turned_ref[g, b], preferred_element_type=jnp.float32)
                    old = max_ref[g, b, :1]
                    top = jnp.maximum(old, jnp.max(s, axis=0, keepdims=True) * scale)
                    p = jnp.exp2(s * scale - top).astype(jnp.bfloat16)
                    max_ref[g, b] = jnp.broadcast_to(top, max_ref.shape[2:])
                    acc_ref[g, b] = acc_ref[g, b] * jnp.exp2(old - top) + jnp.dot(
                        values, p, preferred_element_type=jnp.float32
                    )
                return carry

            lax.fori_loop(0, ends[g], step_exact, 0)

    sublane = lax.broadcasted_iota(jnp.int32, (q_dev, LANES), 0)
    parts = rows // LANES
    for b in range(blocks):
        stats = jnp.zeros((q_dev, LANES), jnp.float32)
        for g in range(kv_local):
            total = acc_ref[g, b, DH : DH + 1, :]
            mean = (acc_ref[g, b, :DH, :] / total).T.astype(jnp.bfloat16)
            for h in range(group):
                head = g * group + h
                out_refs[b][:, head * DH : (head + 1) * DH] = mean[h * q_dev : (h + 1) * q_dev]
            level = max_ref[g, b, :1] + jnp.log2(total)
            high = level.astype(jnp.bfloat16).astype(jnp.float32)
            middle = (level - high).astype(jnp.bfloat16).astype(jnp.float32)
            for i, term in enumerate((high, middle, level - high - middle)):
                for j in range(parts):
                    at = (g * 3 + i) * parts + j
                    stats = jnp.where(sublane == at, term[:, j * LANES : (j + 1) * LANES], stats)
        out_refs[b][:, heads * DH :] = stats.astype(jnp.bfloat16)


def settle_kernel(k_hbm, v_hbm, nk_hbm, nv_hbm, out_ref):
    out_ref[...] = jnp.zeros_like(out_ref)


def settle_call(*arrays):
    return pl.pallas_call(
        settle_kernel,
        out_shape=jax.ShapeDtypeStruct((8, LANES), jnp.float32),
        in_specs=[pl.BlockSpec(memory_space=pltpu.HBM)] * len(arrays),
        out_specs=pl.BlockSpec(memory_space=pltpu.VMEM),
        compiler_params=pltpu.CompilerParams(vmem_limit_bytes=VMEM_PACK),
        name="settle",
    )(*arrays)


def attention_call(
    members, ctx_count, kv_local, slots, turn, blocks, small, keys, values, extra
):
    n = len(blocks)
    q_dev, width = blocks[0].shape
    group = width // DH // kv_local
    rows = q_dev * group
    smem = pl.BlockSpec(memory_space=pltpu.SMEM)
    vmem = pl.BlockSpec(memory_space=pltpu.VMEM)
    work = n * rows * kv_local * slots * TILE
    kept = -(-slots // CHUNK) * CHUNK + 1
    return pl.pallas_call(
        functools.partial(
            attention_kernel, members, ctx_count, group, kv_local, slots, turn, len(extra)
        ),
        out_shape=[jax.ShapeDtypeStruct((q_dev, width + LANES), jnp.bfloat16)] * n
        + [jax.ShapeDtypeStruct((kv_local, DH + ONES, kept * TILE), jnp.bfloat16)] * turn,
        in_specs=[smem] * 3 + [vmem] * (4 + n + len(extra)),
        out_specs=[vmem] * (n + turn),
        scratch_shapes=[
            pltpu.VMEM((kv_local, n, DH, rows), jnp.bfloat16),
            pltpu.VMEM((kv_local, n, DH + ONES, rows), jnp.float32),
            pltpu.VMEM((kv_local, n, 8, rows), jnp.float32),
        ],
        compiler_params=pltpu.CompilerParams(vmem_limit_bytes=VMEM_ATTN),
        cost_estimate=pl.CostEstimate(
            flops=work * DH * 8, bytes_accessed=8 * 2**20, transcendentals=work
        ),
        name="attention",
    )(*small, keys, values, *blocks, *extra)


def merge_kernel(parts, kv_local, *refs):
    in_refs, out_ref = refs[:parts], refs[parts]
    q_dev, width = out_ref.shape
    group = width // DH // kv_local
    lane_parts = q_dev * group // LANES
    per_part = LANES // q_dev
    stats = [ref[:, width:].astype(jnp.float32) for ref in in_refs]
    sublane = lax.broadcasted_iota(jnp.int32, (LANES, LANES), 0)
    for j in range(lane_parts):
        table = jnp.zeros((LANES, LANES), jnp.float32)
        for g in range(kv_local):
            at = [(g * 3 + i) * lane_parts + j for i in range(3)]
            levels = [stat[at[0]] + stat[at[1]] + stat[at[2]] for stat in stats]
            levels = [level.reshape(1, LANES) for level in levels]
            top = functools.reduce(jnp.maximum, levels)
            shares = [jnp.exp2(level - top) for level in levels]
            total = functools.reduce(jnp.add, shares)
            for c, share in enumerate(shares):
                table = jnp.where(sublane == g * parts + c, share / total, table)
        table = table.T
        for g in range(kv_local):
            for i in range(per_part):
                head = g * group + j * per_part + i
                cols = slice(head * DH, (head + 1) * DH)
                share = table[i * q_dev : (i + 1) * q_dev]
                mixed = functools.reduce(
                    jnp.add,
                    [
                        share[:, g * parts + c : g * parts + c + 1]
                        * in_refs[c][:, cols].astype(jnp.float32)
                        for c in range(parts)
                    ],
                )
                out_ref[:, cols] = mixed.astype(jnp.bfloat16)


def merge_call(parts, kv_local):
    q_dev, wide = parts[0].shape
    vmem = pl.BlockSpec(memory_space=pltpu.VMEM)
    return pl.pallas_call(
        functools.partial(merge_kernel, len(parts), kv_local),
        out_shape=jax.ShapeDtypeStruct((q_dev, wide - LANES), jnp.bfloat16),
        in_specs=[vmem] * len(parts),
        out_specs=vmem,
        compiler_params=pltpu.CompilerParams(vmem_limit_bytes=VMEM_MERGE),
        cost_estimate=pl.CostEstimate(
            flops=len(parts) * q_dev * wide * 2,
            bytes_accessed=len(parts) * q_dev * wide * 2,
            transcendentals=0,
        ),
        name="merge",
    )(*parts)


def projection_kernel(members, ctx_count, peers, w_ref, *rest):
    blocks = len(members)
    in_refs, rest = rest[:blocks], rest[blocks:]
    own_ref, send_ref, rows_ref, sum_ref = rest
    q_dev = in_refs[0].shape[0]
    me = lax.axis_index("ctx")
    for member, ref in zip(members, in_refs):
        at = flipped(me, ctx_count, *member) * q_dev
        rows_ref[pl.ds(pl.multiple_of(at, q_dev), q_dev), :] = ref[...]
    steps, part = own_ref.shape[:2]
    my_tp = lax.axis_index("tp")
    sum_ref[...] = jnp.dot(rows_ref[...], w_ref[...], preferred_element_type=jnp.float32)

    def piece(peer):
        return sum_ref[pl.ds(pl.multiple_of(peer * part, part), part), :]

    for j in range(steps):
        own_ref[j] = piece(my_tp ^ (2 * j))
        send_ref[j] = piece(my_tp ^ (2 * j + 1)).astype(jnp.bfloat16)


def projection_call(members, ctx_count, blocks, weight, peers):
    n = len(blocks)
    q_dev, width = blocks[0].shape
    columns = weight.shape[1]
    part = n * q_dev // peers
    vmem = pl.BlockSpec(memory_space=pltpu.VMEM)
    return pl.pallas_call(
        functools.partial(projection_kernel, members, ctx_count, peers),
        out_shape=[
            jax.ShapeDtypeStruct((peers // 2, part, columns), jnp.float32),
            jax.ShapeDtypeStruct((peers // 2, part, columns), jnp.bfloat16),
        ],
        in_specs=[vmem] * (1 + n),
        out_specs=[vmem] * 2,
        scratch_shapes=[
            pltpu.VMEM((n * q_dev, width), jnp.bfloat16),
            pltpu.VMEM((n * q_dev, columns), jnp.float32),
        ],
        compiler_params=pltpu.CompilerParams(vmem_limit_bytes=VMEM_PROJ),
        cost_estimate=pl.CostEstimate(
            flops=2 * n * q_dev * width * columns,
            bytes_accessed=2 * width * columns,
            transcendentals=0,
        ),
        name="projection",
    )(weight, *blocks)


def body(
    queries,
    new_keys,
    new_values,
    cache_keys,
    cache_values,
    keep_tiles,
    tile_count,
    owner_slot,
    out_weight,
):
    ctx_count = lax.axis_size("ctx")
    peers = lax.axis_size("tp")
    low = LOW_SIZE
    high = ctx_count // low

    def move(x, step, flip):
        pairs = [
            (i, (i // low + step) % high * low + (i % low + flip) % low) for i in range(ctx_count)
        ]
        return lax.ppermute(x, "ctx", pairs)

    steps = sorted(range(1, high), key=lambda k: (min(k, high - k), k))
    order = [(k, 0) for k in (0, *steps)] + [(k, 1) for k in (0, *steps)]

    def gather(x, chained):
        held = {(0, 0): x, (0, 1): move(x, 0, 1)}
        for k in steps:
            block = x
            if not chained and 2 * k == high:
                ready = {m: held[m] for m in held if m[0]}
                block, ready = lax.optimization_barrier((block, ready))
                held.update(ready)
            held[k, 0] = move(block, -k, 0)
        behind = None
        for k in steps:
            block = held[k, 0]
            if chained and 2 * k == high and behind is not None:
                block, held[behind] = lax.optimization_barrier((block, held[behind]))
            held[k, 1] = move(block, 0, 1)
            behind = (k, 1)
        return held

    held = gather(queries, False)
    near = [m for m in order[1:] if not m[1] and 2 * m[0] != high]
    middle = [m for m in order[1:] if not m[1] and 2 * m[0] == high]
    flip = [m for m in order if m[1] and m[0] and 2 * m[0] != high]
    late = [m for m in order if m[1] and 2 * m[0] == high] + [(0, 1)]
    groups = [near[i : i + 2] for i in range(0, len(near), 2)]
    groups += [middle + flip[:2]] + [flip[i : i + 2] for i in range(2, len(flip), 2)]
    groups += [late, order[:1]]
    kv_local = new_keys.shape[1] // DH
    small = (owner_slot, keep_tiles[0], tile_count[0], new_keys, new_values)
    token = settle_call(cache_keys, cache_values, new_keys, new_values)

    def attend(members, blocks, turn, values, extra):
        return attention_call(
            members,
            ctx_count,
            kv_local,
            keep_tiles.shape[2],
            turn,
            blocks,
            small,
            cache_keys,
            values,
            extra,
        )

    values = cache_values
    parts, back = {}, {}
    last = None
    for index, members in enumerate(groups):
        blocks = [held[m] for m in members]
        if index == 0:
            blocks, token = lax.optimization_barrier((blocks, token))
        if last is not None:
            blocks, parts[last] = lax.optimization_barrier((blocks, parts[last]))
        if 2 <= index < len(groups) - 1:
            returned = {m: back[m] for m in groups[index - 2] if 2 * m[0] != high}
            blocks, returned = lax.optimization_barrier((blocks, returned))
            back.update(returned)
        extra = [token] if members == groups[-1] else []
        outs = attend(members, blocks, index == 0, values, extra)
        parts.update(zip(members, outs))
        if index == 0:
            values = outs[-1]
        last = members[-1]
        for m in members:
            back[m] = parts[m] if m == (0, 0) else move(parts[m], *m)
    attn = merge_call([back[m] for m in order], kv_local)

    held = gather(attn, True)
    own, send = projection_call(order, ctx_count, [held[m] for m in order], out_weight, peers)
    got = lax.ppermute(send, "tp", [(i, i ^ 1) for i in range(peers)])
    total = own[0] + got[0].astype(jnp.float32)
    for j in range(1, peers // 2):
        piece = (own[j] + got[j].astype(jnp.float32)).astype(jnp.bfloat16)
        piece = lax.ppermute(piece, "tp", [(i, i ^ (2 * j)) for i in range(peers)])
        total = total + piece.astype(jnp.float32)
    return total


def solution(mesh):
    return jax.shard_map(
        body,
        mesh=mesh,
        in_specs=(
            P("ctx", "tp"),
            P("ctx", "tp"),
            P("ctx", "tp"),
            P("ctx", "tp"),
            P("ctx", "tp"),
            P("ctx", "tp", None),
            P("ctx", "tp"),
            P(),
            P("tp", "ctx"),
        ),
        out_specs=P("tp", "ctx"),
        check_vma=False,
    )
```

```python
import functools
import math

import jax
import jax.numpy as jnp
from jax import lax
from jax.experimental import pallas as pl
from jax.experimental.pallas import tpu as pltpu
from jax.sharding import PartitionSpec as P

DH = 128
TILE = 128
LANES = 128
CHUNK = 4
PIECE = 256
LOW = -1e30
LIMIT = 2.0**100
ONES = 16
LOW_SIZE = 2
VMEM_PACK = 58 * 2**20
VMEM_ATTN = 24 * 2**20
VMEM_MERGE = 8 * 2**20
VMEM_PROJ = 16 * 2**20


def flipped(me, count, step, flip):
    high = count // LOW_SIZE
    return lax.rem(me // LOW_SIZE + step, high) * LOW_SIZE + lax.rem(me + flip, LOW_SIZE)


def attention_kernel(
    members, ctx_count, group, kv_local, slots, turn, extra, slot_ref, keep_ref, count_ref, nk_ref, nv_ref, k_ref, v_ref, *rest
):
    blocks = len(members)
    q_refs, rest = rest[:blocks], rest[blocks + extra :]
    out_refs, rest = rest[:blocks], rest[blocks:]
    turned_ref, acc_ref, max_ref = rest[-3:]
    kept_ref = rest[0] if turn else v_ref
    last = kept_ref.shape[2] - TILE
    q_dev = q_refs[0].shape[0]
    heads = kv_local * group
    rows = q_dev * group
    span = CHUNK * TILE
    scale = math.log2(math.e) / math.sqrt(DH)
    me = lax.axis_index("ctx")

    def count_of(g):
        return count_ref[g]

    def slot_of(ctx):
        return slot_ref[ctx]

    ones_tile = jnp.ones((ONES, TILE), jnp.bfloat16)
    place_key = lax.broadcasted_iota(jnp.int32, (TILE, rows), 0)
    place_row = lax.broadcasted_iota(jnp.int32, (TILE, rows), 1) % q_dev
    padding = jnp.zeros((TILE - q_dev, DH), jnp.bfloat16)

    def keys_of(g, chunk):
        cols = slice(g * DH, (g + 1) * DH)
        parts = []
        for i in range(CHUNK):
            slot = chunk * CHUNK + i
            tile = keep_ref[g, jnp.where(slot < count_of(g), slot, 0)]
            parts.append(k_ref[pl.ds(pl.multiple_of(tile * TILE, TILE), TILE), cols])
        return jnp.concatenate(parts, 0)

    def values_of(g, chunk):
        whole = pl.ds(pl.multiple_of(chunk * span, span), span)
        if not turn:
            return kept_ref[g, :, whole]
        cols = slice(g * DH, (g + 1) * DH)
        parts = []
        for i in range(CHUNK):
            slot = chunk * CHUNK + i
            live = slot < count_of(g)
            tile = keep_ref[g, jnp.where(live, slot, 0)]
            at = pl.ds(pl.multiple_of(tile * TILE, TILE), TILE)
            tail = jnp.concatenate([v_ref[at, cols].T, ones_tile], 0)
            parts.append(jnp.where(live, tail, jnp.zeros_like(tail)))
        values = jnp.concatenate(parts, 1)
        kept_ref[g, :, whole] = values
        return values

    def open_head(g):
        cols = slice(g * DH, (g + 1) * DH)
        first = pl.ds(pl.multiple_of(keep_ref[g, 0] * TILE, TILE), TILE)
        keys = jnp.concatenate([nk_ref[:, cols], padding, k_ref[first, cols]], 0)
        for b in range(blocks):
            s = jnp.dot(keys, turned_ref[g, b], preferred_element_type=jnp.float32)
            shift = (slot_of(flipped(me, ctx_count, *members[b])) - slot_of(me)) * q_dev
            live = (place_key < q_dev) & (place_row - place_key + shift >= 0)
            fresh = jnp.where(live, s[:TILE], LOW)
            top = jnp.max(jnp.maximum(fresh, s[TILE:]), axis=0, keepdims=True) * scale
            p = jnp.exp2(fresh * scale - top).astype(jnp.bfloat16)
            max_ref[g, b] = jnp.broadcast_to(top, max_ref.shape[2:])
            acc_ref[g, b] = jnp.dot(
                kept_ref[g, :, last:], p, preferred_element_type=jnp.float32
            )

    for g in range(kv_local):
        if turn:
            fresh_values = nv_ref[:, g * DH : (g + 1) * DH]
            fresh_values = jnp.concatenate([fresh_values, padding], 0).T
            kept_ref[g, :, last:] = jnp.concatenate([fresh_values, ones_tile], 0)
        for b in range(blocks):
            columns = [
                q_refs[b][:, (g * group + h) * DH : (g * group + h + 1) * DH]
                for h in range(group)
            ]
            turned_ref[g, b] = jnp.concatenate(columns, 0).T
        open_head(g)

    def run(kv_heads, chunk):
        loaded = {g: (keys_of(g, chunk), values_of(g, chunk)) for g in kv_heads}
        pieces = [
            (g, b, slice(at, at + PIECE))
            for at in range(0, span, PIECE)
            for b in range(blocks)
            for g in kv_heads
        ]

        def score(g, b, at):
            return jnp.dot(loaded[g][0][at], turned_ref[g, b], preferred_element_type=jnp.float32)

        def add(g, b, at, p):
            acc_ref[g, b] += jnp.dot(loaded[g][1][:, at], p, preferred_element_type=jnp.float32)

        ahead, behind = score(*pieces[0]), None
        for i, piece in enumerate(pieces):
            s = ahead
            if i + 1 < len(pieces):
                ahead = score(*pieces[i + 1])
            p = jnp.exp2(s * scale - max_ref[piece[0], piece[1], :1]).astype(jnp.bfloat16)
            if behind is not None:
                add(*behind)
            behind = (*piece, p)
        add(*behind)

    ends = [(count_of(g) + CHUNK - 1) // CHUNK for g in range(kv_local)]
    shared = functools.reduce(jnp.minimum, ends)

    def step_all(chunk, carry):
        run(range(kv_local), chunk)
        return carry

    lax.fori_loop(0, shared, step_all, 0)
    for g in range(kv_local):

        def step_one(chunk, carry, g=g):
            run([g], chunk)
            return carry

        lax.fori_loop(shared, ends[g], step_one, 0)

    large = jnp.zeros((1, rows), jnp.float32)
    for g in range(kv_local):
        for b in range(blocks):
            fits = acc_ref[g, b, DH : DH + 1, :] < LIMIT
            large = jnp.maximum(large, jnp.where(fits, 0.0, 1.0))

    @pl.when(jnp.max(large) > 0.0)
    def again():
        for g in range(kv_local):
            open_head(g)

            def step_exact(chunk, carry, g=g):
                keys = keys_of(g, chunk)
                values = kept_ref[g, :, pl.ds(pl.multiple_of(chunk * span, span), span)]
                for b in range(blocks):
                    s = jnp.dot(keys, turned_ref[g, b], preferred_element_type=jnp.float32)
                    old = max_ref[g, b, :1]
                    top = jnp.maximum(old, jnp.max(s, axis=0, keepdims=True) * scale)
                    p = jnp.exp2(s * scale - top).astype(jnp.bfloat16)
                    max_ref[g, b] = jnp.broadcast_to(top, max_ref.shape[2:])
                    acc_ref[g, b] = acc_ref[g, b] * jnp.exp2(old - top) + jnp.dot(
                        values, p, preferred_element_type=jnp.float32
                    )
                return carry

            lax.fori_loop(0, ends[g], step_exact, 0)

    sublane = lax.broadcasted_iota(jnp.int32, (q_dev, LANES), 0)
    parts = rows // LANES
    for b in range(blocks):
        stats = jnp.zeros((q_dev, LANES), jnp.float32)
        for g in range(kv_local):
            total = acc_ref[g, b, DH : DH + 1, :]
            mean = (acc_ref[g, b, :DH, :] / total).T.astype(jnp.bfloat16)
            for h in range(group):
                head = g * group + h
                out_refs[b][:, head * DH : (head + 1) * DH] = mean[h * q_dev : (h + 1) * q_dev]
            level = max_ref[g, b, :1] + jnp.log2(total)
            high = level.astype(jnp.bfloat16).astype(jnp.float32)
            middle = (level - high).astype(jnp.bfloat16).astype(jnp.float32)
            for i, term in enumerate((high, middle, level - high - middle)):
                for j in range(parts):
                    at = (g * 3 + i) * parts + j
                    stats = jnp.where(sublane == at, term[:, j * LANES : (j + 1) * LANES], stats)
        out_refs[b][:, heads * DH :] = stats.astype(jnp.bfloat16)


def settle_kernel(k_hbm, v_hbm, nk_hbm, nv_hbm, out_ref):
    out_ref[...] = jnp.zeros_like(out_ref)


def settle_call(*arrays):
    return pl.pallas_call(
        settle_kernel,
        out_shape=jax.ShapeDtypeStruct((8, LANES), jnp.float32),
        in_specs=[pl.BlockSpec(memory_space=pltpu.HBM)] * len(arrays),
        out_specs=pl.BlockSpec(memory_space=pltpu.VMEM),
        compiler_params=pltpu.CompilerParams(vmem_limit_bytes=VMEM_PACK),
        name="settle",
    )(*arrays)


def attention_call(
    members, ctx_count, kv_local, slots, turn, blocks, small, keys, values, extra
):
    n = len(blocks)
    q_dev, width = blocks[0].shape
    group = width // DH // kv_local
    rows = q_dev * group
    smem = pl.BlockSpec(memory_space=pltpu.SMEM)
    vmem = pl.BlockSpec(memory_space=pltpu.VMEM)
    work = n * rows * kv_local * slots * TILE
    kept = -(-slots // CHUNK) * CHUNK + 1
    return pl.pallas_call(
        functools.partial(
            attention_kernel, members, ctx_count, group, kv_local, slots, turn, len(extra)
        ),
        out_shape=[jax.ShapeDtypeStruct((q_dev, width + LANES), jnp.bfloat16)] * n
        + [jax.ShapeDtypeStruct((kv_local, DH + ONES, kept * TILE), jnp.bfloat16)] * turn,
        in_specs=[smem] * 3 + [vmem] * (4 + n + len(extra)),
        out_specs=[vmem] * (n + turn),
        scratch_shapes=[
            pltpu.VMEM((kv_local, n, DH, rows), jnp.bfloat16),
            pltpu.VMEM((kv_local, n, DH + ONES, rows), jnp.float32),
            pltpu.VMEM((kv_local, n, 8, rows), jnp.float32),
        ],
        compiler_params=pltpu.CompilerParams(vmem_limit_bytes=VMEM_ATTN),
        cost_estimate=pl.CostEstimate(
            flops=work * DH * 8, bytes_accessed=8 * 2**20, transcendentals=work
        ),
        name="attention",
    )(*small, keys, values, *blocks, *extra)


def merge_kernel(parts, kv_local, *refs):
    in_refs, out_ref = refs[:parts], refs[parts]
    q_dev, width = out_ref.shape
    group = width // DH // kv_local
    lane_parts = q_dev * group // LANES
    per_part = LANES // q_dev
    stats = [ref[:, width:].astype(jnp.float32) for ref in in_refs]
    sublane = lax.broadcasted_iota(jnp.int32, (LANES, LANES), 0)
    for j in range(lane_parts):
        table = jnp.zeros((LANES, LANES), jnp.float32)
        for g in range(kv_local):
            at = [(g * 3 + i) * lane_parts + j for i in range(3)]
            levels = [stat[at[0]] + stat[at[1]] + stat[at[2]] for stat in stats]
            levels = [level.reshape(1, LANES) for level in levels]
            top = functools.reduce(jnp.maximum, levels)
            shares = [jnp.exp2(level - top) for level in levels]
            total = functools.reduce(jnp.add, shares)
            for c, share in enumerate(shares):
                table = jnp.where(sublane == g * parts + c, share / total, table)
        table = table.T
        for g in range(kv_local):
            for i in range(per_part):
                head = g * group + j * per_part + i
                cols = slice(head * DH, (head + 1) * DH)
                share = table[i * q_dev : (i + 1) * q_dev]
                mixed = functools.reduce(
                    jnp.add,
                    [
                        share[:, g * parts + c : g * parts + c + 1]
                        * in_refs[c][:, cols].astype(jnp.float32)
                        for c in range(parts)
                    ],
                )
                out_ref[:, cols] = mixed.astype(jnp.bfloat16)


def merge_call(parts, kv_local):
    q_dev, wide = parts[0].shape
    vmem = pl.BlockSpec(memory_space=pltpu.VMEM)
    return pl.pallas_call(
        functools.partial(merge_kernel, len(parts), kv_local),
        out_shape=jax.ShapeDtypeStruct((q_dev, wide - LANES), jnp.bfloat16),
        in_specs=[vmem] * len(parts),
        out_specs=vmem,
        compiler_params=pltpu.CompilerParams(vmem_limit_bytes=VMEM_MERGE),
        cost_estimate=pl.CostEstimate(
            flops=len(parts) * q_dev * wide * 2,
            bytes_accessed=len(parts) * q_dev * wide * 2,
            transcendentals=0,
        ),
        name="merge",
    )(*parts)


def projection_kernel(members, ctx_count, peers, w_ref, *rest):
    blocks = len(members)
    in_refs, rest = rest[:blocks], rest[blocks:]
    own_ref, send_ref, rows_ref, sum_ref = rest
    q_dev = in_refs[0].shape[0]
    me = lax.axis_index("ctx")
    for member, ref in zip(members, in_refs):
        at = flipped(me, ctx_count, *member) * q_dev
        rows_ref[pl.ds(pl.multiple_of(at, q_dev), q_dev), :] = ref[...]
    steps, part = own_ref.shape[:2]
    my_tp = lax.axis_index("tp")
    sum_ref[...] = jnp.dot(rows_ref[...], w_ref[...], preferred_element_type=jnp.float32)

    def piece(peer):
        return sum_ref[pl.ds(pl.multiple_of(peer * part, part), part), :]

    for j in range(steps):
        own_ref[j] = piece(my_tp ^ (2 * j))
        send_ref[j] = piece(my_tp ^ (2 * j + 1)).astype(jnp.bfloat16)


def projection_call(members, ctx_count, blocks, weight, peers):
    n = len(blocks)
    q_dev, width = blocks[0].shape
    columns = weight.shape[1]
    part = n * q_dev // peers
    vmem = pl.BlockSpec(memory_space=pltpu.VMEM)
    return pl.pallas_call(
        functools.partial(projection_kernel, members, ctx_count, peers),
        out_shape=[
            jax.ShapeDtypeStruct((peers // 2, part, columns), jnp.float32),
            jax.ShapeDtypeStruct((peers // 2, part, columns), jnp.bfloat16),
        ],
        in_specs=[vmem] * (1 + n),
        out_specs=[vmem] * 2,
        scratch_shapes=[
            pltpu.VMEM((n * q_dev, width), jnp.bfloat16),
            pltpu.VMEM((n * q_dev, columns), jnp.float32),
        ],
        compiler_params=pltpu.CompilerParams(vmem_limit_bytes=VMEM_PROJ),
        cost_estimate=pl.CostEstimate(
            flops=2 * n * q_dev * width * columns,
            bytes_accessed=2 * width * columns,
            transcendentals=0,
        ),
        name="projection",
    )(weight, *blocks)


def body(
    queries,
    new_keys,
    new_values,
    cache_keys,
    cache_values,
    keep_tiles,
    tile_count,
    owner_slot,
    out_weight,
):
    ctx_count = lax.axis_size("ctx")
    peers = lax.axis_size("tp")
    low = LOW_SIZE
    high = ctx_count // low

    def move(x, step, flip):
        pairs = [
            (i, (i // low + step) % high * low + (i % low + flip) % low) for i in range(ctx_count)
        ]
        return lax.ppermute(x, "ctx", pairs)

    steps = sorted(range(1, high), key=lambda k: (min(k, high - k), k))
    order = [(k, 0) for k in (0, *steps)] + [(k, 1) for k in (0, *steps)]

    def gather(x, chained):
        held = {(0, 0): x, (0, 1): move(x, 0, 1)}
        for k in steps:
            block = x
            if not chained and 2 * k == high:
                ready = {m: held[m] for m in held if m[0]}
                block, ready = lax.optimization_barrier((block, ready))
                held.update(ready)
            held[k, 0] = move(block, -k, 0)
        behind = None
        for k in steps:
            block = held[k, 0]
            if chained and 2 * k == high and behind is not None:
                block, held[behind] = lax.optimization_barrier((block, held[behind]))
            held[k, 1] = move(block, 0, 1)
            behind = (k, 1)
        return held

    held = gather(queries, False)
    near = [m for m in order[1:] if not m[1] and 2 * m[0] != high]
    middle = [m for m in order[1:] if not m[1] and 2 * m[0] == high]
    flip = [m for m in order if m[1] and m[0] and 2 * m[0] != high]
    late = [m for m in order if m[1] and 2 * m[0] == high] + [(0, 1)]
    groups = [near[i : i + 2] for i in range(0, len(near), 2)]
    groups += [middle + flip[:2]] + [flip[i : i + 2] for i in range(2, len(flip), 2)]
    groups += [late, order[:1]]
    kv_local = new_keys.shape[1] // DH
    small = (owner_slot, keep_tiles[0], tile_count[0], new_keys, new_values)
    token = settle_call(cache_keys, cache_values, new_keys, new_values)

    def attend(members, blocks, turn, values, extra):
        return attention_call(
            members,
            ctx_count,
            kv_local,
            keep_tiles.shape[2],
            turn,
            blocks,
            small,
            cache_keys,
            values,
            extra,
        )

    values = cache_values
    parts, back = {}, {}
    last = None
    for index, members in enumerate(groups):
        blocks = [held[m] for m in members]
        if index == 0:
            blocks, token = lax.optimization_barrier((blocks, token))
        if last is not None:
            blocks, parts[last] = lax.optimization_barrier((blocks, parts[last]))
        if 2 <= index < len(groups) - 1:
            returned = {m: back[m] for m in groups[index - 2] if 2 * m[0] != high}
            blocks, returned = lax.optimization_barrier((blocks, returned))
            back.update(returned)
        extra = [token] if members == groups[-1] else []
        outs = attend(members, blocks, index == 0, values, extra)
        parts.update(zip(members, outs))
        if index == 0:
            values = outs[-1]
        last = members[-1]
        for m in members:
            back[m] = parts[m] if m == (0, 0) else move(parts[m], *m)
    attn = merge_call([back[m] for m in order], kv_local)

    held = gather(attn, True)
    own, send = projection_call(order, ctx_count, [held[m] for m in order], out_weight, peers)
    got = lax.ppermute(send, "tp", [(i, i ^ 1) for i in range(peers)])
    total = own[0] + got[0].astype(jnp.float32)
    for j in range(1, peers // 2):
        piece = (own[j] + got[j].astype(jnp.float32)).astype(jnp.bfloat16)
        piece = lax.ppermute(piece, "tp", [(i, i ^ (2 * j)) for i in range(peers)])
        total = total + piece.astype(jnp.float32)
    return total


def solution(mesh):
    return jax.shard_map(
        body,
        mesh=mesh,
        in_specs=(
            P("ctx", "tp"),
            P("ctx", "tp"),
            P("ctx", "tp"),
            P("ctx", "tp"),
            P("ctx", "tp"),
            P("ctx", "tp", None),
            P("ctx", "tp"),
            P(),
            P("tp", "ctx"),
        ),
        out_specs=P("tp", "ctx"),
        check_vma=False,
    )
```

```python
import functools
import math

import jax
import jax.numpy as jnp
from jax import lax
from jax.experimental import pallas as pl
from jax.experimental.pallas import tpu as pltpu
from jax.sharding import PartitionSpec as P

DH = 128
TILE = 128
LANES = 128
CHUNK = 6
LOW = -1e30
LIMIT = 2.0**100
ONES = 16
LOW_SIZE = 2
VMEM_PACK = 58 * 2**20
VMEM_ATTN = 24 * 2**20
VMEM_MERGE = 8 * 2**20
VMEM_PROJ = 16 * 2**20


def flipped(me, count, step, flip):
    high = count // LOW_SIZE
    return lax.rem(me // LOW_SIZE + step, high) * LOW_SIZE + lax.rem(me + flip, LOW_SIZE)


def attention_kernel(
    members, ctx_count, group, kv_local, slots, turn, extra, slot_ref, keep_ref, count_ref, nk_ref, nv_ref, k_ref, v_ref, *rest
):
    blocks = len(members)
    q_refs, rest = rest[:blocks], rest[blocks + extra :]
    out_refs, rest = rest[:blocks], rest[blocks:]
    turned_ref, acc_ref, max_ref = rest[-3:]
    kept_ref = rest[0] if turn else v_ref
    last = kept_ref.shape[2] - TILE
    q_dev = q_refs[0].shape[0]
    heads = kv_local * group
    rows = q_dev * group
    span = CHUNK * TILE
    scale = math.log2(math.e) / math.sqrt(DH)
    me = lax.axis_index("ctx")

    def count_of(g):
        return count_ref[g]

    def slot_of(ctx):
        return slot_ref[ctx]

    ones_tile = jnp.ones((ONES, TILE), jnp.bfloat16)
    place_key = lax.broadcasted_iota(jnp.int32, (TILE, rows), 0)
    place_row = lax.broadcasted_iota(jnp.int32, (TILE, rows), 1) % q_dev
    padding = jnp.zeros((TILE - q_dev, DH), jnp.bfloat16)

    def keys_of(g, chunk):
        cols = slice(g * DH, (g + 1) * DH)
        parts = []
        for i in range(CHUNK):
            slot = chunk * CHUNK + i
            tile = keep_ref[g, jnp.where(slot < count_of(g), slot, 0)]
            parts.append(k_ref[pl.ds(pl.multiple_of(tile * TILE, TILE), TILE), cols])
        return jnp.concatenate(parts, 0)

    def values_of(g, chunk):
        whole = pl.ds(pl.multiple_of(chunk * span, span), span)
        if not turn:
            return kept_ref[g, :, whole]
        cols = slice(g * DH, (g + 1) * DH)
        parts = []
        for i in range(CHUNK):
            slot = chunk * CHUNK + i
            live = slot < count_of(g)
            tile = keep_ref[g, jnp.where(live, slot, 0)]
            at = pl.ds(pl.multiple_of(tile * TILE, TILE), TILE)
            tail = jnp.concatenate([v_ref[at, cols].T, ones_tile], 0)
            parts.append(jnp.where(live, tail, jnp.zeros_like(tail)))
        values = jnp.concatenate(parts, 1)
        kept_ref[g, :, whole] = values
        return values

    def open_head(g):
        cols = slice(g * DH, (g + 1) * DH)
        first = pl.ds(pl.multiple_of(keep_ref[g, 0] * TILE, TILE), TILE)
        keys = jnp.concatenate([nk_ref[:, cols], padding, k_ref[first, cols]], 0)
        for b in range(blocks):
            s = jnp.dot(keys, turned_ref[g, b], preferred_element_type=jnp.float32)
            shift = (slot_of(flipped(me, ctx_count, *members[b])) - slot_of(me)) * q_dev
            live = (place_key < q_dev) & (place_row - place_key + shift >= 0)
            fresh = jnp.where(live, s[:TILE], LOW)
            top = jnp.max(jnp.maximum(fresh, s[TILE:]), axis=0, keepdims=True) * scale
            p = jnp.exp2(fresh * scale - top).astype(jnp.bfloat16)
            max_ref[g, b] = jnp.broadcast_to(top, max_ref.shape[2:])
            acc_ref[g, b] = jnp.dot(
                kept_ref[g, :, last:], p, preferred_element_type=jnp.float32
            )

    for g in range(kv_local):
        if turn:
            fresh_values = nv_ref[:, g * DH : (g + 1) * DH]
            fresh_values = jnp.concatenate([fresh_values, padding], 0).T
            kept_ref[g, :, last:] = jnp.concatenate([fresh_values, ones_tile], 0)
        for b in range(blocks):
            columns = [
                q_refs[b][:, (g * group + h) * DH : (g * group + h + 1) * DH]
                for h in range(group)
            ]
            turned_ref[g, b] = jnp.concatenate(columns, 0).T
        open_head(g)

    def run(kv_heads, chunk):
        loaded = {g: (keys_of(g, chunk), values_of(g, chunk)) for g in kv_heads}
        chains = [(g, b) for b in range(blocks) for g in kv_heads]

        def score(g, b):
            return jnp.dot(loaded[g][0], turned_ref[g, b], preferred_element_type=jnp.float32)

        ahead = score(*chains[0])
        for at, (g, b) in enumerate(chains):
            s = ahead
            if at + 1 < len(chains):
                ahead = score(*chains[at + 1])
            p = jnp.exp2(s * scale - max_ref[g, b, :1]).astype(jnp.bfloat16)
            acc_ref[g, b] += jnp.dot(loaded[g][1], p, preferred_element_type=jnp.float32)

    ends = [(count_of(g) + CHUNK - 1) // CHUNK for g in range(kv_local)]
    shared = functools.reduce(jnp.minimum, ends)

    def step_all(chunk, carry):
        run(range(kv_local), chunk)
        return carry

    lax.fori_loop(0, shared, step_all, 0)
    for g in range(kv_local):

        def step_one(chunk, carry, g=g):
            run([g], chunk)
            return carry

        lax.fori_loop(shared, ends[g], step_one, 0)

    large = jnp.zeros((1, rows), jnp.float32)
    for g in range(kv_local):
        for b in range(blocks):
            fits = acc_ref[g, b, DH : DH + 1, :] < LIMIT
            large = jnp.maximum(large, jnp.where(fits, 0.0, 1.0))

    @pl.when(jnp.max(large) > 0.0)
    def again():
        for g in range(kv_local):
            open_head(g)

            def step_exact(chunk, carry, g=g):
                keys = keys_of(g, chunk)
                values = kept_ref[g, :, pl.ds(pl.multiple_of(chunk * span, span), span)]
                for b in range(blocks):
                    s = jnp.dot(keys, turned_ref[g, b], preferred_element_type=jnp.float32)
                    old = max_ref[g, b, :1]
                    top = jnp.maximum(old, jnp.max(s, axis=0, keepdims=True) * scale)
                    p = jnp.exp2(s * scale - top).astype(jnp.bfloat16)
                    max_ref[g, b] = jnp.broadcast_to(top, max_ref.shape[2:])
                    acc_ref[g, b] = acc_ref[g, b] * jnp.exp2(old - top) + jnp.dot(
                        values, p, preferred_element_type=jnp.float32
                    )
                return carry

            lax.fori_loop(0, ends[g], step_exact, 0)

    sublane = lax.broadcasted_iota(jnp.int32, (q_dev, LANES), 0)
    parts = rows // LANES
    for b in range(blocks):
        stats = jnp.zeros((q_dev, LANES), jnp.float32)
        for g in range(kv_local):
            total = acc_ref[g, b, DH : DH + 1, :]
            mean = (acc_ref[g, b, :DH, :] / total).T.astype(jnp.bfloat16)
            for h in range(group):
                head = g * group + h
                out_refs[b][:, head * DH : (head + 1) * DH] = mean[h * q_dev : (h + 1) * q_dev]
            level = max_ref[g, b, :1] + jnp.log2(total)
            high = level.astype(jnp.bfloat16).astype(jnp.float32)
            middle = (level - high).astype(jnp.bfloat16).astype(jnp.float32)
            for i, term in enumerate((high, middle, level - high - middle)):
                for j in range(parts):
                    at = (g * 3 + i) * parts + j
                    stats = jnp.where(sublane == at, term[:, j * LANES : (j + 1) * LANES], stats)
        out_refs[b][:, heads * DH :] = stats.astype(jnp.bfloat16)


def settle_kernel(k_hbm, v_hbm, nk_hbm, nv_hbm, out_ref):
    out_ref[...] = jnp.zeros_like(out_ref)


def settle_call(*arrays):
    return pl.pallas_call(
        settle_kernel,
        out_shape=jax.ShapeDtypeStruct((8, LANES), jnp.float32),
        in_specs=[pl.BlockSpec(memory_space=pltpu.HBM)] * len(arrays),
        out_specs=pl.BlockSpec(memory_space=pltpu.VMEM),
        compiler_params=pltpu.CompilerParams(vmem_limit_bytes=VMEM_PACK),
        name="settle",
    )(*arrays)


def attention_call(
    members, ctx_count, kv_local, slots, turn, blocks, small, keys, values, extra
):
    n = len(blocks)
    q_dev, width = blocks[0].shape
    group = width // DH // kv_local
    rows = q_dev * group
    smem = pl.BlockSpec(memory_space=pltpu.SMEM)
    vmem = pl.BlockSpec(memory_space=pltpu.VMEM)
    work = n * rows * kv_local * slots * TILE
    kept = -(-slots // CHUNK) * CHUNK + 1
    return pl.pallas_call(
        functools.partial(
            attention_kernel, members, ctx_count, group, kv_local, slots, turn, len(extra)
        ),
        out_shape=[jax.ShapeDtypeStruct((q_dev, width + LANES), jnp.bfloat16)] * n
        + [jax.ShapeDtypeStruct((kv_local, DH + ONES, kept * TILE), jnp.bfloat16)] * turn,
        in_specs=[smem] * 3 + [vmem] * (4 + n + len(extra)),
        out_specs=[vmem] * (n + turn),
        scratch_shapes=[
            pltpu.VMEM((kv_local, n, DH, rows), jnp.bfloat16),
            pltpu.VMEM((kv_local, n, DH + ONES, rows), jnp.float32),
            pltpu.VMEM((kv_local, n, 8, rows), jnp.float32),
        ],
        compiler_params=pltpu.CompilerParams(vmem_limit_bytes=VMEM_ATTN),
        cost_estimate=pl.CostEstimate(
            flops=work * DH * 8, bytes_accessed=8 * 2**20, transcendentals=work
        ),
        name="attention",
    )(*small, keys, values, *blocks, *extra)


def merge_kernel(parts, kv_local, *refs):
    in_refs, out_ref = refs[:parts], refs[parts]
    q_dev, width = out_ref.shape
    group = width // DH // kv_local
    lane_parts = q_dev * group // LANES
    per_part = LANES // q_dev
    stats = [ref[:, width:].astype(jnp.float32) for ref in in_refs]
    sublane = lax.broadcasted_iota(jnp.int32, (LANES, LANES), 0)
    for j in range(lane_parts):
        table = jnp.zeros((LANES, LANES), jnp.float32)
        for g in range(kv_local):
            at = [(g * 3 + i) * lane_parts + j for i in range(3)]
            levels = [stat[at[0]] + stat[at[1]] + stat[at[2]] for stat in stats]
            levels = [level.reshape(1, LANES) for level in levels]
            top = functools.reduce(jnp.maximum, levels)
            shares = [jnp.exp2(level - top) for level in levels]
            total = functools.reduce(jnp.add, shares)
            for c, share in enumerate(shares):
                table = jnp.where(sublane == g * parts + c, share / total, table)
        table = table.T
        for g in range(kv_local):
            for i in range(per_part):
                head = g * group + j * per_part + i
                cols = slice(head * DH, (head + 1) * DH)
                share = table[i * q_dev : (i + 1) * q_dev]
                mixed = functools.reduce(
                    jnp.add,
                    [
                        share[:, g * parts + c : g * parts + c + 1]
                        * in_refs[c][:, cols].astype(jnp.float32)
                        for c in range(parts)
                    ],
                )
                out_ref[:, cols] = mixed.astype(jnp.bfloat16)


def merge_call(parts, kv_local):
    q_dev, wide = parts[0].shape
    vmem = pl.BlockSpec(memory_space=pltpu.VMEM)
    return pl.pallas_call(
        functools.partial(merge_kernel, len(parts), kv_local),
        out_shape=jax.ShapeDtypeStruct((q_dev, wide - LANES), jnp.bfloat16),
        in_specs=[vmem] * len(parts),
        out_specs=vmem,
        compiler_params=pltpu.CompilerParams(vmem_limit_bytes=VMEM_MERGE),
        cost_estimate=pl.CostEstimate(
            flops=len(parts) * q_dev * wide * 2,
            bytes_accessed=len(parts) * q_dev * wide * 2,
            transcendentals=0,
        ),
        name="merge",
    )(*parts)


def projection_kernel(members, ctx_count, peers, w_ref, *rest):
    blocks = len(members)
    in_refs, rest = rest[:blocks], rest[blocks:]
    own_ref, send_ref, rows_ref, sum_ref = rest
    q_dev = in_refs[0].shape[0]
    me = lax.axis_index("ctx")
    for member, ref in zip(members, in_refs):
        at = flipped(me, ctx_count, *member) * q_dev
        rows_ref[pl.ds(pl.multiple_of(at, q_dev), q_dev), :] = ref[...]
    steps, part = own_ref.shape[:2]
    my_tp = lax.axis_index("tp")
    sum_ref[...] = jnp.dot(rows_ref[...], w_ref[...], preferred_element_type=jnp.float32)

    def piece(peer):
        return sum_ref[pl.ds(pl.multiple_of(peer * part, part), part), :]

    for j in range(steps):
        own_ref[j] = piece(my_tp ^ (2 * j))
        send_ref[j] = piece(my_tp ^ (2 * j + 1)).astype(jnp.bfloat16)


def projection_call(members, ctx_count, blocks, weight, peers):
    n = len(blocks)
    q_dev, width = blocks[0].shape
    columns = weight.shape[1]
    part = n * q_dev // peers
    vmem = pl.BlockSpec(memory_space=pltpu.VMEM)
    return pl.pallas_call(
        functools.partial(projection_kernel, members, ctx_count, peers),
        out_shape=[
            jax.ShapeDtypeStruct((peers // 2, part, columns), jnp.float32),
            jax.ShapeDtypeStruct((peers // 2, part, columns), jnp.bfloat16),
        ],
        in_specs=[vmem] * (1 + n),
        out_specs=[vmem] * 2,
        scratch_shapes=[
            pltpu.VMEM((n * q_dev, width), jnp.bfloat16),
            pltpu.VMEM((n * q_dev, columns), jnp.float32),
        ],
        compiler_params=pltpu.CompilerParams(vmem_limit_bytes=VMEM_PROJ),
        cost_estimate=pl.CostEstimate(
            flops=2 * n * q_dev * width * columns,
            bytes_accessed=2 * width * columns,
            transcendentals=0,
        ),
        name="projection",
    )(weight, *blocks)


def body(
    queries,
    new_keys,
    new_values,
    cache_keys,
    cache_values,
    keep_tiles,
    tile_count,
    owner_slot,
    out_weight,
):
    ctx_count = lax.axis_size("ctx")
    peers = lax.axis_size("tp")
    low = LOW_SIZE
    high = ctx_count // low

    def move(x, step, flip):
        pairs = [
            (i, (i // low + step) % high * low + (i % low + flip) % low) for i in range(ctx_count)
        ]
        return lax.ppermute(x, "ctx", pairs)

    steps = sorted(range(1, high), key=lambda k: (min(k, high - k), k))
    order = [(k, 0) for k in (0, *steps)] + [(k, 1) for k in (0, *steps)]

    def gather(x, chained):
        held = {(0, 0): x, (0, 1): move(x, 0, 1)}
        for k in steps:
            block = x
            if not chained and 2 * k == high:
                ready = {m: held[m] for m in held if m[0]}
                block, ready = lax.optimization_barrier((block, ready))
                held.update(ready)
            held[k, 0] = move(block, -k, 0)
        behind = None
        for k in steps:
            block = held[k, 0]
            if chained and 2 * k == high and behind is not None:
                block, held[behind] = lax.optimization_barrier((block, held[behind]))
            held[k, 1] = move(block, 0, 1)
            behind = (k, 1)
        return held

    held = gather(queries, False)
    near = [m for m in order[1:] if not m[1] and 2 * m[0] != high]
    middle = [m for m in order[1:] if not m[1] and 2 * m[0] == high]
    flip = [m for m in order if m[1] and m[0] and 2 * m[0] != high]
    late = [m for m in order if m[1] and 2 * m[0] == high] + [(0, 1)]
    groups = [near[i : i + 2] for i in range(0, len(near), 2)]
    groups += [middle + flip[:2]] + [flip[i : i + 2] for i in range(2, len(flip), 2)]
    groups += [late, order[:1]]
    kv_local = new_keys.shape[1] // DH
    small = (owner_slot, keep_tiles[0], tile_count[0], new_keys, new_values)
    token = settle_call(cache_keys, cache_values, new_keys, new_values)

    def attend(members, blocks, turn, values, extra):
        return attention_call(
            members,
            ctx_count,
            kv_local,
            keep_tiles.shape[2],
            turn,
            blocks,
            small,
            cache_keys,
            values,
            extra,
        )

    values = cache_values
    parts, back = {}, {}
    last = None
    for index, members in enumerate(groups):
        blocks = [held[m] for m in members]
        if index == 0:
            blocks, token = lax.optimization_barrier((blocks, token))
        if last is not None:
            blocks, parts[last] = lax.optimization_barrier((blocks, parts[last]))
        if 2 <= index < len(groups) - 1:
            returned = {m: back[m] for m in groups[index - 2] if 2 * m[0] != high}
            blocks, returned = lax.optimization_barrier((blocks, returned))
            back.update(returned)
        extra = [token] if members == groups[-1] else []
        outs = attend(members, blocks, index == 0, values, extra)
        parts.update(zip(members, outs))
        if index == 0:
            values = outs[-1]
        last = members[-1]
        for m in members:
            back[m] = parts[m] if m == (0, 0) else move(parts[m], *m)
    attn = merge_call([back[m] for m in order], kv_local)

    held = gather(attn, True)
    own, send = projection_call(order, ctx_count, [held[m] for m in order], out_weight, peers)
    got = lax.ppermute(send, "tp", [(i, i ^ 1) for i in range(peers)])
    total = own[0] + got[0].astype(jnp.float32)
    for j in range(1, peers // 2):
        piece = (own[j] + got[j].astype(jnp.float32)).astype(jnp.bfloat16)
        piece = lax.ppermute(piece, "tp", [(i, i ^ (2 * j)) for i in range(peers)])
        total = total + piece.astype(jnp.float32)
    return total


def solution(mesh):
    return jax.shard_map(
        body,
        mesh=mesh,
        in_specs=(
            P("ctx", "tp"),
            P("ctx", "tp"),
            P("ctx", "tp"),
            P("ctx", "tp"),
            P("ctx", "tp"),
            P("ctx", "tp", None),
            P("ctx", "tp"),
            P(),
            P("tp", "ctx"),
        ),
        out_specs=P("tp", "ctx"),
        check_vma=False,
    )
```

```python
import functools
import math

import jax
import jax.numpy as jnp
from jax import lax
from jax.experimental import pallas as pl
from jax.experimental.pallas import tpu as pltpu
from jax.sharding import PartitionSpec as P

DH = 128
TILE = 128
LANES = 128
CHUNK = 6
LOW = -1e30
LIMIT = 2.0**100
ONES = 16
LOW_SIZE = 2
VMEM_PACK = 58 * 2**20
VMEM_ATTN = 24 * 2**20
VMEM_MERGE = 8 * 2**20
VMEM_PROJ = 16 * 2**20


def flipped(me, count, step, flip):
    high = count // LOW_SIZE
    return lax.rem(me // LOW_SIZE + step, high) * LOW_SIZE + lax.rem(me + flip, LOW_SIZE)


def attention_kernel(
    members, ctx_count, group, kv_local, slots, turn, extra, slot_ref, keep_ref, count_ref, nk_ref, nv_ref, k_ref, v_ref, *rest
):
    blocks = len(members)
    q_refs, rest = rest[:blocks], rest[blocks + extra :]
    out_refs, rest = rest[:blocks], rest[blocks:]
    turned_ref, acc_ref, max_ref = rest[-3:]
    kept_ref = rest[0] if turn else v_ref
    last = kept_ref.shape[2] - TILE
    q_dev = q_refs[0].shape[0]
    heads = kv_local * group
    rows = q_dev * group
    span = CHUNK * TILE
    scale = math.log2(math.e) / math.sqrt(DH)
    me = lax.axis_index("ctx")

    def count_of(g):
        return count_ref[g]

    def slot_of(ctx):
        return slot_ref[ctx]

    ones_tile = jnp.ones((ONES, TILE), jnp.bfloat16)
    place_key = lax.broadcasted_iota(jnp.int32, (TILE, rows), 0)
    place_row = lax.broadcasted_iota(jnp.int32, (TILE, rows), 1) % q_dev
    padding = jnp.zeros((TILE - q_dev, DH), jnp.bfloat16)

    def keys_of(g, chunk):
        cols = slice(g * DH, (g + 1) * DH)
        parts = []
        for i in range(CHUNK):
            slot = chunk * CHUNK + i
            tile = keep_ref[g, jnp.where(slot < count_of(g), slot, 0)]
            parts.append(k_ref[pl.ds(pl.multiple_of(tile * TILE, TILE), TILE), cols])
        return jnp.concatenate(parts, 0)

    def values_of(g, chunk):
        whole = pl.ds(pl.multiple_of(chunk * span, span), span)
        if not turn:
            return kept_ref[g, :, whole]
        cols = slice(g * DH, (g + 1) * DH)
        parts = []
        for i in range(CHUNK):
            slot = chunk * CHUNK + i
            live = slot < count_of(g)
            tile = keep_ref[g, jnp.where(live, slot, 0)]
            at = pl.ds(pl.multiple_of(tile * TILE, TILE), TILE)
            tail = jnp.concatenate([v_ref[at, cols].T, ones_tile], 0)
            parts.append(jnp.where(live, tail, jnp.zeros_like(tail)))
        values = jnp.concatenate(parts, 1)
        kept_ref[g, :, whole] = values
        return values

    def open_head(g):
        cols = slice(g * DH, (g + 1) * DH)
        first = pl.ds(pl.multiple_of(keep_ref[g, 0] * TILE, TILE), TILE)
        keys = jnp.concatenate([nk_ref[:, cols], padding, k_ref[first, cols]], 0)
        for b in range(blocks):
            s = jnp.dot(keys, turned_ref[g, b], preferred_element_type=jnp.float32)
            shift = (slot_of(flipped(me, ctx_count, *members[b])) - slot_of(me)) * q_dev
            live = (place_key < q_dev) & (place_row - place_key + shift >= 0)
            fresh = jnp.where(live, s[:TILE], LOW)
            top = jnp.max(jnp.maximum(fresh, s[TILE:]), axis=0, keepdims=True) * scale
            p = jnp.exp2(fresh * scale - top).astype(jnp.bfloat16)
            max_ref[g, b] = jnp.broadcast_to(top, max_ref.shape[2:])
            acc_ref[g, b] = jnp.dot(
                kept_ref[g, :, last:], p, preferred_element_type=jnp.float32
            )

    for g in range(kv_local):
        if turn:
            fresh_values = nv_ref[:, g * DH : (g + 1) * DH]
            fresh_values = jnp.concatenate([fresh_values, padding], 0).T
            kept_ref[g, :, last:] = jnp.concatenate([fresh_values, ones_tile], 0)
        for b in range(blocks):
            columns = [
                q_refs[b][:, (g * group + h) * DH : (g * group + h + 1) * DH]
                for h in range(group)
            ]
            turned_ref[g, b] = jnp.concatenate(columns, 0).T
        open_head(g)

    def run(kv_heads, chunk):
        loaded = {g: (keys_of(g, chunk), values_of(g, chunk)) for g in kv_heads}
        chains = [(g, b) for b in range(blocks) for g in kv_heads]

        def score(g, b):
            return jnp.dot(loaded[g][0], turned_ref[g, b], preferred_element_type=jnp.float32)

        ahead = score(*chains[0])
        for at, (g, b) in enumerate(chains):
            s = ahead
            if at + 1 < len(chains):
                ahead = score(*chains[at + 1])
            p = jnp.exp2(s * scale - max_ref[g, b, :1]).astype(jnp.bfloat16)
            acc_ref[g, b] += jnp.dot(loaded[g][1], p, preferred_element_type=jnp.float32)

    ends = [(count_of(g) + CHUNK - 1) // CHUNK for g in range(kv_local)]
    shared = functools.reduce(jnp.minimum, ends)

    def step_all(chunk, carry):
        run(range(kv_local), chunk)
        return carry

    lax.fori_loop(0, shared, step_all, 0)
    for g in range(kv_local):

        def step_one(chunk, carry, g=g):
            run([g], chunk)
            return carry

        lax.fori_loop(shared, ends[g], step_one, 0)

    large = jnp.zeros((1, rows), jnp.float32)
    for g in range(kv_local):
        for b in range(blocks):
            fits = acc_ref[g, b, DH : DH + 1, :] < LIMIT
            large = jnp.maximum(large, jnp.where(fits, 0.0, 1.0))

    @pl.when(jnp.max(large) > 0.0)
    def again():
        for g in range(kv_local):
            open_head(g)

            def step_exact(chunk, carry, g=g):
                keys = keys_of(g, chunk)
                values = kept_ref[g, :, pl.ds(pl.multiple_of(chunk * span, span), span)]
                for b in range(blocks):
                    s = jnp.dot(keys, turned_ref[g, b], preferred_element_type=jnp.float32)
                    old = max_ref[g, b, :1]
                    top = jnp.maximum(old, jnp.max(s, axis=0, keepdims=True) * scale)
                    p = jnp.exp2(s * scale - top).astype(jnp.bfloat16)
                    max_ref[g, b] = jnp.broadcast_to(top, max_ref.shape[2:])
                    acc_ref[g, b] = acc_ref[g, b] * jnp.exp2(old - top) + jnp.dot(
                        values, p, preferred_element_type=jnp.float32
                    )
                return carry

            lax.fori_loop(0, ends[g], step_exact, 0)

    sublane = lax.broadcasted_iota(jnp.int32, (q_dev, LANES), 0)
    parts = rows // LANES
    for b in range(blocks):
        stats = jnp.zeros((q_dev, LANES), jnp.float32)
        for g in range(kv_local):
            total = acc_ref[g, b, DH : DH + 1, :]
            mean = (acc_ref[g, b, :DH, :] / total).T.astype(jnp.bfloat16)
            for h in range(group):
                head = g * group + h
                out_refs[b][:, head * DH : (head + 1) * DH] = mean[h * q_dev : (h + 1) * q_dev]
            level = max_ref[g, b, :1] + jnp.log2(total)
            high = level.astype(jnp.bfloat16).astype(jnp.float32)
            middle = (level - high).astype(jnp.bfloat16).astype(jnp.float32)
            for i, term in enumerate((high, middle, level - high - middle)):
                for j in range(parts):
                    at = (g * 3 + i) * parts + j
                    stats = jnp.where(sublane == at, term[:, j * LANES : (j + 1) * LANES], stats)
        out_refs[b][:, heads * DH :] = stats.astype(jnp.bfloat16)


def settle_kernel(k_hbm, v_hbm, nk_hbm, nv_hbm, out_ref):
    out_ref[...] = jnp.zeros_like(out_ref)


def settle_call(*arrays):
    return pl.pallas_call(
        settle_kernel,
        out_shape=jax.ShapeDtypeStruct((8, LANES), jnp.float32),
        in_specs=[pl.BlockSpec(memory_space=pltpu.HBM)] * len(arrays),
        out_specs=pl.BlockSpec(memory_space=pltpu.VMEM),
        compiler_params=pltpu.CompilerParams(vmem_limit_bytes=VMEM_PACK),
        name="settle",
    )(*arrays)


def attention_call(
    members, ctx_count, kv_local, slots, turn, blocks, small, keys, values, extra
):
    n = len(blocks)
    q_dev, width = blocks[0].shape
    group = width // DH // kv_local
    rows = q_dev * group
    smem = pl.BlockSpec(memory_space=pltpu.SMEM)
    vmem = pl.BlockSpec(memory_space=pltpu.VMEM)
    work = n * rows * kv_local * slots * TILE
    kept = -(-slots // CHUNK) * CHUNK + 1
    return pl.pallas_call(
        functools.partial(
            attention_kernel, members, ctx_count, group, kv_local, slots, turn, len(extra)
        ),
        out_shape=[jax.ShapeDtypeStruct((q_dev, width + LANES), jnp.bfloat16)] * n
        + [jax.ShapeDtypeStruct((kv_local, DH + ONES, kept * TILE), jnp.bfloat16)] * turn,
        in_specs=[smem] * 3 + [vmem] * (4 + n + len(extra)),
        out_specs=[vmem] * (n + turn),
        scratch_shapes=[
            pltpu.VMEM((kv_local, n, DH, rows), jnp.bfloat16),
            pltpu.VMEM((kv_local, n, DH + ONES, rows), jnp.float32),
            pltpu.VMEM((kv_local, n, 8, rows), jnp.float32),
        ],
        compiler_params=pltpu.CompilerParams(vmem_limit_bytes=VMEM_ATTN),
        cost_estimate=pl.CostEstimate(
            flops=work * DH * 8, bytes_accessed=8 * 2**20, transcendentals=work
        ),
        name="attention",
    )(*small, keys, values, *blocks, *extra)


def merge_kernel(parts, kv_local, *refs):
    in_refs, out_ref = refs[:parts], refs[parts]
    q_dev, width = out_ref.shape
    group = width // DH // kv_local
    lane_parts = q_dev * group // LANES
    per_part = LANES // q_dev
    stats = [ref[:, width:].astype(jnp.float32) for ref in in_refs]
    sublane = lax.broadcasted_iota(jnp.int32, (LANES, LANES), 0)
    for j in range(lane_parts):
        table = jnp.zeros((LANES, LANES), jnp.float32)
        for g in range(kv_local):
            at = [(g * 3 + i) * lane_parts + j for i in range(3)]
            levels = [stat[at[0]] + stat[at[1]] + stat[at[2]] for stat in stats]
            levels = [level.reshape(1, LANES) for level in levels]
            top = functools.reduce(jnp.maximum, levels)
            shares = [jnp.exp2(level - top) for level in levels]
            total = functools.reduce(jnp.add, shares)
            for c, share in enumerate(shares):
                table = jnp.where(sublane == g * parts + c, share / total, table)
        table = table.T
        for g in range(kv_local):
            for i in range(per_part):
                head = g * group + j * per_part + i
                cols = slice(head * DH, (head + 1) * DH)
                share = table[i * q_dev : (i + 1) * q_dev]
                mixed = functools.reduce(
                    jnp.add,
                    [
                        share[:, g * parts + c : g * parts + c + 1]
                        * in_refs[c][:, cols].astype(jnp.float32)
                        for c in range(parts)
                    ],
                )
                out_ref[:, cols] = mixed.astype(jnp.bfloat16)


def merge_call(parts, kv_local):
    q_dev, wide = parts[0].shape
    vmem = pl.BlockSpec(memory_space=pltpu.VMEM)
    return pl.pallas_call(
        functools.partial(merge_kernel, len(parts), kv_local),
        out_shape=jax.ShapeDtypeStruct((q_dev, wide - LANES), jnp.bfloat16),
        in_specs=[vmem] * len(parts),
        out_specs=vmem,
        compiler_params=pltpu.CompilerParams(vmem_limit_bytes=VMEM_MERGE),
        cost_estimate=pl.CostEstimate(
            flops=len(parts) * q_dev * wide * 2,
            bytes_accessed=len(parts) * q_dev * wide * 2,
            transcendentals=0,
        ),
        name="merge",
    )(*parts)


def projection_kernel(members, ctx_count, peers, w_ref, *rest):
    blocks = len(members)
    in_refs, rest = rest[:blocks], rest[blocks:]
    own_ref, send_ref, rows_ref, sum_ref = rest
    q_dev = in_refs[0].shape[0]
    me = lax.axis_index("ctx")
    for member, ref in zip(members, in_refs):
        at = flipped(me, ctx_count, *member) * q_dev
        rows_ref[pl.ds(pl.multiple_of(at, q_dev), q_dev), :] = ref[...]
    steps, part = own_ref.shape[:2]
    my_tp = lax.axis_index("tp")
    sum_ref[...] = jnp.dot(rows_ref[...], w_ref[...], preferred_element_type=jnp.float32)

    def piece(peer):
        return sum_ref[pl.ds(pl.multiple_of(peer * part, part), part), :]

    for j in range(steps):
        own_ref[j] = piece(my_tp ^ (2 * j))
        send_ref[j] = piece(my_tp ^ (2 * j + 1)).astype(jnp.bfloat16)


def projection_call(members, ctx_count, blocks, weight, peers):
    n = len(blocks)
    q_dev, width = blocks[0].shape
    columns = weight.shape[1]
    part = n * q_dev // peers
    vmem = pl.BlockSpec(memory_space=pltpu.VMEM)
    return pl.pallas_call(
        functools.partial(projection_kernel, members, ctx_count, peers),
        out_shape=[
            jax.ShapeDtypeStruct((peers // 2, part, columns), jnp.float32),
            jax.ShapeDtypeStruct((peers // 2, part, columns), jnp.bfloat16),
        ],
        in_specs=[vmem] * (1 + n),
        out_specs=[vmem] * 2,
        scratch_shapes=[
            pltpu.VMEM((n * q_dev, width), jnp.bfloat16),
            pltpu.VMEM((n * q_dev, columns), jnp.float32),
        ],
        compiler_params=pltpu.CompilerParams(vmem_limit_bytes=VMEM_PROJ),
        cost_estimate=pl.CostEstimate(
            flops=2 * n * q_dev * width * columns,
            bytes_accessed=2 * width * columns,
            transcendentals=0,
        ),
        name="projection",
    )(weight, *blocks)


def body(
    queries,
    new_keys,
    new_values,
    cache_keys,
    cache_values,
    keep_tiles,
    tile_count,
    owner_slot,
    out_weight,
):
    ctx_count = lax.axis_size("ctx")
    peers = lax.axis_size("tp")
    low = LOW_SIZE
    high = ctx_count // low

    def move(x, step, flip):
        pairs = [
            (i, (i // low + step) % high * low + (i % low + flip) % low) for i in range(ctx_count)
        ]
        return lax.ppermute(x, "ctx", pairs)

    steps = sorted(range(1, high), key=lambda k: (min(k, high - k), k))
    order = [(k, 0) for k in (0, *steps)] + [(k, 1) for k in (0, *steps)]

    def gather(x, chained):
        held = {(0, 0): x, (0, 1): move(x, 0, 1)}
        for k in steps:
            block = x
            if not chained and 2 * k == high:
                ready = {m: held[m] for m in held if m[0]}
                block, ready = lax.optimization_barrier((block, ready))
                held.update(ready)
            held[k, 0] = move(block, -k, 0)
        behind = None
        for k in steps:
            block = held[k, 0]
            if chained and 2 * k == high and behind is not None:
                block, held[behind] = lax.optimization_barrier((block, held[behind]))
            held[k, 1] = move(block, 0, 1)
            behind = (k, 1)
        return held

    held = gather(queries, False)
    near = [m for m in order[1:] if not m[1] and 2 * m[0] != high]
    middle = [m for m in order[1:] if not m[1] and 2 * m[0] == high]
    flip = [m for m in order if m[1] and m[0] and 2 * m[0] != high]
    late = [m for m in order if m[1] and 2 * m[0] == high] + [(0, 1)]
    late = late[::-1]
    groups = [near[i : i + 2] for i in range(0, len(near), 2)]
    groups += [middle + flip[:2]] + [flip[i : i + 2] for i in range(2, len(flip), 2)]
    groups += [late, order[:1]]
    kv_local = new_keys.shape[1] // DH
    small = (owner_slot, keep_tiles[0], tile_count[0], new_keys, new_values)
    token = settle_call(cache_keys, cache_values, new_keys, new_values)

    def attend(members, blocks, turn, values, extra):
        return attention_call(
            members,
            ctx_count,
            kv_local,
            keep_tiles.shape[2],
            turn,
            blocks,
            small,
            cache_keys,
            values,
            extra,
        )

    values = cache_values
    parts, back = {}, {}
    last = None
    for index, members in enumerate(groups):
        blocks = [held[m] for m in members]
        if index == 0:
            blocks, token = lax.optimization_barrier((blocks, token))
        if last is not None:
            blocks, parts[last] = lax.optimization_barrier((blocks, parts[last]))
        if 2 <= index < len(groups) - 1:
            returned = {m: back[m] for m in groups[index - 2] if 2 * m[0] != high}
            blocks, returned = lax.optimization_barrier((blocks, returned))
            back.update(returned)
        extra = [token] if members == groups[-1] else []
        outs = attend(members, blocks, index == 0, values, extra)
        parts.update(zip(members, outs))
        if index == 0:
            values = outs[-1]
        last = members[-1]
        for m in members:
            back[m] = parts[m] if m == (0, 0) else move(parts[m], *m)
    attn = merge_call([back[m] for m in order], kv_local)

    held = gather(attn, True)
    own, send = projection_call(order, ctx_count, [held[m] for m in order], out_weight, peers)
    got = lax.ppermute(send, "tp", [(i, i ^ 1) for i in range(peers)])
    total = own[0] + got[0].astype(jnp.float32)
    for j in range(1, peers // 2):
        piece = (own[j] + got[j].astype(jnp.float32)).astype(jnp.bfloat16)
        piece = lax.ppermute(piece, "tp", [(i, i ^ (2 * j)) for i in range(peers)])
        total = total + piece.astype(jnp.float32)
    return total


def solution(mesh):
    return jax.shard_map(
        body,
        mesh=mesh,
        in_specs=(
            P("ctx", "tp"),
            P("ctx", "tp"),
            P("ctx", "tp"),
            P("ctx", "tp"),
            P("ctx", "tp"),
            P("ctx", "tp", None),
            P("ctx", "tp"),
            P(),
            P("tp", "ctx"),
        ),
        out_specs=P("tp", "ctx"),
        check_vma=False,
    )
```

```python
import functools
import math

import jax
import jax.numpy as jnp
from jax import lax
from jax.experimental import pallas as pl
from jax.experimental.pallas import tpu as pltpu
from jax.sharding import PartitionSpec as P

DH = 128
TILE = 128
LANES = 128
CHUNK = 6
LOW = -1e30
LIMIT = 2.0**100
ONES = 16
LOW_SIZE = 2
VMEM_PACK = 58 * 2**20
VMEM_ATTN = 24 * 2**20
VMEM_MERGE = 8 * 2**20
VMEM_PROJ = 16 * 2**20


def flipped(me, count, step, flip):
    high = count // LOW_SIZE
    return lax.rem(me // LOW_SIZE + step, high) * LOW_SIZE + lax.rem(me + flip, LOW_SIZE)


def attention_kernel(
    members, ctx_count, group, kv_local, slots, turn, extra, slot_ref, keep_ref, count_ref, nk_ref, nv_ref, k_ref, v_ref, *rest
):
    blocks = len(members)
    q_refs, rest = rest[:blocks], rest[blocks + extra :]
    out_refs, rest = rest[:blocks], rest[blocks:]
    turned_ref, acc_ref, max_ref = rest[-3:]
    kept_ref = rest[0] if turn else v_ref
    last = kept_ref.shape[2] - TILE
    q_dev = q_refs[0].shape[0]
    heads = kv_local * group
    rows = q_dev * group
    span = CHUNK * TILE
    scale = math.log2(math.e) / math.sqrt(DH)
    me = lax.axis_index("ctx")

    def count_of(g):
        return count_ref[g]

    def slot_of(ctx):
        return slot_ref[ctx]

    ones_tile = jnp.ones((ONES, TILE), jnp.bfloat16)
    place_key = lax.broadcasted_iota(jnp.int32, (TILE, rows), 0)
    place_row = lax.broadcasted_iota(jnp.int32, (TILE, rows), 1) % q_dev
    padding = jnp.zeros((TILE - q_dev, DH), jnp.bfloat16)

    def keys_of(g, chunk):
        cols = slice(g * DH, (g + 1) * DH)
        parts = []
        for i in range(CHUNK):
            slot = chunk * CHUNK + i
            tile = keep_ref[g, jnp.where(slot < count_of(g), slot, 0)]
            parts.append(k_ref[pl.ds(pl.multiple_of(tile * TILE, TILE), TILE), cols])
        return jnp.concatenate(parts, 0)

    def values_of(g, chunk):
        whole = pl.ds(pl.multiple_of(chunk * span, span), span)
        if not turn:
            return kept_ref[g, :, whole]
        cols = slice(g * DH, (g + 1) * DH)
        parts = []
        for i in range(CHUNK):
            slot = chunk * CHUNK + i
            live = slot < count_of(g)
            tile = keep_ref[g, jnp.where(live, slot, 0)]
            at = pl.ds(pl.multiple_of(tile * TILE, TILE), TILE)
            tail = jnp.concatenate([v_ref[at, cols].T, ones_tile], 0)
            parts.append(jnp.where(live, tail, jnp.zeros_like(tail)))
        values = jnp.concatenate(parts, 1)
        kept_ref[g, :, whole] = values
        return values

    def open_head(g):
        cols = slice(g * DH, (g + 1) * DH)
        first = pl.ds(pl.multiple_of(keep_ref[g, 0] * TILE, TILE), TILE)
        keys = jnp.concatenate([nk_ref[:, cols], padding, k_ref[first, cols]], 0)
        for b in range(blocks):
            s = jnp.dot(keys, turned_ref[g, b], preferred_element_type=jnp.float32)
            shift = (slot_of(flipped(me, ctx_count, *members[b])) - slot_of(me)) * q_dev
            live = (place_key < q_dev) & (place_row - place_key + shift >= 0)
            fresh = jnp.where(live, s[:TILE], LOW)
            top = jnp.max(jnp.maximum(fresh, s[TILE:]), axis=0, keepdims=True) * scale
            p = jnp.exp2(fresh * scale - top).astype(jnp.bfloat16)
            max_ref[g, b] = jnp.broadcast_to(top, max_ref.shape[2:])
            acc_ref[g, b] = jnp.dot(
                kept_ref[g, :, last:], p, preferred_element_type=jnp.float32
            )

    for g in range(kv_local):
        if turn:
            fresh_values = nv_ref[:, g * DH : (g + 1) * DH]
            fresh_values = jnp.concatenate([fresh_values, padding], 0).T
            kept_ref[g, :, last:] = jnp.concatenate([fresh_values, ones_tile], 0)
        for b in range(blocks):
            columns = [
                q_refs[b][:, (g * group + h) * DH : (g * group + h + 1) * DH]
                for h in range(group)
            ]
            turned_ref[g, b] = jnp.concatenate(columns, 0).T
        open_head(g)

    def run(kv_heads, chunk):
        loaded = {g: (keys_of(g, chunk), values_of(g, chunk)) for g in kv_heads}
        chains = [(g, b) for b in range(blocks) for g in kv_heads]

        def score(g, b):
            return jnp.dot(loaded[g][0], turned_ref[g, b], preferred_element_type=jnp.float32)

        ahead = score(*chains[0])
        for at, (g, b) in enumerate(chains):
            s = ahead
            if at + 1 < len(chains):
                ahead = score(*chains[at + 1])
            p = jnp.exp2(s * scale - max_ref[g, b, :1]).astype(jnp.bfloat16)
            acc_ref[g, b] += jnp.dot(loaded[g][1], p, preferred_element_type=jnp.float32)

    ends = [(count_of(g) + CHUNK - 1) // CHUNK for g in range(kv_local)]
    shared = functools.reduce(jnp.minimum, ends)

    def step_all(chunk, carry):
        run(range(kv_local), chunk)
        return carry

    lax.fori_loop(0, shared, step_all, 0)
    for g in range(kv_local):

        def step_one(chunk, carry, g=g):
            run([g], chunk)
            return carry

        lax.fori_loop(shared, ends[g], step_one, 0)

    large = jnp.zeros((1, rows), jnp.float32)
    for g in range(kv_local):
        for b in range(blocks):
            fits = acc_ref[g, b, DH : DH + 1, :] < LIMIT
            large = jnp.maximum(large, jnp.where(fits, 0.0, 1.0))

    @pl.when(jnp.max(large) > 0.0)
    def again():
        for g in range(kv_local):
            open_head(g)

            def step_exact(chunk, carry, g=g):
                keys = keys_of(g, chunk)
                values = kept_ref[g, :, pl.ds(pl.multiple_of(chunk * span, span), span)]
                for b in range(blocks):
                    s = jnp.dot(keys, turned_ref[g, b], preferred_element_type=jnp.float32)
                    old = max_ref[g, b, :1]
                    top = jnp.maximum(old, jnp.max(s, axis=0, keepdims=True) * scale)
                    p = jnp.exp2(s * scale - top).astype(jnp.bfloat16)
                    max_ref[g, b] = jnp.broadcast_to(top, max_ref.shape[2:])
                    acc_ref[g, b] = acc_ref[g, b] * jnp.exp2(old - top) + jnp.dot(
                        values, p, preferred_element_type=jnp.float32
                    )
                return carry

            lax.fori_loop(0, ends[g], step_exact, 0)

    sublane = lax.broadcasted_iota(jnp.int32, (q_dev, LANES), 0)
    parts = rows // LANES
    for b in range(blocks):
        stats = jnp.zeros((q_dev, LANES), jnp.float32)
        for g in range(kv_local):
            total = acc_ref[g, b, DH : DH + 1, :]
            mean = (acc_ref[g, b, :DH, :] / total).T.astype(jnp.bfloat16)
            for h in range(group):
                head = g * group + h
                out_refs[b][:, head * DH : (head + 1) * DH] = mean[h * q_dev : (h + 1) * q_dev]
            level = max_ref[g, b, :1] + jnp.log2(total)
            high = level.astype(jnp.bfloat16).astype(jnp.float32)
            middle = (level - high).astype(jnp.bfloat16).astype(jnp.float32)
            for i, term in enumerate((high, middle, level - high - middle)):
                for j in range(parts):
                    at = (g * 3 + i) * parts + j
                    stats = jnp.where(sublane == at, term[:, j * LANES : (j + 1) * LANES], stats)
        out_refs[b][:, heads * DH :] = stats.astype(jnp.bfloat16)


def settle_kernel(k_hbm, v_hbm, nk_hbm, nv_hbm, out_ref):
    out_ref[...] = jnp.zeros_like(out_ref)


def settle_call(*arrays):
    return pl.pallas_call(
        settle_kernel,
        out_shape=jax.ShapeDtypeStruct((8, LANES), jnp.float32),
        in_specs=[pl.BlockSpec(memory_space=pltpu.HBM)] * len(arrays),
        out_specs=pl.BlockSpec(memory_space=pltpu.VMEM),
        compiler_params=pltpu.CompilerParams(vmem_limit_bytes=VMEM_PACK),
        name="settle",
    )(*arrays)


def attention_call(
    members, ctx_count, kv_local, slots, turn, blocks, small, keys, values, extra
):
    n = len(blocks)
    q_dev, width = blocks[0].shape
    group = width // DH // kv_local
    rows = q_dev * group
    smem = pl.BlockSpec(memory_space=pltpu.SMEM)
    vmem = pl.BlockSpec(memory_space=pltpu.VMEM)
    work = n * rows * kv_local * slots * TILE
    kept = -(-slots // CHUNK) * CHUNK + 1
    return pl.pallas_call(
        functools.partial(
            attention_kernel, members, ctx_count, group, kv_local, slots, turn, len(extra)
        ),
        out_shape=[jax.ShapeDtypeStruct((q_dev, width + LANES), jnp.bfloat16)] * n
        + [jax.ShapeDtypeStruct((kv_local, DH + ONES, kept * TILE), jnp.bfloat16)] * turn,
        in_specs=[smem] * 3 + [vmem] * (4 + n + len(extra)),
        out_specs=[vmem] * (n + turn),
        scratch_shapes=[
            pltpu.VMEM((kv_local, n, DH, rows), jnp.bfloat16),
            pltpu.VMEM((kv_local, n, DH + ONES, rows), jnp.float32),
            pltpu.VMEM((kv_local, n, 8, rows), jnp.float32),
        ],
        compiler_params=pltpu.CompilerParams(vmem_limit_bytes=VMEM_ATTN),
        cost_estimate=pl.CostEstimate(
            flops=work * DH * 8, bytes_accessed=8 * 2**20, transcendentals=work
        ),
        name="attention",
    )(*small, keys, values, *blocks, *extra)


def merge_kernel(parts, kv_local, *refs):
    in_refs, out_ref = refs[:parts], refs[parts]
    q_dev, width = out_ref.shape
    group = width // DH // kv_local
    lane_parts = q_dev * group // LANES
    per_part = LANES // q_dev
    stats = [ref[:, width:].astype(jnp.float32) for ref in in_refs]
    sublane = lax.broadcasted_iota(jnp.int32, (LANES, LANES), 0)
    for j in range(lane_parts):
        table = jnp.zeros((LANES, LANES), jnp.float32)
        for g in range(kv_local):
            at = [(g * 3 + i) * lane_parts + j for i in range(3)]
            levels = [stat[at[0]] + stat[at[1]] + stat[at[2]] for stat in stats]
            levels = [level.reshape(1, LANES) for level in levels]
            top = functools.reduce(jnp.maximum, levels)
            shares = [jnp.exp2(level - top) for level in levels]
            total = functools.reduce(jnp.add, shares)
            for c, share in enumerate(shares):
                table = jnp.where(sublane == g * parts + c, share / total, table)
        table = table.T
        for g in range(kv_local):
            for i in range(per_part):
                head = g * group + j * per_part + i
                cols = slice(head * DH, (head + 1) * DH)
                share = table[i * q_dev : (i + 1) * q_dev]
                mixed = functools.reduce(
                    jnp.add,
                    [
                        share[:, g * parts + c : g * parts + c + 1]
                        * in_refs[c][:, cols].astype(jnp.float32)
                        for c in range(parts)
                    ],
                )
                out_ref[:, cols] = mixed.astype(jnp.bfloat16)


def merge_call(parts, kv_local):
    q_dev, wide = parts[0].shape
    vmem = pl.BlockSpec(memory_space=pltpu.VMEM)
    return pl.pallas_call(
        functools.partial(merge_kernel, len(parts), kv_local),
        out_shape=jax.ShapeDtypeStruct((q_dev, wide - LANES), jnp.bfloat16),
        in_specs=[vmem] * len(parts),
        out_specs=vmem,
        compiler_params=pltpu.CompilerParams(vmem_limit_bytes=VMEM_MERGE),
        cost_estimate=pl.CostEstimate(
            flops=len(parts) * q_dev * wide * 2,
            bytes_accessed=len(parts) * q_dev * wide * 2,
            transcendentals=0,
        ),
        name="merge",
    )(*parts)


def projection_kernel(members, ctx_count, peers, w_ref, *rest):
    blocks = len(members)
    in_refs, rest = rest[:blocks], rest[blocks:]
    own_ref, send_ref, rows_ref, sum_ref = rest
    q_dev = in_refs[0].shape[0]
    me = lax.axis_index("ctx")
    for member, ref in zip(members, in_refs):
        at = flipped(me, ctx_count, *member) * q_dev
        rows_ref[pl.ds(pl.multiple_of(at, q_dev), q_dev), :] = ref[...]
    steps, part = own_ref.shape[:2]
    my_tp = lax.axis_index("tp")
    sum_ref[...] = jnp.dot(rows_ref[...], w_ref[...], preferred_element_type=jnp.float32)

    def piece(peer):
        return sum_ref[pl.ds(pl.multiple_of(peer * part, part), part), :]

    for j in range(steps):
        own_ref[j] = piece(my_tp ^ (2 * j))
        send_ref[j] = piece(my_tp ^ (2 * j + 1)).astype(jnp.bfloat16)


def projection_call(members, ctx_count, blocks, weight, peers):
    n = len(blocks)
    q_dev, width = blocks[0].shape
    columns = weight.shape[1]
    part = n * q_dev // peers
    vmem = pl.BlockSpec(memory_space=pltpu.VMEM)
    return pl.pallas_call(
        functools.partial(projection_kernel, members, ctx_count, peers),
        out_shape=[
            jax.ShapeDtypeStruct((peers // 2, part, columns), jnp.float32),
            jax.ShapeDtypeStruct((peers // 2, part, columns), jnp.bfloat16),
        ],
        in_specs=[vmem] * (1 + n),
        out_specs=[vmem] * 2,
        scratch_shapes=[
            pltpu.VMEM((n * q_dev, width), jnp.bfloat16),
            pltpu.VMEM((n * q_dev, columns), jnp.float32),
        ],
        compiler_params=pltpu.CompilerParams(vmem_limit_bytes=VMEM_PROJ),
        cost_estimate=pl.CostEstimate(
            flops=2 * n * q_dev * width * columns,
            bytes_accessed=2 * width * columns,
            transcendentals=0,
        ),
        name="projection",
    )(weight, *blocks)


def body(
    queries,
    new_keys,
    new_values,
    cache_keys,
    cache_values,
    keep_tiles,
    tile_count,
    owner_slot,
    out_weight,
):
    ctx_count = lax.axis_size("ctx")
    peers = lax.axis_size("tp")
    low = LOW_SIZE
    high = ctx_count // low

    def move(x, step, flip):
        pairs = [
            (i, (i // low + step) % high * low + (i % low + flip) % low) for i in range(ctx_count)
        ]
        return lax.ppermute(x, "ctx", pairs)

    steps = sorted(range(1, high), key=lambda k: (min(k, high - k), k))
    order = [(k, 0) for k in (0, *steps)] + [(k, 1) for k in (0, *steps)]

    def gather(x, chained):
        held = {(0, 0): x, (0, 1): move(x, 0, 1)}
        for k in steps:
            block = x
            if not chained and 2 * k == high:
                ready = {m: held[m] for m in held if m[0]}
                block, ready = lax.optimization_barrier((block, ready))
                held.update(ready)
            held[k, 0] = move(block, -k, 0)
        behind = None
        for k in steps:
            block = held[k, 0]
            if chained and behind is None:
                block, held[0, 1] = lax.optimization_barrier((block, held[0, 1]))
            if chained and 2 * k == high and behind is not None:
                block, held[behind] = lax.optimization_barrier((block, held[behind]))
            held[k, 1] = move(block, 0, 1)
            behind = (k, 1)
        return held

    held = gather(queries, False)
    near = [m for m in order[1:] if not m[1] and 2 * m[0] != high]
    middle = [m for m in order[1:] if not m[1] and 2 * m[0] == high]
    flip = [m for m in order if m[1] and m[0] and 2 * m[0] != high]
    late = [m for m in order if m[1] and 2 * m[0] == high] + [(0, 1)]
    late = late[::-1]
    groups = [near[i : i + 2] for i in range(0, len(near), 2)]
    groups += [middle + flip[:2]] + [flip[i : i + 2] for i in range(2, len(flip), 2)]
    groups += [late, order[:1]]
    kv_local = new_keys.shape[1] // DH
    small = (owner_slot, keep_tiles[0], tile_count[0], new_keys, new_values)
    token = settle_call(cache_keys, cache_values, new_keys, new_values)

    def attend(members, blocks, turn, values, extra):
        return attention_call(
            members,
            ctx_count,
            kv_local,
            keep_tiles.shape[2],
            turn,
            blocks,
            small,
            cache_keys,
            values,
            extra,
        )

    values = cache_values
    parts, back = {}, {}
    last = None
    for index, members in enumerate(groups):
        blocks = [held[m] for m in members]
        if index == 0:
            blocks, token = lax.optimization_barrier((blocks, token))
        if last is not None:
            blocks, parts[last] = lax.optimization_barrier((blocks, parts[last]))
        if 2 <= index < len(groups) - 1:
            returned = {m: back[m] for m in groups[index - 2] if 2 * m[0] != high}
            blocks, returned = lax.optimization_barrier((blocks, returned))
            back.update(returned)
        extra = [token] if members == groups[-1] else []
        outs = attend(members, blocks, index == 0, values, extra)
        parts.update(zip(members, outs))
        if index == 0:
            values = outs[-1]
        last = members[-1]
        for m in members:
            back[m] = parts[m] if m == (0, 0) else move(parts[m], *m)
    attn = merge_call([back[m] for m in order], kv_local)

    held = gather(attn, True)
    own, send = projection_call(order, ctx_count, [held[m] for m in order], out_weight, peers)
    got = lax.ppermute(send, "tp", [(i, i ^ 1) for i in range(peers)])
    total = own[0] + got[0].astype(jnp.float32)
    for j in range(1, peers // 2):
        piece = (own[j] + got[j].astype(jnp.float32)).astype(jnp.bfloat16)
        piece = lax.ppermute(piece, "tp", [(i, i ^ (2 * j)) for i in range(peers)])
        total = total + piece.astype(jnp.float32)
    return total


def solution(mesh):
    return jax.shard_map(
        body,
        mesh=mesh,
        in_specs=(
            P("ctx", "tp"),
            P("ctx", "tp"),
            P("ctx", "tp"),
            P("ctx", "tp"),
            P("ctx", "tp"),
            P("ctx", "tp", None),
            P("ctx", "tp"),
            P(),
            P("tp", "ctx"),
        ),
        out_specs=P("tp", "ctx"),
        check_vma=False,
    )
```
